32 devices in a mesh: case: 2 (over y), row: 4 (over z), col: 2 (over x), band: 2 (over core).
Axes of the slice: x: 2, y: 2, z: 4, core: 2. Of those that a mesh axis runs over, the one named last changes fastest.
Arguments:
- positions: float32 [3, 4096], P(None, ('case', 'row', 'col')), parts along dimension 1, as said below
- normals: float32 [3, 4096], P(None, ('case', 'row', 'col')), parts along dimension 1, as said below
- areas: float32 [4096], P(('case', 'row', 'col')), parts along dimension 0, as said below
- emission: float32 [64, 4096], P('band', ('case', 'row', 'col')), parts along dimension 1, may hold values from 0.2 to 2
- reflect: float32 [64, 4096], P('band', ('case', 'row', 'col')), parts along dimension 1, may hold values from 0.2 to 0.9
- pair_row: int32 [512], P(('case', 'row', 'col')), parts along dimension 0, may hold values from 0 to 15, as said below
- pair_col: int32 [512], P(('case', 'row', 'col')), parts along dimension 0, may hold values from 0 to 15, as said below
- pair_live: int32 [512], P(('case', 'row', 'col')), parts along dimension 0, may hold values from 0 to 1, as said below
Outputs:
- radiosity: float32 [64, 4096], P('band', ('case', 'row', 'col')), parts along dimension 1
The draws below stay inside these ranges and needn't reach their ends.
There are 2 independent parts, one for each index of `case`. The reference program is written for one: setup_inputs(seed, part) draws one part's arguments, and reference() takes and returns one part's arrays. A program takes and returns all parts, laid end to end along the dimension named above; each array names one. Nothing has to cross between parts.
Inputs may be any that keep to these rules, and one draw needn't show every extreme that they name: `pair_row`: blocks are numbered so that device r * 2 + c of the row and col axes owns blocks of segment r * 2 + c (2 each). The 32 slots of that device hold every ordered pair (p, q) with p in blocks r * 4 to r * 4 + 3 and q a block whose segment is congruent to c modulo 2, exactly once, its live slots first. Each unordered visible block pair is live in exactly one slot of a part, in one of its two orders. At most 31 slots of one device are live, and some device has exactly that many. `pair_col`: second block of the slot's pair, as described for pair_row. `pair_live`: live slots come first on each device. `positions`: patch centres. `normals`: unit vectors. `areas`: Positive.
All inputs are finite; a program needn't handle non-finite values.
Results may differ from the reference program's by a relative error of at most 0.0003.
Values may be sent and summed in bfloat16 or wider, within the bound.
No kernel may reach another device: no remote copies, remote signals or barrier semaphores. Data moves between devices by JAX's collectives and lax.ppermute only.
A program may use at most 64 MiB of HBM per device.

```python
import math
import jax
import jax.numpy as jnp
from jax import lax

BANDS = 64
BLOCK = 128
DEV_BLOCKS = 2
ITERS = 2
BLOCKS = 16
PATCHES = 2048
SLOTS = 256
N_ROW = 4
N_COL = 2


def draw_positions(key, part):
    side = 4.0 * (BLOCKS / 256.0) ** (1.0 / 3.0)
    spread = 0.75
    centres = jax.random.uniform(jax.random.fold_in(key, 1), (3, BLOCKS, 1), jnp.float32, 0.0, side)
    jitter = jax.random.uniform(jax.random.fold_in(key, 2), (3, BLOCKS, BLOCK), jnp.float32, -spread, spread)
    return (centres + jitter).reshape(3, PATCHES)


def draw_normals(key, part):
    raw = jax.random.normal(jax.random.fold_in(key, 3), (3, PATCHES), jnp.float32)
    return raw / jnp.sqrt(jnp.sum(raw * raw, axis=0, keepdims=True) + 0.001)


def draw_areas(key, part):
    factor = (256.0 / BLOCKS) ** (1.0 / 3.0)
    logs = jax.random.uniform(jax.random.fold_in(key, 4), (PATCHES,), jnp.float32, math.log(0.007), math.log(0.028))
    return jnp.exp(logs) * factor


def slot_table(key):
    row_blocks = DEV_BLOCKS * N_COL
    col_blocks = DEV_BLOCKS * N_ROW
    devices = N_ROW * N_COL
    device_ids = jnp.arange(devices, dtype=jnp.int32)
    row_of = device_ids // N_COL
    col_of = device_ids % N_COL
    near_local = jnp.arange(row_blocks, dtype=jnp.int32)
    near_ids = row_of[:, None] * row_blocks + near_local[None, :]
    far_local = jnp.arange(col_blocks, dtype=jnp.int32)
    far_ids = (far_local[None, :] // DEV_BLOCKS * N_COL + col_of[:, None]) * DEV_BLOCKS + far_local[None, :] % DEV_BLOCKS
    near_full = jnp.broadcast_to(near_ids[:, :, None], (devices, row_blocks, col_blocks))
    far_full = jnp.broadcast_to(far_ids[:, None, :], (devices, row_blocks, col_blocks))
    lower = jnp.minimum(near_full, far_full)
    upper = jnp.maximum(near_full, far_full)
    rolls = jax.random.randint(jax.random.fold_in(key, 11), (BLOCKS, BLOCKS), 0, 10, jnp.int32)
    occlusion = jax.random.randint(jax.random.fold_in(key, 12), (BLOCKS,), 5, 11, jnp.int32)
    on_first = (near_full // row_blocks == 0) & (far_full // DEV_BLOCKS % N_COL == 0)
    mirror_first = (far_full // row_blocks == 0) & (near_full // DEV_BLOCKS % N_COL == 0)
    parity_even = (near_full + far_full) % 2 == 0
    parity_ok = (near_full < far_full) == parity_even
    neither = jnp.logical_not(on_first) & jnp.logical_not(mirror_first)
    oriented = (near_full == far_full) | on_first & jnp.logical_not(mirror_first) | on_first & mirror_first & (near_full <= far_full) | neither & parity_ok
    visible = (rolls[lower, upper] < jnp.minimum(occlusion[lower], occlusion[upper])) | on_first | mirror_first
    live = (oriented & visible).astype(jnp.int32).reshape(devices, row_blocks * col_blocks)
    near_flat = near_full.reshape(devices, row_blocks * col_blocks)
    far_flat = far_full.reshape(devices, row_blocks * col_blocks)
    shuffle = jax.random.permutation(jax.random.fold_in(key, 13), row_blocks * col_blocks).astype(jnp.int32)
    score = (1 - live) * (row_blocks * col_blocks) + shuffle[None, :]
    order = jnp.argsort(score, axis=1, stable=True)
    near_sorted = jnp.take_along_axis(near_flat, order, axis=1).reshape(-1)
    far_sorted = jnp.take_along_axis(far_flat, order, axis=1).reshape(-1)
    live_sorted = jnp.take_along_axis(live, order, axis=1).reshape(-1)
    return (near_sorted, far_sorted, live_sorted)


def draw_pair_row(key, part):
    return slot_table(key)[0]


def draw_pair_col(key, part):
    return slot_table(key)[1]


def draw_pair_live(key, part):
    return slot_table(key)[2]


def shard_levels(stream_key, shape, split, smallest, largest):
    def one(position, parts):
        heights = jax.random.uniform(jax.random.fold_in(jax.random.fold_in(stream_key, 6), position), (parts,), jnp.float32, smallest / len(split), largest / len(split))
        return jnp.repeat(jnp.exp(heights), shape[position] // parts).reshape((-1,) + (1,) * (len(shape) - position - 1))

    factor_of = one(*split[0])
    for cut in split[1:]:
        factor_of = factor_of * one(*cut)
    return factor_of


def setup_inputs(seed: int = 0, part: int = 0) -> dict:
    streams_of = jax.random.split(jax.random.key(seed), 9)
    part_splits = jax.random.split(jax.random.fold_in(streams_of[8], part), 9)
    positions = draw_positions(jax.random.fold_in(jax.random.fold_in(streams_of[8], part), 71), part)
    normals = draw_normals(jax.random.fold_in(jax.random.fold_in(streams_of[8], part), 71), part)
    areas = draw_areas(jax.random.fold_in(jax.random.fold_in(streams_of[8], part), 71), part)
    emission = jnp.clip(0.2 + 1.8 * jax.random.uniform(part_splits[3], (BANDS, PATCHES), jnp.float32) ** shard_levels(part_splits[3], (BANDS, PATCHES), ((0, 2), (1, 8)), -0.2, 0.2), 0.2, 2.0)
    reflect = jnp.clip(0.2 + 0.7 * jax.random.uniform(part_splits[4], (BANDS, PATCHES), jnp.float32) ** shard_levels(part_splits[4], (BANDS, PATCHES), ((0, 2), (1, 8)), -0.2, 0.2), 0.2, 0.9)
    pair_row = draw_pair_row(jax.random.fold_in(jax.random.fold_in(streams_of[8], part), 71), part)
    pair_col = draw_pair_col(jax.random.fold_in(jax.random.fold_in(streams_of[8], part), 71), part)
    pair_live = draw_pair_live(jax.random.fold_in(jax.random.fold_in(streams_of[8], part), 71), part)
    return dict(positions=positions, normals=normals, areas=areas, emission=emission, reflect=reflect, pair_row=pair_row, pair_col=pair_col, pair_live=pair_live)


SOFTEN = 0.02


def form_tiles(near, far):
    offset = far[0:3, :, None, :] - near[0:3, :, :, None]
    leaving = jnp.sum(near[3:6, :, :, None] * offset, axis=0)
    arriving = -jnp.sum(far[3:6, :, None, :] * offset, axis=0)
    spacing = jnp.sum(offset * offset, axis=0) + SOFTEN
    return jax.nn.relu(leaving) * jax.nn.relu(arriving) / (math.pi * spacing * spacing)


def reference(positions, normals, areas, emission, reflect, pair_row, pair_col, pair_live):
    geometry = jnp.concatenate([positions, normals], axis=0).reshape(6, BLOCKS, BLOCK)
    group_size = math.gcd(SLOTS, 256)
    rows_all = pair_row.reshape(SLOTS // group_size, group_size)
    cols_all = pair_col.reshape(SLOTS // group_size, group_size)
    live_all = pair_live.reshape(SLOTS // group_size, group_size)
    radiosity = emission
    for sweep in range(ITERS):
        weighted = (areas[None, :] * radiosity).astype(jnp.bfloat16).reshape(BANDS, BLOCKS, BLOCK)

        def one_group(summed, inputs):
            near_ids, far_ids, live_ids = inputs
            tiles_now = form_tiles(geometry[:, near_ids], geometry[:, far_ids]).astype(jnp.bfloat16)
            tiles_wide = lax.optimization_barrier(tiles_now).astype(jnp.float32)
            live_float = live_ids.astype(jnp.float32)
            mirror = live_float * (near_ids != far_ids).astype(jnp.float32)
            far_weights = weighted[:, far_ids].astype(jnp.float32)
            near_weights = weighted[:, near_ids].astype(jnp.float32)
            to_rows = jnp.einsum("buv,kbv->kbu", tiles_wide, far_weights) * live_float[None, :, None]
            to_cols = jnp.einsum("buv,kbu->kbv", tiles_wide, near_weights) * mirror[None, :, None]
            summed = summed.at[:, near_ids].add(to_rows)
            summed = summed.at[:, far_ids].add(to_cols)
            return summed, None

        start_sum = jnp.zeros((BANDS, BLOCKS, BLOCK), jnp.float32)
        gathered, unused = lax.scan(one_group, start_sum, (rows_all, cols_all, live_all))
        radiosity = emission + reflect * gathered.reshape(BANDS, PATCHES)
    return radiosity
```

```python
import functools
import math

import jax
import jax.numpy as jnp
from jax import lax
from jax.experimental import pallas as pl
from jax.experimental.pallas import tpu as pltpu
from jax.sharding import PartitionSpec as P

BLOCK = 128
ITERS = 2


SOFTEN = 0.02

PAD_ROWS = 16
GEO_ROWS = 18


def bit_reverse(value, bits):
    out = value * 0
    for bit in range(bits):
        out = out | (((value >> bit) & 1) << (bits - 1 - bit))
    return out


def pack_kernel(col_bits, n_far, pos, nrm, area, emi, ref, prow, pcol, plive, out):
    seg = (lax.axis_index("row") << col_bits) | lax.axis_index("col")
    bands, width = emi.shape
    a = area[...]
    out[0:bands, :] = (a * emi[...]).astype(jnp.bfloat16)
    out[bands : 2 * bands, :] = (a * ref[...]).astype(jnp.bfloat16)
    geo = jnp.concatenate([pos[...], nrm[...]], axis=0)
    high = geo.astype(jnp.bfloat16).astype(jnp.float32)
    rest = geo - high
    middle = rest.astype(jnp.bfloat16).astype(jnp.float32)
    low = rest - middle
    lane = lax.broadcasted_iota(jnp.int32, (1, width), 1)
    col_mask = (1 << col_bits) - 1

    def add_slot(i, flags):
        p, q = prow[i], pcol[i]
        near = ((((p >> 1) ^ seg) & col_mask) << 1) | (p & 1)
        far = ((((q >> 1) ^ seg) >> col_bits) << 1) | (q & 1)
        return flags + jnp.where(lane == near * n_far + far, plive[i], 0)

    flags = lax.fori_loop(0, prow.shape[0], add_slot, jnp.zeros((1, width), jnp.int32), unroll=True)
    tail = jnp.zeros((2 * PAD_ROWS - GEO_ROWS - 1, width), jnp.float32)
    out[2 * bands : 2 * bands + 2 * PAD_ROWS, :] = jnp.concatenate(
        [high, middle, low, flags.astype(jnp.float32), tail], axis=0
    ).astype(jnp.bfloat16)


def main_kernel(
    n_seg, seg_bits, col_bits, n_far, emi, ref, low_half, high_half, out,
    held, far_rep, near_col, tiles, sums, flag_vec, flag_sm, sems,
):
    bands, width = emi.shape
    half = n_seg // 2
    n_pairs = n_seg * (n_seg + 1) // 2
    halves = width // BLOCK
    first = pltpu.make_async_copy(low_half, held.at[0:half], sems.at[0])
    second = pltpu.make_async_copy(high_half, held.at[half:n_seg], sems.at[1])
    first.start()
    second.start()
    sums[...] = jnp.zeros_like(sums)
    first.wait()
    second.wait()
    geo_at = 2 * bands
    for k in range(n_seg):
        piece = held[k, geo_at : geo_at + 2 * PAD_ROWS, :].astype(jnp.float32)
        flag_vec[k : k + 1, :] = piece[GEO_ROWS : GEO_ROWS + 1, 0:BLOCK].astype(jnp.int32)
    flag_copy = pltpu.make_async_copy(flag_vec, flag_sm, sems.at[2])
    flag_copy.start()
    for k in range(n_seg):
        piece = held[k, geo_at : geo_at + 2 * PAD_ROWS, :].astype(jnp.float32)
        geo = (piece[0:6] + piece[6:12]) + piece[12:18]
        near_col[k, :, 0:8] = jnp.transpose(
            jnp.concatenate([geo, jnp.zeros((2, width), jnp.float32)], axis=0)
        )
        for c in range(6):
            row = geo[c : c + 1]
            if c >= 3:
                row = row * (-1.0 / math.pi)
            far_rep[k, c] = jnp.broadcast_to(row, (8, width))
    flag_copy.wait()
    col_mask = (1 << col_bits) - 1

    def pair_of(t):
        t = jnp.int32(t)
        shift = t // n_seg
        near = t % n_seg
        return near, (near + shift) % n_seg

    def live(near_at, far_at, i, j):
        near = bit_reverse(near_at, seg_bits)
        far = bit_reverse(far_at, seg_bits)
        holder = (near & ~col_mask) | (far & col_mask)
        apart = near ^ far
        index = ((((apart & col_mask) << 1) | i) * n_far) + (((apart >> col_bits) << 1) | j)
        return flag_sm[bit_reverse(holder, seg_bits), index]

    def form(t):
        near_at, far_at = pair_of(t)
        for j in range(halves):
            cols = slice(j * BLOCK, (j + 1) * BLOCK)
            fx, fy, fz = (far_rep[far_at, c, :, cols] for c in range(3))
            bare = [far_rep[far_at, c, :, cols] for c in range(3, 6)]
            for i in range(halves):
                flag = live(near_at, far_at, i, j) | live(far_at, near_at, j, i)
                gx, gy, gz = (v * flag.astype(jnp.float32) for v in bare)
                for strip in range(BLOCK // 16):
                    parts = []
                    for part in range(2):
                        at = i * BLOCK + strip * 16 + part * 8
                        cols_now = near_col[near_at, at : at + 8, :]
                        px, py, pz, nx, ny, nz = (
                            jnp.broadcast_to(cols_now[:, c : c + 1], (8, BLOCK)) for c in range(6)
                        )
                        dx, dy, dz = fx - px, fy - py, fz - pz
                        leaving = nx * dx + ny * dy + nz * dz
                        arriving = gx * dx + gy * dy + gz * dz
                        spacing = dx * dx + dy * dy + dz * dz + SOFTEN
                        inverse = pl.reciprocal(spacing, approx=True)
                        inverse = inverse * (2.0 - spacing * inverse)
                        product = jnp.maximum(leaving, 0.0) * jnp.maximum(arriving, 0.0)
                        parts.append(product * inverse * inverse)
                    at = i * BLOCK + strip * 16
                    tiles[t, at : at + 16, cols] = jnp.concatenate(parts, axis=0).astype(jnp.bfloat16)

    def apply(t):
        near_at, far_at = pair_of(t)
        tile = tiles[t]
        to_near = lax.dot_general(
            held[far_at, 0:bands, :], tile, (((1,), (1,)), ((), ())), preferred_element_type=jnp.float32
        )
        to_far = lax.dot_general(
            held[near_at, 0:bands, :], tile, (((1,), (0,)), ((), ())), preferred_element_type=jnp.float32
        )
        sums[near_at] = sums[near_at] + to_near
        mirrored = (near_at != far_at).astype(jnp.float32)
        sums[far_at] = sums[far_at] + to_far * mirrored

    form(0)

    def step(t, carry):
        apply(t - 1)
        form(t)
        return carry

    lax.fori_loop(1, n_pairs, step, 0)
    apply(n_pairs - 1)
    total = jnp.zeros((bands, width), jnp.float32)
    for k in range(n_seg):
        base = held[k, 0:bands, :].astype(jnp.float32)
        gain = held[k, bands : 2 * bands, :].astype(jnp.float32)
        weighted = (base + gain * sums[k]).astype(jnp.bfloat16)
        if k <= half:
            tile, over = tiles[k * n_seg], 1
        else:
            tile, over = tiles[(n_seg - k) * n_seg + k], 0
        total += lax.dot_general(
            weighted, tile, (((1,), (over,)), ((), ())), preferred_element_type=jnp.float32
        )
    out[...] = emi[...] + ref[...] * total


def one_exchange(positions, normals, areas, emission, reflect, pair_row, pair_col, pair_live):
    n_row = lax.axis_size("row")
    n_col = lax.axis_size("col")
    n_seg = n_row * n_col
    seg_bits = n_seg.bit_length() - 1
    col_bits = n_col.bit_length() - 1
    bands, width = emission.shape
    n_far = width // BLOCK * n_row
    rows = 2 * bands + 2 * PAD_ROWS
    vmem = pl.BlockSpec(memory_space=pltpu.VMEM)
    smem = pl.BlockSpec(memory_space=pltpu.SMEM)
    hbm = pl.BlockSpec(memory_space=pl.ANY)
    packed = pl.pallas_call(
        functools.partial(pack_kernel, col_bits, n_far),
        out_shape=jax.ShapeDtypeStruct((rows, width), jnp.bfloat16),
        in_specs=[vmem] * 5 + [smem] * 3,
        out_specs=vmem,
    )(positions, normals, areas.reshape(1, width), emission, reflect, pair_row, pair_col, pair_live)
    gathered = packed[None]
    for bit in reversed(range(seg_bits)):
        arrived = lax.ppermute(
            gathered, ("row", "col"), [(i, i ^ (1 << bit)) for i in range(n_seg)]
        )
        if bit:
            gathered = jnp.concatenate([gathered, arrived])
    n_pairs = n_seg * (n_seg + 1) // 2
    return pl.pallas_call(
        functools.partial(main_kernel, n_seg, seg_bits, col_bits, n_far),
        out_shape=jax.ShapeDtypeStruct((bands, width), jnp.float32),
        in_specs=[vmem, vmem, hbm, hbm],
        out_specs=vmem,
        scratch_shapes=[
            pltpu.VMEM((n_seg, rows, width), jnp.bfloat16),
            pltpu.VMEM((n_seg, 6, 8, width), jnp.float32),
            pltpu.VMEM((n_seg, width, BLOCK), jnp.float32),
            pltpu.VMEM((n_pairs, width, width), jnp.bfloat16),
            pltpu.VMEM((n_seg, bands, width), jnp.float32),
            pltpu.VMEM((n_seg, BLOCK), jnp.int32),
            pltpu.SMEM((n_seg, BLOCK), jnp.int32),
            pltpu.SemaphoreType.DMA((3,)),
        ],
        compiler_params=pltpu.CompilerParams(vmem_limit_bytes=40 * 1024 * 1024),
    )(emission, reflect, gathered, arrived)


def form_tiles(near, far):
    offset = far[0:3, :, None, :] - near[0:3, :, :, None]
    leaving = jnp.sum(near[3:6, :, :, None] * offset, axis=0)
    arriving = -jnp.sum(far[3:6, :, None, :] * offset, axis=0)
    spacing = jnp.sum(offset * offset, axis=0) + SOFTEN
    return jax.nn.relu(leaving) * jax.nn.relu(arriving) / (math.pi * spacing * spacing)


def two_exchanges(positions, normals, areas, emission, reflect, pair_row, pair_col, pair_live):
    patch_dev = areas.shape[0]
    own_blocks = patch_dev // BLOCK
    n_row = lax.axis_size("row")
    n_col = lax.axis_size("col")
    row_blocks = own_blocks * n_col
    col_blocks = own_blocks * n_row
    all_blocks = row_blocks * n_row
    band_half = emission.shape[0]
    row_here = lax.axis_index("row")
    col_here = lax.axis_index("col")
    geometry = jnp.concatenate([positions, normals], axis=0)
    geo_rows = lax.all_gather(geometry, "col", axis=1, tiled=True).reshape(6, row_blocks, BLOCK)
    geo_cols = lax.all_gather(geometry, "row", axis=1, tiled=True).reshape(6, col_blocks, BLOCK)
    slots = pair_row.shape[0]
    rows_seen, cols_seen, live_seen = (
        lax.all_gather(pair_row, ("row", "col"), axis=0, tiled=True),
        lax.all_gather(pair_col, ("row", "col"), axis=0, tiled=True),
        lax.all_gather(pair_live, ("row", "col"), axis=0, tiled=True),
    )
    seen = jnp.zeros((all_blocks * all_blocks,), jnp.int32)
    seen = seen.at[rows_seen * all_blocks + cols_seen].max(live_seen)
    seen = seen.at[cols_seen * all_blocks + rows_seen].max(live_seen)
    near_grid = row_here * row_blocks + jnp.arange(row_blocks, dtype=jnp.int32)
    far_local = jnp.arange(col_blocks, dtype=jnp.int32)
    far_grid = (far_local // own_blocks * n_col + col_here) * own_blocks + far_local % own_blocks
    flags = seen[(near_grid[:, None] * all_blocks + far_grid[None, :]).reshape(-1)]
    order = jnp.argsort(1 - flags, stable=True)
    near_index = order // col_blocks
    far_index = order % col_blocks
    live_float = flags[order].astype(jnp.float32)
    live_count = jnp.sum(flags)
    group_size = math.gcd(slots, 32)
    turns = (live_count + group_size - 1) // group_size
    stored_init = jnp.zeros((1, 1, 1), jnp.bfloat16)
    stored = stored_init
    radiosity = emission
    for sweep in range(ITERS):
        weighted = (areas[None, :] * radiosity).astype(jnp.bfloat16)
        w_cols = lax.all_gather(weighted, "row", axis=1, tiled=True).reshape(
            band_half, col_blocks, BLOCK
        )

        def one_turn(turn_index, state_now):
            acc_rows, acc_cols, kept = state_now
            first_slot = turn_index * group_size
            near_now = lax.dynamic_slice_in_dim(near_index, first_slot, group_size)
            far_now = lax.dynamic_slice_in_dim(far_index, first_slot, group_size)
            live_now = lax.dynamic_slice_in_dim(live_float, first_slot, group_size)
            tiles_now = form_tiles(geo_rows[:, near_now], geo_cols[:, far_now]).astype(jnp.bfloat16)
            far_weights = w_cols[:, far_now]
            to_rows = jnp.einsum(
                "buv,kbv->kbu", tiles_now, far_weights, preferred_element_type=jnp.float32
            )
            acc_rows = acc_rows.at[:, near_now].add(to_rows * live_now[None, :, None])
            return (acc_rows, acc_cols, kept)

        zero_rows = jnp.zeros((band_half, row_blocks, BLOCK), jnp.float32)
        zero_cols = jnp.zeros((1, 1, 1), jnp.float32)
        acc_rows, acc_cols, stored = lax.fori_loop(
            0, turns, one_turn, (zero_rows, zero_cols, stored)
        )
        row_sum = lax.psum_scatter(
            acc_rows.reshape(band_half, row_blocks * BLOCK), "col", scatter_dimension=1, tiled=True
        )
        radiosity = emission + reflect * row_sum
    return radiosity


def shards(positions, normals, areas, emission, reflect, pair_row, pair_col, pair_live):
    n_row, n_col = lax.axis_size("row"), lax.axis_size("col")
    n_seg = n_row * n_col
    powers = n_row & (n_row - 1) == 0 and n_col & (n_col - 1) == 0
    small = areas.shape[0] == 2 * BLOCK and 2 <= n_seg <= 16
    plan = one_exchange if powers and small else two_exchanges
    return plan(positions, normals, areas, emission, reflect, pair_row, pair_col, pair_live)


def solution(mesh):
    return jax.shard_map(
        shards,
        mesh=mesh,
        in_specs=(
            P(None, ("case", "row", "col")),
            P(None, ("case", "row", "col")),
            P(("case", "row", "col")),
            P("band", ("case", "row", "col")),
            P("band", ("case", "row", "col")),
            P(("case", "row", "col")),
            P(("case", "row", "col")),
            P(("case", "row", "col")),
        ),
        out_specs=P("band", ("case", "row", "col")),
        check_vma=False,
    )
```

```python
import functools
import math

import jax
import jax.numpy as jnp
from jax import lax
from jax.experimental import pallas as pl
from jax.experimental.pallas import tpu as pltpu
from jax.sharding import PartitionSpec as P

BLOCK = 128
ITERS = 2


SOFTEN = 0.02

GEO_ROWS = 32
FLAG_ROW = 6


def bit_reverse(value, bits):
    out = value * 0
    for bit in range(bits):
        out = out | (((value >> bit) & 1) << (bits - 1 - bit))
    return out


def three_pieces(x):
    high = x.astype(jnp.bfloat16).astype(jnp.float32)
    rest = x - high
    middle = rest.astype(jnp.bfloat16).astype(jnp.float32)
    return high, middle, rest - middle


def pack_kernel(col_bits, n_far, pos, nrm, area, emi, ref, prow, pcol, plive, out):
    seg = (lax.axis_index("row") << col_bits) | lax.axis_index("col")
    bands, width = emi.shape
    a = area[...]
    out[0:bands, :] = (a * emi[...]).astype(jnp.bfloat16)
    out[bands : 2 * bands, :] = (a * ref[...]).astype(jnp.bfloat16)
    lane = lax.broadcasted_iota(jnp.int32, (1, width), 1)
    col_mask = (1 << col_bits) - 1

    def add_slot(i, flags):
        p, q = prow[i], pcol[i]
        near = ((((p >> 1) ^ seg) & col_mask) << 1) | (p & 1)
        far = ((((q >> 1) ^ seg) >> col_bits) << 1) | (q & 1)
        return flags + jnp.where(lane == near * n_far + far, plive[i], 0)

    flags = lax.fori_loop(0, prow.shape[0], add_slot, jnp.zeros((1, width), jnp.int32), unroll=True)
    geo = jnp.concatenate(
        [pos[...], nrm[...], flags.astype(jnp.float32), jnp.zeros((1, width), jnp.float32)], axis=0
    )
    out[2 * bands : 2 * bands + GEO_ROWS, :] = jnp.concatenate(
        [*three_pieces(geo), jnp.zeros((8, width), jnp.float32)], axis=0
    ).astype(jnp.bfloat16)


def near_stack(x):
    high, middle, low = three_pieces(x)
    return jnp.concatenate([high, high, middle, high, low, middle], axis=0)


def far_stack(x):
    high, middle, low = three_pieces(x)
    return jnp.concatenate([high, middle, high, low, high, middle], axis=0).astype(jnp.bfloat16)


def main_kernel(
    n_seg, seg_bits, col_bits, n_far, emi, ref, low_half, high_half, out,
    held, geo_all, centre, far_rep, near_pos, near_rep, near_leave, near_arrive, leave_even,
    arrive_even, leave_odd, arrive_odd, tiles, sums, flag_vec, flag_sm, sems,
):
    bands, width = emi.shape
    half = n_seg // 2
    n_pairs = n_seg * (n_seg + 1) // 2
    halves = width // BLOCK
    first = pltpu.make_async_copy(low_half, held.at[0:half], sems.at[0])
    second = pltpu.make_async_copy(high_half, held.at[half:n_seg], sems.at[1])
    first.start()
    second.start()
    sums[...] = jnp.zeros_like(sums)
    tiles[n_pairs] = jnp.zeros((width, width), jnp.bfloat16)
    first.wait()
    second.wait()
    geo_at = 2 * bands
    for k in range(n_seg):
        piece = held[k, geo_at : geo_at + GEO_ROWS, :].astype(jnp.float32)
        geo = (piece[0:8] + piece[8:16]) + piece[16:24]
        geo_all[k] = geo
        flag_vec[k : k + 1, :] = geo[FLAG_ROW : FLAG_ROW + 1, 0:BLOCK].astype(jnp.int32)
    flag_copy = pltpu.make_async_copy(flag_vec, flag_sm, sems.at[2])
    flag_copy.start()
    row = lax.broadcasted_iota(jnp.int32, (8, width), 0)
    for k in range(n_seg):
        geo = geo_all[k]
        for c in range(3):
            far_rep[k, c] = jnp.broadcast_to(geo[c : c + 1], (8, width))
        near_pos[k, :, 0:8] = jnp.transpose(geo)
        middle = jnp.broadcast_to(geo[:, 0:1], (8, width))
        centre[k] = middle
        offset = jnp.where(row < 3, geo - middle, 0.0)
        normal = jnp.where(row < 3, pltpu.roll(geo, 5, 0), 0.0)
        along = jnp.sum(normal * offset, axis=0, keepdims=True)
        near_leave[k] = jnp.transpose(near_stack(jnp.where(row == 3, -along, normal))).astype(jnp.bfloat16)
        near_arrive[k] = jnp.transpose(near_stack(jnp.where(row == 3, 1.0, -offset))).astype(jnp.bfloat16)
    flag_copy.wait()
    col_mask = (1 << col_bits) - 1

    def pair_of(t):
        t = jnp.int32(t)
        shift = t // n_seg
        near = t % n_seg
        return near, (near + shift) % n_seg

    def live(near_at, far_at, i, j):
        near = bit_reverse(near_at, seg_bits)
        far = bit_reverse(far_at, seg_bits)
        holder = (near & ~col_mask) | (far & col_mask)
        apart = near ^ far
        index = ((((apart & col_mask) << 1) | i) * n_far) + (((apart >> col_bits) << 1) | j)
        return flag_sm[bit_reverse(holder, seg_bits), index]

    def project(t, leave, arrive):
        near_at, far_at = pair_of(t)
        geo = geo_all[far_at]
        offset = jnp.where(row < 3, geo - centre[near_at], 0.0)
        normal = jnp.where(row < 3, pltpu.roll(geo, 5, 0), 0.0) * (-1.0 / math.pi)
        along = jnp.sum(normal * offset, axis=0, keepdims=True)
        leave[...] = jnp.dot(
            near_leave[near_at], far_stack(jnp.where(row == 3, 1.0, offset)),
            preferred_element_type=jnp.float32,
        )
        arrive[...] = jnp.dot(
            near_arrive[near_at], far_stack(jnp.where(row == 3, along, normal)),
            preferred_element_type=jnp.float32,
        )

    def form(t, leave, arrive, fresh):
        near_at, far_at = pair_of(t)
        flags = [
            [
                (live(near_at, far_at, i, j) | live(far_at, near_at, j, i)).astype(jnp.float32)
                for j in range(halves)
            ]
            for i in range(halves)
        ]
        fars = [
            [far_rep[far_at, c, :, j * BLOCK : (j + 1) * BLOCK] for c in range(3)]
            for j in range(halves)
        ]
        for strip in range(width // 16):
            i = strip * 16 // BLOCK
            nears = []
            for part in range(2):
                at = strip * 16 + part * 8
                if fresh:
                    cols_now = near_pos[near_at, at : at + 8, :]
                    now = [jnp.broadcast_to(cols_now[:, c : c + 1], (8, BLOCK)) for c in range(3)]
                    for c in range(3):
                        near_rep[near_at, c, at : at + 8, :] = now[c]
                else:
                    now = [near_rep[near_at, c, at : at + 8, :] for c in range(3)]
                nears.append(now)
            for j in range(halves):
                cols = slice(j * BLOCK, (j + 1) * BLOCK)
                parts = []
                for part in range(2):
                    at = strip * 16 + part * 8
                    dx, dy, dz = (f - n for f, n in zip(fars[j], nears[part]))
                    spacing = dx * dx + dy * dy + dz * dz + SOFTEN
                    inverse = 1.0 / spacing
                    product = jnp.maximum(leave[at : at + 8, cols], 0.0) * jnp.maximum(
                        arrive[at : at + 8, cols], 0.0
                    )
                    parts.append(product * inverse * inverse)
                strip_now = jnp.concatenate(parts, axis=0).astype(jnp.bfloat16)
                tiles[t, strip * 16 : strip * 16 + 16, cols] = strip_now * flags[i][j].astype(jnp.bfloat16)

    def apply(t):
        near_at, far_at = pair_of(t)
        tile = tiles[t]
        to_near = lax.dot_general(
            held[far_at, 0:bands, :], tile, (((1,), (1,)), ((), ())), preferred_element_type=jnp.float32
        )
        to_far = lax.dot_general(
            held[near_at, 0:bands, :], tile, (((1,), (0,)), ((), ())), preferred_element_type=jnp.float32
        )
        sums[near_at] = sums[near_at] + to_near
        mirrored = (near_at != far_at).astype(jnp.float32)
        sums[far_at] = sums[far_at] + to_far * mirrored

    def two_steps(fresh, i, carry):
        for part, (now, later) in enumerate(((even, odd), (odd, even))):
            t = 2 * i + part
            apply(jnp.where(t == 0, n_pairs, t - 1))
            project(t + 1, *later)
            form(t, *now, fresh)
        return carry

    even, odd = (leave_even, arrive_even), (leave_odd, arrive_odd)
    project(0, *even)
    lax.fori_loop(0, n_seg // 2, functools.partial(two_steps, True), 0)
    lax.fori_loop(n_seg // 2, n_pairs // 2, functools.partial(two_steps, False), 0)
    apply(n_pairs - 1)
    total = jnp.zeros((bands, width), jnp.float32)
    for k in range(n_seg):
        base = held[k, 0:bands, :].astype(jnp.float32)
        gain = held[k, bands : 2 * bands, :].astype(jnp.float32)
        weighted = (base + gain * sums[k]).astype(jnp.bfloat16)
        if k <= half:
            tile, over = tiles[k * n_seg], 1
        else:
            tile, over = tiles[(n_seg - k) * n_seg + k], 0
        total += lax.dot_general(
            weighted, tile, (((1,), (over,)), ((), ())), preferred_element_type=jnp.float32
        )
    out[...] = emi[...] + ref[...] * total


def main_scratch(n_seg, rows, bands, width):
    n_pairs = n_seg * (n_seg + 1) // 2
    return [
        pltpu.VMEM((n_seg, rows, width), jnp.bfloat16),
        pltpu.VMEM((n_seg, 8, width), jnp.float32),
        pltpu.VMEM((n_seg, 8, width), jnp.float32),
        pltpu.VMEM((n_seg, 3, 8, width), jnp.float32),
        pltpu.VMEM((n_seg, width, BLOCK), jnp.float32),
        pltpu.VMEM((n_seg, 3, width, BLOCK), jnp.float32),
        pltpu.VMEM((n_seg, width, 48), jnp.bfloat16),
        pltpu.VMEM((n_seg, width, 48), jnp.bfloat16),
        *[pltpu.VMEM((width, width), jnp.float32)] * 4,
        pltpu.VMEM((n_pairs + 1, width, width), jnp.bfloat16),
        pltpu.VMEM((n_seg, bands, width), jnp.float32),
        pltpu.VMEM((n_seg, BLOCK), jnp.int32),
        pltpu.SMEM((n_seg, BLOCK), jnp.int32),
        pltpu.SemaphoreType.DMA((3,)),
    ]


def one_exchange(positions, normals, areas, emission, reflect, pair_row, pair_col, pair_live):
    n_row = lax.axis_size("row")
    n_col = lax.axis_size("col")
    n_seg = n_row * n_col
    seg_bits = n_seg.bit_length() - 1
    col_bits = n_col.bit_length() - 1
    bands, width = emission.shape
    n_far = width // BLOCK * n_row
    rows = 2 * bands + GEO_ROWS
    vmem = pl.BlockSpec(memory_space=pltpu.VMEM)
    smem = pl.BlockSpec(memory_space=pltpu.SMEM)
    hbm = pl.BlockSpec(memory_space=pl.ANY)
    packed = pl.pallas_call(
        functools.partial(pack_kernel, col_bits, n_far),
        out_shape=jax.ShapeDtypeStruct((rows, width), jnp.bfloat16),
        in_specs=[vmem] * 5 + [smem] * 3,
        out_specs=vmem,
    )(positions, normals, areas.reshape(1, width), emission, reflect, pair_row, pair_col, pair_live)
    gathered = packed[None]
    for bit in reversed(range(seg_bits)):
        arrived = lax.ppermute(
            gathered, ("row", "col"), [(i, i ^ (1 << bit)) for i in range(n_seg)]
        )
        if bit:
            gathered = jnp.concatenate([gathered, arrived])
    return pl.pallas_call(
        functools.partial(main_kernel, n_seg, seg_bits, col_bits, n_far),
        out_shape=jax.ShapeDtypeStruct((bands, width), jnp.float32),
        in_specs=[vmem, vmem, hbm, hbm],
        out_specs=vmem,
        scratch_shapes=main_scratch(n_seg, rows, bands, width),
        compiler_params=pltpu.CompilerParams(vmem_limit_bytes=40 * 1024 * 1024),
    )(emission, reflect, gathered, arrived)


def form_tiles(near, far):
    offset = far[0:3, :, None, :] - near[0:3, :, :, None]
    leaving = jnp.sum(near[3:6, :, :, None] * offset, axis=0)
    arriving = -jnp.sum(far[3:6, :, None, :] * offset, axis=0)
    spacing = jnp.sum(offset * offset, axis=0) + SOFTEN
    return jax.nn.relu(leaving) * jax.nn.relu(arriving) / (math.pi * spacing * spacing)


def two_exchanges(positions, normals, areas, emission, reflect, pair_row, pair_col, pair_live):
    patch_dev = areas.shape[0]
    own_blocks = patch_dev // BLOCK
    n_row = lax.axis_size("row")
    n_col = lax.axis_size("col")
    row_blocks = own_blocks * n_col
    col_blocks = own_blocks * n_row
    all_blocks = row_blocks * n_row
    band_half = emission.shape[0]
    row_here = lax.axis_index("row")
    col_here = lax.axis_index("col")
    geometry = jnp.concatenate([positions, normals], axis=0)
    geo_rows = lax.all_gather(geometry, "col", axis=1, tiled=True).reshape(6, row_blocks, BLOCK)
    geo_cols = lax.all_gather(geometry, "row", axis=1, tiled=True).reshape(6, col_blocks, BLOCK)
    slots = pair_row.shape[0]
    rows_seen, cols_seen, live_seen = (
        lax.all_gather(pair_row, ("row", "col"), axis=0, tiled=True),
        lax.all_gather(pair_col, ("row", "col"), axis=0, tiled=True),
        lax.all_gather(pair_live, ("row", "col"), axis=0, tiled=True),
    )
    seen = jnp.zeros((all_blocks * all_blocks,), jnp.int32)
    seen = seen.at[rows_seen * all_blocks + cols_seen].max(live_seen)
    seen = seen.at[cols_seen * all_blocks + rows_seen].max(live_seen)
    near_grid = row_here * row_blocks + jnp.arange(row_blocks, dtype=jnp.int32)
    far_local = jnp.arange(col_blocks, dtype=jnp.int32)
    far_grid = (far_local // own_blocks * n_col + col_here) * own_blocks + far_local % own_blocks
    flags = seen[(near_grid[:, None] * all_blocks + far_grid[None, :]).reshape(-1)]
    order = jnp.argsort(1 - flags, stable=True)
    near_index = order // col_blocks
    far_index = order % col_blocks
    live_float = flags[order].astype(jnp.float32)
    live_count = jnp.sum(flags)
    group_size = math.gcd(slots, 32)
    turns = (live_count + group_size - 1) // group_size
    stored_init = jnp.zeros((1, 1, 1), jnp.bfloat16)
    stored = stored_init
    radiosity = emission
    for sweep in range(ITERS):
        weighted = (areas[None, :] * radiosity).astype(jnp.bfloat16)
        w_cols = lax.all_gather(weighted, "row", axis=1, tiled=True).reshape(
            band_half, col_blocks, BLOCK
        )

        def one_turn(turn_index, state_now):
            acc_rows, acc_cols, kept = state_now
            first_slot = turn_index * group_size
            near_now = lax.dynamic_slice_in_dim(near_index, first_slot, group_size)
            far_now = lax.dynamic_slice_in_dim(far_index, first_slot, group_size)
            live_now = lax.dynamic_slice_in_dim(live_float, first_slot, group_size)
            tiles_now = form_tiles(geo_rows[:, near_now], geo_cols[:, far_now]).astype(jnp.bfloat16)
            far_weights = w_cols[:, far_now]
            to_rows = jnp.einsum(
                "buv,kbv->kbu", tiles_now, far_weights, preferred_element_type=jnp.float32
            )
            acc_rows = acc_rows.at[:, near_now].add(to_rows * live_now[None, :, None])
            return (acc_rows, acc_cols, kept)

        zero_rows = jnp.zeros((band_half, row_blocks, BLOCK), jnp.float32)
        zero_cols = jnp.zeros((1, 1, 1), jnp.float32)
        acc_rows, acc_cols, stored = lax.fori_loop(
            0, turns, one_turn, (zero_rows, zero_cols, stored)
        )
        row_sum = lax.psum_scatter(
            acc_rows.reshape(band_half, row_blocks * BLOCK), "col", scatter_dimension=1, tiled=True
        )
        radiosity = emission + reflect * row_sum
    return radiosity


def shards(positions, normals, areas, emission, reflect, pair_row, pair_col, pair_live):
    n_row, n_col = lax.axis_size("row"), lax.axis_size("col")
    n_seg = n_row * n_col
    powers = n_row & (n_row - 1) == 0 and n_col & (n_col - 1) == 0
    small = areas.shape[0] == 2 * BLOCK and 4 <= n_seg <= 16
    plan = one_exchange if powers and small else two_exchanges
    return plan(positions, normals, areas, emission, reflect, pair_row, pair_col, pair_live)


def solution(mesh):
    return jax.shard_map(
        shards,
        mesh=mesh,
        in_specs=(
            P(None, ("case", "row", "col")),
            P(None, ("case", "row", "col")),
            P(("case", "row", "col")),
            P("band", ("case", "row", "col")),
            P("band", ("case", "row", "col")),
            P(("case", "row", "col")),
            P(("case", "row", "col")),
            P(("case", "row", "col")),
        ),
        out_specs=P("band", ("case", "row", "col")),
        check_vma=False,
    )
```

```python
import functools
import math

import jax
import jax.numpy as jnp
from jax import lax
from jax.experimental import pallas as pl
from jax.experimental.pallas import tpu as pltpu
from jax.sharding import PartitionSpec as P

BLOCK = 128
ITERS = 2


SOFTEN = 0.02

GEO_ROWS = 32
FLAG_ROW = 6


def bit_reverse(value, bits):
    out = value * 0
    for bit in range(bits):
        out = out | (((value >> bit) & 1) << (bits - 1 - bit))
    return out


def three_pieces(x):
    high = x.astype(jnp.bfloat16).astype(jnp.float32)
    rest = x - high
    middle = rest.astype(jnp.bfloat16).astype(jnp.float32)
    return high, middle, rest - middle


def pack_kernel(col_bits, n_far, pos, nrm, area, emi, ref, prow, pcol, plive, out):
    seg = (lax.axis_index("row") << col_bits) | lax.axis_index("col")
    bands, width = emi.shape
    a = area[...]
    out[0:bands, :] = (a * emi[...]).astype(jnp.bfloat16)
    out[bands : 2 * bands, :] = (a * ref[...]).astype(jnp.bfloat16)
    lane = lax.broadcasted_iota(jnp.int32, (1, width), 1)
    col_mask = (1 << col_bits) - 1

    def add_slot(i, flags):
        p, q = prow[i], pcol[i]
        near = ((((p >> 1) ^ seg) & col_mask) << 1) | (p & 1)
        far = ((((q >> 1) ^ seg) >> col_bits) << 1) | (q & 1)
        return flags + jnp.where(lane == near * n_far + far, plive[i], 0)

    flags = lax.fori_loop(0, prow.shape[0], add_slot, jnp.zeros((1, width), jnp.int32), unroll=True)
    geo = jnp.concatenate(
        [pos[...], nrm[...], flags.astype(jnp.float32), jnp.zeros((1, width), jnp.float32)], axis=0
    )
    out[2 * bands : 2 * bands + GEO_ROWS, :] = jnp.concatenate(
        [*three_pieces(geo), jnp.zeros((8, width), jnp.float32)], axis=0
    ).astype(jnp.bfloat16)


def near_stack(x):
    high, middle, low = three_pieces(x)
    return jnp.concatenate([high, high, middle, high, low, middle], axis=0)


def far_stack(x):
    high, middle, low = three_pieces(x)
    return jnp.concatenate([high, middle, high, low, high, middle], axis=0).astype(jnp.bfloat16)


def triangle(count):
    return count * (count + 1) // 2


def own_tile(k, count):
    if k <= count // 2:
        return k * count, 1
    return (count - k) * count + k, 0


def grow_kernel(n_old, n_new, bits, seg_bits, col_bits, n_far, last, *refs):
    if last:
        emi, ref, held, old_sums, old_tiles, out, tiles, sums, *scratch = refs
    else:
        held, sums, tiles, *scratch = refs
    (
        geo_all, centre, far_rep, near_pos, near_rep, near_leave, near_arrive,
        leave_even, arrive_even, leave_odd, arrive_odd, flag_vec, flag_sm, sem,
    ) = scratch
    n_seg = n_old + n_new
    bands, width = held.shape[1] // 2 - GEO_ROWS // 2, held.shape[2]
    n_tri = triangle(n_new)
    n_pairs = n_tri + n_new * n_old
    halves = width // BLOCK
    geo_at = 2 * bands
    for k in range(n_seg):
        piece = held[k, geo_at : geo_at + GEO_ROWS, :].astype(jnp.float32)
        geo = (piece[0:8] + piece[8:16]) + piece[16:24]
        geo_all[k] = geo
        flag_vec[k : k + 1, :] = geo[FLAG_ROW : FLAG_ROW + 1, 0:BLOCK].astype(jnp.int32)
    flag_copy = pltpu.make_async_copy(flag_vec, flag_sm, sem)
    flag_copy.start()
    if n_old:
        sums[0:n_old] = old_sums[...]
    sums[n_old:n_seg] = jnp.zeros((n_new, bands, width), jnp.float32)
    tiles[n_pairs] = jnp.zeros((width, width), jnp.bfloat16)
    row = lax.broadcasted_iota(jnp.int32, (8, width), 0)
    for k in range(n_seg):
        geo = geo_all[k]
        for c in range(3):
            far_rep[k, c] = jnp.broadcast_to(geo[c : c + 1], (8, width))
        if k < n_old:
            continue
        at = k - n_old
        near_pos[at, :, 0:8] = jnp.transpose(geo)
        middle = jnp.broadcast_to(geo[:, 0:1], (8, width))
        centre[at] = middle
        offset = jnp.where(row < 3, geo - middle, 0.0)
        normal = jnp.where(row < 3, pltpu.roll(geo, 5, 0), 0.0)
        along = jnp.sum(normal * offset, axis=0, keepdims=True)
        near_leave[at] = jnp.transpose(near_stack(jnp.where(row == 3, -along, normal))).astype(jnp.bfloat16)
        near_arrive[at] = jnp.transpose(near_stack(jnp.where(row == 3, 1.0, -offset))).astype(jnp.bfloat16)
    flag_copy.wait()
    col_mask = (1 << col_bits) - 1

    def pair_of(t):
        t = jnp.int32(t)
        near = t % n_new
        far = (near + t // n_new) % n_new + n_old
        if n_old:
            far = jnp.where(t < n_tri, far, jnp.minimum((t - n_tri) // n_new, n_old - 1))
            near = jnp.where(t < n_tri, near, (t - n_tri) % n_new)
        return near, near + n_old, far

    def live(near_at, far_at, i, j):
        near = bit_reverse(near_at, bits) << (seg_bits - bits)
        far = bit_reverse(far_at, bits) << (seg_bits - bits)
        holder = (near & ~col_mask) | (far & col_mask)
        apart = near ^ far
        index = ((((apart & col_mask) << 1) | i) * n_far) + (((apart >> col_bits) << 1) | j)
        return flag_sm[bit_reverse(holder >> (seg_bits - bits), bits), index]

    def project(t, leave, arrive):
        local, near_at, far_at = pair_of(t)
        geo = geo_all[far_at]
        offset = jnp.where(row < 3, geo - centre[local], 0.0)
        normal = jnp.where(row < 3, pltpu.roll(geo, 5, 0), 0.0) * (-1.0 / math.pi)
        along = jnp.sum(normal * offset, axis=0, keepdims=True)
        leave[...] = jnp.dot(
            near_leave[local], far_stack(jnp.where(row == 3, 1.0, offset)),
            preferred_element_type=jnp.float32,
        )
        arrive[...] = jnp.dot(
            near_arrive[local], far_stack(jnp.where(row == 3, along, normal)),
            preferred_element_type=jnp.float32,
        )

    def form(t, leave, arrive, fresh):
        local, near_at, far_at = pair_of(t)
        flags = [
            [
                (live(near_at, far_at, i, j) | live(far_at, near_at, j, i)).astype(jnp.float32)
                for j in range(halves)
            ]
            for i in range(halves)
        ]
        fars = [
            [far_rep[far_at, c, :, j * BLOCK : (j + 1) * BLOCK] for c in range(3)]
            for j in range(halves)
        ]
        for strip in range(width // 16):
            i = strip * 16 // BLOCK
            nears = []
            for part in range(2):
                at = strip * 16 + part * 8
                if fresh:
                    cols_now = near_pos[local, at : at + 8, :]
                    now = [jnp.broadcast_to(cols_now[:, c : c + 1], (8, BLOCK)) for c in range(3)]
                    for c in range(3):
                        near_rep[local, c, at : at + 8, :] = now[c]
                else:
                    now = [near_rep[local, c, at : at + 8, :] for c in range(3)]
                nears.append(now)
            for j in range(halves):
                cols = slice(j * BLOCK, (j + 1) * BLOCK)
                parts = []
                for part in range(2):
                    at = strip * 16 + part * 8
                    dx, dy, dz = (f - n for f, n in zip(fars[j], nears[part]))
                    spacing = dx * dx + dy * dy + dz * dz + SOFTEN
                    inverse = 1.0 / spacing
                    product = jnp.maximum(leave[at : at + 8, cols], 0.0) * jnp.maximum(
                        arrive[at : at + 8, cols], 0.0
                    )
                    parts.append(product * inverse * inverse)
                strip_now = jnp.concatenate(parts, axis=0).astype(jnp.bfloat16)
                tiles[t, strip * 16 : strip * 16 + 16, cols] = strip_now * flags[i][j].astype(jnp.bfloat16)

    def apply(t):
        local, near_at, far_at = pair_of(t)
        tile = tiles[t]
        to_near = lax.dot_general(
            held[far_at, 0:bands, :], tile, (((1,), (1,)), ((), ())), preferred_element_type=jnp.float32
        )
        to_far = lax.dot_general(
            held[near_at, 0:bands, :], tile, (((1,), (0,)), ((), ())), preferred_element_type=jnp.float32
        )
        sums[near_at] = sums[near_at] + to_near
        mirrored = (near_at != far_at).astype(jnp.float32)
        sums[far_at] = sums[far_at] + to_far * mirrored

    def two_steps(fresh, i, carry):
        for part, (now, later) in enumerate(((even, odd), (odd, even))):
            t = 2 * i + part
            apply(jnp.where(t == 0, n_pairs, t - 1))
            project(t + 1, *later)
            form(t, *now, fresh)
        return carry

    even, odd = (leave_even, arrive_even), (leave_odd, arrive_odd)
    project(0, *even)
    lax.fori_loop(0, n_new // 2, functools.partial(two_steps, True), 0)
    lax.fori_loop(n_new // 2, n_pairs // 2, functools.partial(two_steps, False), 0)
    apply(n_pairs - 1)
    if not last:
        return
    total = jnp.zeros((bands, width), jnp.float32)
    for k in range(n_seg):
        base = held[k, 0:bands, :].astype(jnp.float32)
        gain = held[k, bands : 2 * bands, :].astype(jnp.float32)
        weighted = (base + gain * sums[k]).astype(jnp.bfloat16)
        if k < n_old:
            t, over = own_tile(k, n_old)
            tile = old_tiles[t]
        else:
            tile, over = tiles[n_tri + k - n_old], 0
        total += lax.dot_general(
            weighted, tile, (((1,), (over,)), ((), ())), preferred_element_type=jnp.float32
        )
    out[...] = emi[...] + ref[...] * total


def grow(n_old, n_new, seg_bits, col_bits, n_far, held, rest):
    rows, width = held.shape[1:]
    bands = (rows - GEO_ROWS) // 2
    n_seg = n_old + n_new
    bits = n_seg.bit_length() - 1
    last = bits == seg_bits
    n_pairs = triangle(n_new) + n_new * n_old
    vmem = pl.BlockSpec(memory_space=pltpu.VMEM)
    state = [
        pltpu.VMEM((n_pairs + 1, width, width), jnp.bfloat16),
        pltpu.VMEM((n_seg, bands, width), jnp.float32),
    ]
    if last:
        args = (rest[0], rest[1], held, rest[2], rest[3])
        outs = jax.ShapeDtypeStruct((bands, width), jnp.float32)
    else:
        args, outs = (held,), state[::-1]
    pieces = 48
    work = n_pairs * width * width
    return pl.pallas_call(
        functools.partial(grow_kernel, n_old, n_new, bits, seg_bits, col_bits, n_far, last),
        out_shape=outs,
        in_specs=[vmem] * len(args),
        out_specs=vmem if last else [vmem, vmem],
        scratch_shapes=(state if last else [])
        + [
            pltpu.VMEM((n_seg, 8, width), jnp.float32),
            pltpu.VMEM((n_new, 8, width), jnp.float32),
            pltpu.VMEM((n_seg, 3, 8, width), jnp.float32),
            pltpu.VMEM((n_new, width, BLOCK), jnp.float32),
            pltpu.VMEM((n_new, 3, width, BLOCK), jnp.float32),
            pltpu.VMEM((n_new, width, pieces), jnp.bfloat16),
            pltpu.VMEM((n_new, width, pieces), jnp.bfloat16),
            *[pltpu.VMEM((width, width), jnp.float32)] * 4,
            pltpu.VMEM((n_seg, BLOCK), jnp.int32),
            pltpu.SMEM((n_seg, BLOCK), jnp.int32),
            pltpu.SemaphoreType.DMA,
        ],
        compiler_params=pltpu.CompilerParams(vmem_limit_bytes=32 * 1024 * 1024),
        cost_estimate=pl.CostEstimate(
            flops=work * (4 * pieces + 4 * bands), bytes_accessed=held.size * 2, transcendentals=work
        ),
    )(*args)


def one_exchange(positions, normals, areas, emission, reflect, pair_row, pair_col, pair_live):
    n_row = lax.axis_size("row")
    n_col = lax.axis_size("col")
    n_seg = n_row * n_col
    seg_bits = n_seg.bit_length() - 1
    col_bits = n_col.bit_length() - 1
    bands, width = emission.shape
    n_far = width // BLOCK * n_row
    rows = 2 * bands + GEO_ROWS
    vmem = pl.BlockSpec(memory_space=pltpu.VMEM)
    smem = pl.BlockSpec(memory_space=pltpu.SMEM)
    packed = pl.pallas_call(
        functools.partial(pack_kernel, col_bits, n_far),
        out_shape=pltpu.VMEM((rows, width), jnp.bfloat16),
        in_specs=[vmem] * 5 + [smem] * 3,
        out_specs=vmem,
    )(positions, normals, areas.reshape(1, width), emission, reflect, pair_row, pair_col, pair_live)
    gathered = packed[None]
    state = ()
    for bit in reversed(range(seg_bits)):
        arrived = lax.ppermute(
            gathered, ("row", "col"), [(i, i ^ (1 << bit)) for i in range(n_seg)]
        )
        if bit == 0:
            state = grow(0, n_seg // 2, seg_bits, col_bits, n_far, gathered, ())
        gathered = jnp.concatenate([gathered, arrived])
    half = n_seg // 2
    return grow(half, half, seg_bits, col_bits, n_far, gathered, (emission, reflect, *state))


def form_tiles(near, far):
    offset = far[0:3, :, None, :] - near[0:3, :, :, None]
    leaving = jnp.sum(near[3:6, :, :, None] * offset, axis=0)
    arriving = -jnp.sum(far[3:6, :, None, :] * offset, axis=0)
    spacing = jnp.sum(offset * offset, axis=0) + SOFTEN
    return jax.nn.relu(leaving) * jax.nn.relu(arriving) / (math.pi * spacing * spacing)


def two_exchanges(positions, normals, areas, emission, reflect, pair_row, pair_col, pair_live):
    patch_dev = areas.shape[0]
    own_blocks = patch_dev // BLOCK
    n_row = lax.axis_size("row")
    n_col = lax.axis_size("col")
    row_blocks = own_blocks * n_col
    col_blocks = own_blocks * n_row
    all_blocks = row_blocks * n_row
    band_half = emission.shape[0]
    row_here = lax.axis_index("row")
    col_here = lax.axis_index("col")
    geometry = jnp.concatenate([positions, normals], axis=0)
    geo_rows = lax.all_gather(geometry, "col", axis=1, tiled=True).reshape(6, row_blocks, BLOCK)
    geo_cols = lax.all_gather(geometry, "row", axis=1, tiled=True).reshape(6, col_blocks, BLOCK)
    slots = pair_row.shape[0]
    rows_seen, cols_seen, live_seen = (
        lax.all_gather(pair_row, ("row", "col"), axis=0, tiled=True),
        lax.all_gather(pair_col, ("row", "col"), axis=0, tiled=True),
        lax.all_gather(pair_live, ("row", "col"), axis=0, tiled=True),
    )
    seen = jnp.zeros((all_blocks * all_blocks,), jnp.int32)
    seen = seen.at[rows_seen * all_blocks + cols_seen].max(live_seen)
    seen = seen.at[cols_seen * all_blocks + rows_seen].max(live_seen)
    near_grid = row_here * row_blocks + jnp.arange(row_blocks, dtype=jnp.int32)
    far_local = jnp.arange(col_blocks, dtype=jnp.int32)
    far_grid = (far_local // own_blocks * n_col + col_here) * own_blocks + far_local % own_blocks
    flags = seen[(near_grid[:, None] * all_blocks + far_grid[None, :]).reshape(-1)]
    order = jnp.argsort(1 - flags, stable=True)
    near_index = order // col_blocks
    far_index = order % col_blocks
    live_float = flags[order].astype(jnp.float32)
    live_count = jnp.sum(flags)
    group_size = math.gcd(slots, 32)
    turns = (live_count + group_size - 1) // group_size
    stored_init = jnp.zeros((1, 1, 1), jnp.bfloat16)
    stored = stored_init
    radiosity = emission
    for sweep in range(ITERS):
        weighted = (areas[None, :] * radiosity).astype(jnp.bfloat16)
        w_cols = lax.all_gather(weighted, "row", axis=1, tiled=True).reshape(
            band_half, col_blocks, BLOCK
        )

        def one_turn(turn_index, state_now):
            acc_rows, acc_cols, kept = state_now
            first_slot = turn_index * group_size
            near_now = lax.dynamic_slice_in_dim(near_index, first_slot, group_size)
            far_now = lax.dynamic_slice_in_dim(far_index, first_slot, group_size)
            live_now = lax.dynamic_slice_in_dim(live_float, first_slot, group_size)
            tiles_now = form_tiles(geo_rows[:, near_now], geo_cols[:, far_now]).astype(jnp.bfloat16)
            far_weights = w_cols[:, far_now]
            to_rows = jnp.einsum(
                "buv,kbv->kbu", tiles_now, far_weights, preferred_element_type=jnp.float32
            )
            acc_rows = acc_rows.at[:, near_now].add(to_rows * live_now[None, :, None])
            return (acc_rows, acc_cols, kept)

        zero_rows = jnp.zeros((band_half, row_blocks, BLOCK), jnp.float32)
        zero_cols = jnp.zeros((1, 1, 1), jnp.float32)
        acc_rows, acc_cols, stored = lax.fori_loop(
            0, turns, one_turn, (zero_rows, zero_cols, stored)
        )
        row_sum = lax.psum_scatter(
            acc_rows.reshape(band_half, row_blocks * BLOCK), "col", scatter_dimension=1, tiled=True
        )
        radiosity = emission + reflect * row_sum
    return radiosity


def shards(positions, normals, areas, emission, reflect, pair_row, pair_col, pair_live):
    n_row, n_col = lax.axis_size("row"), lax.axis_size("col")
    n_seg = n_row * n_col
    powers = n_row & (n_row - 1) == 0 and n_col & (n_col - 1) == 0
    small = areas.shape[0] == 2 * BLOCK and 8 <= n_seg <= 16
    plan = one_exchange if powers and small else two_exchanges
    return plan(positions, normals, areas, emission, reflect, pair_row, pair_col, pair_live)


def solution(mesh):
    return jax.shard_map(
        shards,
        mesh=mesh,
        in_specs=(
            P(None, ("case", "row", "col")),
            P(None, ("case", "row", "col")),
            P(("case", "row", "col")),
            P("band", ("case", "row", "col")),
            P("band", ("case", "row", "col")),
            P(("case", "row", "col")),
            P(("case", "row", "col")),
            P(("case", "row", "col")),
        ),
        out_specs=P("band", ("case", "row", "col")),
        check_vma=False,
    )
```

```python
import functools
import math

import jax
import jax.numpy as jnp
from jax import lax
from jax.experimental import pallas as pl
from jax.experimental.pallas import tpu as pltpu
from jax.sharding import PartitionSpec as P

BLOCK = 128
ITERS = 2


SOFTEN = 0.02

GEO_ROWS = 32
FLAG_ROW = 6


def bit_reverse(value, bits):
    out = value * 0
    for bit in range(bits):
        out = out | (((value >> bit) & 1) << (bits - 1 - bit))
    return out


def three_pieces(x):
    high = x.astype(jnp.bfloat16).astype(jnp.float32)
    rest = x - high
    middle = rest.astype(jnp.bfloat16).astype(jnp.float32)
    return high, middle, rest - middle


def pack_kernel(col_bits, n_far, pos, nrm, area, emi, ref, prow, pcol, plive, out):
    seg = (lax.axis_index("row") << col_bits) | lax.axis_index("col")
    bands, width = emi.shape
    a = area[...]
    out[0:bands, :] = (a * emi[...]).astype(jnp.bfloat16)
    out[bands : 2 * bands, :] = (a * ref[...]).astype(jnp.bfloat16)
    lane = lax.broadcasted_iota(jnp.int32, (1, width), 1)
    col_mask = (1 << col_bits) - 1

    def add_slot(i, flags):
        p, q = prow[i], pcol[i]
        near = ((((p >> 1) ^ seg) & col_mask) << 1) | (p & 1)
        far = ((((q >> 1) ^ seg) >> col_bits) << 1) | (q & 1)
        return flags + jnp.where(lane == near * n_far + far, plive[i], 0)

    flags = lax.fori_loop(0, prow.shape[0], add_slot, jnp.zeros((1, width), jnp.int32), unroll=True)
    geo = jnp.concatenate(
        [pos[...], nrm[...], flags.astype(jnp.float32), jnp.zeros((1, width), jnp.float32)], axis=0
    )
    out[2 * bands : 2 * bands + GEO_ROWS, :] = jnp.concatenate(
        [*three_pieces(geo), jnp.zeros((8, width), jnp.float32)], axis=0
    ).astype(jnp.bfloat16)


def near_stack(x):
    high, middle, low = three_pieces(x)
    return jnp.concatenate([high, high, middle, high, low, middle], axis=0)


def far_stack(x):
    high, middle, low = three_pieces(x)
    return jnp.concatenate([high, middle, high, low, high, middle], axis=0).astype(jnp.bfloat16)


def triangle(count):
    return count * (count + 1) // 2


def own_tile(k, count):
    if k <= count // 2:
        return k * count, 1
    return (count - k) * count + k, 0


def grow_kernel(n_old, n_new, bits, seg_bits, col_bits, n_far, last, *refs):
    if last:
        emi, ref, held, old_sums, old_tiles, out, tiles, sums, *scratch = refs
    else:
        held, sums, tiles, *scratch = refs
    (
        geo_all, centre, far_rep, near_pos, near_rep, near_leave, near_arrive,
        leave_even, arrive_even, leave_odd, arrive_odd, flag_vec, flag_sm, sem,
    ) = scratch
    n_seg = n_old + n_new
    bands, width = held.shape[1] // 2 - GEO_ROWS // 2, held.shape[2]
    n_tri = triangle(n_new)
    n_pairs = n_tri + n_new * n_old
    halves = width // BLOCK
    geo_at = 2 * bands
    for k in range(n_seg):
        piece = held[k, geo_at : geo_at + GEO_ROWS, :].astype(jnp.float32)
        geo = (piece[0:8] + piece[8:16]) + piece[16:24]
        geo_all[k] = geo
        flag_vec[k : k + 1, :] = geo[FLAG_ROW : FLAG_ROW + 1, 0:BLOCK].astype(jnp.int32)
    flag_copy = pltpu.make_async_copy(flag_vec, flag_sm, sem)
    flag_copy.start()
    if n_old:
        sums[0:n_old] = old_sums[...]
    sums[n_old:n_seg] = jnp.zeros((n_new, bands, width), jnp.float32)
    tiles[n_pairs] = jnp.zeros((width, width), jnp.bfloat16)
    row = lax.broadcasted_iota(jnp.int32, (8, width), 0)
    for k in range(n_seg):
        geo = geo_all[k]
        for c in range(3):
            far_rep[k, c] = jnp.broadcast_to(geo[c : c + 1], (8, width))
        if k < n_old:
            continue
        at = k - n_old
        near_pos[at, :, 0:8] = jnp.transpose(geo)
        middle = jnp.broadcast_to(geo[:, 0:1], (8, width))
        centre[at] = middle
        offset = jnp.where(row < 3, geo - middle, 0.0)
        normal = jnp.where(row < 3, pltpu.roll(geo, 5, 0), 0.0)
        along = jnp.sum(normal * offset, axis=0, keepdims=True)
        near_leave[at] = jnp.transpose(near_stack(jnp.where(row == 3, -along, normal))).astype(jnp.bfloat16)
        near_arrive[at] = jnp.transpose(near_stack(jnp.where(row == 3, 1.0, -offset))).astype(jnp.bfloat16)
    flag_copy.wait()
    col_mask = (1 << col_bits) - 1

    def pair_of(t):
        t = jnp.int32(t)
        near = t % n_new
        far = (near + t // n_new) % n_new + n_old
        if n_old:
            far = jnp.where(t < n_tri, far, jnp.minimum((t - n_tri) // n_new, n_old - 1))
            near = jnp.where(t < n_tri, near, (t - n_tri) % n_new)
        return near, near + n_old, far

    def live(near_at, far_at, i, j):
        near = bit_reverse(near_at, bits) << (seg_bits - bits)
        far = bit_reverse(far_at, bits) << (seg_bits - bits)
        holder = (near & ~col_mask) | (far & col_mask)
        apart = near ^ far
        index = ((((apart & col_mask) << 1) | i) * n_far) + (((apart >> col_bits) << 1) | j)
        return flag_sm[bit_reverse(holder >> (seg_bits - bits), bits), index]

    def project(t, leave, arrive):
        local, near_at, far_at = pair_of(t)
        geo = geo_all[far_at]
        offset = jnp.where(row < 3, geo - centre[local], 0.0)
        normal = jnp.where(row < 3, pltpu.roll(geo, 5, 0), 0.0) * (-1.0 / math.pi)
        along = jnp.sum(normal * offset, axis=0, keepdims=True)
        leave[...] = jnp.dot(
            near_leave[local], far_stack(jnp.where(row == 3, 1.0, offset)),
            preferred_element_type=jnp.float32,
        )
        arrive[...] = jnp.dot(
            near_arrive[local], far_stack(jnp.where(row == 3, along, normal)),
            preferred_element_type=jnp.float32,
        )

    def form(t, leave, arrive, fresh):
        local, near_at, far_at = pair_of(t)
        flags = [
            [
                (live(near_at, far_at, i, j) | live(far_at, near_at, j, i)).astype(jnp.float32)
                for j in range(halves)
            ]
            for i in range(halves)
        ]
        fars = [
            [far_rep[far_at, c, :, j * BLOCK : (j + 1) * BLOCK] for c in range(3)]
            for j in range(halves)
        ]
        for strip in range(width // 16):
            i = strip * 16 // BLOCK
            nears = []
            for part in range(2):
                at = strip * 16 + part * 8
                if fresh:
                    cols_now = near_pos[local, at : at + 8, :]
                    now = [jnp.broadcast_to(cols_now[:, c : c + 1], (8, BLOCK)) for c in range(3)]
                    for c in range(3):
                        near_rep[local, c, at : at + 8, :] = now[c]
                else:
                    now = [near_rep[local, c, at : at + 8, :] for c in range(3)]
                nears.append(now)
            for j in range(halves):
                cols = slice(j * BLOCK, (j + 1) * BLOCK)
                parts = []
                for part in range(2):
                    at = strip * 16 + part * 8
                    dx, dy, dz = (f - n for f, n in zip(fars[j], nears[part]))
                    spacing = dx * dx + dy * dy + dz * dz + SOFTEN
                    inverse = 1.0 / spacing
                    product = jnp.maximum(leave[at : at + 8, cols], 0.0) * jnp.maximum(
                        arrive[at : at + 8, cols], 0.0
                    )
                    parts.append(product * inverse * inverse)
                strip_now = jnp.concatenate(parts, axis=0).astype(jnp.bfloat16)
                tiles[t, strip * 16 : strip * 16 + 16, cols] = strip_now * flags[i][j].astype(jnp.bfloat16)

    def apply(t):
        local, near_at, far_at = pair_of(t)
        tile = tiles[t]
        to_near = lax.dot_general(
            held[far_at, 0:bands, :], tile, (((1,), (1,)), ((), ())), preferred_element_type=jnp.float32
        )
        to_far = lax.dot_general(
            held[near_at, 0:bands, :], tile, (((1,), (0,)), ((), ())), preferred_element_type=jnp.float32
        )
        sums[near_at] = sums[near_at] + to_near
        mirrored = (near_at != far_at).astype(jnp.float32)
        sums[far_at] = sums[far_at] + to_far * mirrored

    def two_steps(fresh, i, carry):
        for part, (now, later) in enumerate(((even, odd), (odd, even))):
            t = 2 * i + part
            apply(jnp.where(t == 0, n_pairs, t - 1))
            project(t + 1, *later)
            form(t, *now, fresh)
        return carry

    even, odd = (leave_even, arrive_even), (leave_odd, arrive_odd)
    project(0, *even)
    lax.fori_loop(0, n_new // 2, functools.partial(two_steps, True), 0)
    lax.fori_loop(n_new // 2, n_pairs // 2, functools.partial(two_steps, False), 0)
    apply(n_pairs - 1)
    if not last:
        return
    total = jnp.zeros((bands, width), jnp.float32)
    for k in range(n_seg):
        base = held[k, 0:bands, :].astype(jnp.float32)
        gain = held[k, bands : 2 * bands, :].astype(jnp.float32)
        weighted = (base + gain * sums[k]).astype(jnp.bfloat16)
        if k < n_old:
            t, over = own_tile(k, n_old)
            tile = old_tiles[t]
        else:
            tile, over = tiles[n_tri + k - n_old], 0
        total += lax.dot_general(
            weighted, tile, (((1,), (over,)), ((), ())), preferred_element_type=jnp.float32
        )
    out[...] = emi[...] + ref[...] * total


def grow(n_old, n_new, seg_bits, col_bits, n_far, held, rest):
    rows, width = held.shape[1:]
    bands = (rows - GEO_ROWS) // 2
    n_seg = n_old + n_new
    bits = n_seg.bit_length() - 1
    last = bits == seg_bits
    n_pairs = triangle(n_new) + n_new * n_old
    vmem = pl.BlockSpec(memory_space=pltpu.VMEM)
    state = [
        pltpu.VMEM((n_pairs + 1, width, width), jnp.bfloat16),
        pltpu.VMEM((n_seg, bands, width), jnp.float32),
    ]
    if last:
        args = (rest[0], rest[1], held, rest[2], rest[3])
        outs = jax.ShapeDtypeStruct((bands, width), jnp.float32)
    else:
        args, outs = (held,), state[::-1]
    pieces = 48
    work = n_pairs * width * width
    return pl.pallas_call(
        functools.partial(grow_kernel, n_old, n_new, bits, seg_bits, col_bits, n_far, last),
        out_shape=outs,
        in_specs=[vmem] * len(args),
        out_specs=vmem if last else [vmem, vmem],
        scratch_shapes=(state if last else [])
        + [
            pltpu.VMEM((n_seg, 8, width), jnp.float32),
            pltpu.VMEM((n_new, 8, width), jnp.float32),
            pltpu.VMEM((n_seg, 3, 8, width), jnp.float32),
            pltpu.VMEM((n_new, width, BLOCK), jnp.float32),
            pltpu.VMEM((n_new, 3, width, BLOCK), jnp.float32),
            pltpu.VMEM((n_new, width, pieces), jnp.bfloat16),
            pltpu.VMEM((n_new, width, pieces), jnp.bfloat16),
            *[pltpu.VMEM((width, width), jnp.float32)] * 4,
            pltpu.VMEM((n_seg, BLOCK), jnp.int32),
            pltpu.SMEM((n_seg, BLOCK), jnp.int32),
            pltpu.SemaphoreType.DMA,
        ],
        compiler_params=pltpu.CompilerParams(vmem_limit_bytes=32 * 1024 * 1024),
        cost_estimate=pl.CostEstimate(
            flops=work * (4 * pieces + 4 * bands), bytes_accessed=held.size * 2, transcendentals=work
        ),
    )(*args)


def one_exchange(positions, normals, areas, emission, reflect, pair_row, pair_col, pair_live):
    n_row = lax.axis_size("row")
    n_col = lax.axis_size("col")
    n_seg = n_row * n_col
    seg_bits = n_seg.bit_length() - 1
    col_bits = n_col.bit_length() - 1
    bands, width = emission.shape
    n_far = width // BLOCK * n_row
    rows = 2 * bands + GEO_ROWS
    vmem = pl.BlockSpec(memory_space=pltpu.VMEM)
    smem = pl.BlockSpec(memory_space=pltpu.SMEM)
    packed = pl.pallas_call(
        functools.partial(pack_kernel, col_bits, n_far),
        out_shape=pltpu.VMEM((rows, width), jnp.bfloat16),
        in_specs=[vmem] * 5 + [smem] * 3,
        out_specs=vmem,
    )(positions, normals, areas.reshape(1, width), emission, reflect, pair_row, pair_col, pair_live)
    gathered = packed[None]

    def swap(value, distance):
        return lax.ppermute(value, ("row", "col"), [(i, i ^ distance) for i in range(n_seg)])

    for bit in reversed(range(2, seg_bits)):
        gathered = jnp.concatenate([gathered, swap(gathered, 1 << bit)])
    beside, across, diagonal = (swap(gathered, distance) for distance in (2, 1, 3))
    gathered = jnp.concatenate([gathered, beside])
    state = grow(0, n_seg // 2, seg_bits, col_bits, n_far, gathered, ())
    gathered = jnp.concatenate([gathered, across, diagonal])
    half = n_seg // 2
    return grow(half, half, seg_bits, col_bits, n_far, gathered, (emission, reflect, *state))


def form_tiles(near, far):
    offset = far[0:3, :, None, :] - near[0:3, :, :, None]
    leaving = jnp.sum(near[3:6, :, :, None] * offset, axis=0)
    arriving = -jnp.sum(far[3:6, :, None, :] * offset, axis=0)
    spacing = jnp.sum(offset * offset, axis=0) + SOFTEN
    return jax.nn.relu(leaving) * jax.nn.relu(arriving) / (math.pi * spacing * spacing)


def two_exchanges(positions, normals, areas, emission, reflect, pair_row, pair_col, pair_live):
    patch_dev = areas.shape[0]
    own_blocks = patch_dev // BLOCK
    n_row = lax.axis_size("row")
    n_col = lax.axis_size("col")
    row_blocks = own_blocks * n_col
    col_blocks = own_blocks * n_row
    all_blocks = row_blocks * n_row
    band_half = emission.shape[0]
    row_here = lax.axis_index("row")
    col_here = lax.axis_index("col")
    geometry = jnp.concatenate([positions, normals], axis=0)
    geo_rows = lax.all_gather(geometry, "col", axis=1, tiled=True).reshape(6, row_blocks, BLOCK)
    geo_cols = lax.all_gather(geometry, "row", axis=1, tiled=True).reshape(6, col_blocks, BLOCK)
    slots = pair_row.shape[0]
    rows_seen, cols_seen, live_seen = (
        lax.all_gather(pair_row, ("row", "col"), axis=0, tiled=True),
        lax.all_gather(pair_col, ("row", "col"), axis=0, tiled=True),
        lax.all_gather(pair_live, ("row", "col"), axis=0, tiled=True),
    )
    seen = jnp.zeros((all_blocks * all_blocks,), jnp.int32)
    seen = seen.at[rows_seen * all_blocks + cols_seen].max(live_seen)
    seen = seen.at[cols_seen * all_blocks + rows_seen].max(live_seen)
    near_grid = row_here * row_blocks + jnp.arange(row_blocks, dtype=jnp.int32)
    far_local = jnp.arange(col_blocks, dtype=jnp.int32)
    far_grid = (far_local // own_blocks * n_col + col_here) * own_blocks + far_local % own_blocks
    flags = seen[(near_grid[:, None] * all_blocks + far_grid[None, :]).reshape(-1)]
    order = jnp.argsort(1 - flags, stable=True)
    near_index = order // col_blocks
    far_index = order % col_blocks
    live_float = flags[order].astype(jnp.float32)
    live_count = jnp.sum(flags)
    group_size = math.gcd(slots, 32)
    turns = (live_count + group_size - 1) // group_size
    stored_init = jnp.zeros((1, 1, 1), jnp.bfloat16)
    stored = stored_init
    radiosity = emission
    for sweep in range(ITERS):
        weighted = (areas[None, :] * radiosity).astype(jnp.bfloat16)
        w_cols = lax.all_gather(weighted, "row", axis=1, tiled=True).reshape(
            band_half, col_blocks, BLOCK
        )

        def one_turn(turn_index, state_now):
            acc_rows, acc_cols, kept = state_now
            first_slot = turn_index * group_size
            near_now = lax.dynamic_slice_in_dim(near_index, first_slot, group_size)
            far_now = lax.dynamic_slice_in_dim(far_index, first_slot, group_size)
            live_now = lax.dynamic_slice_in_dim(live_float, first_slot, group_size)
            tiles_now = form_tiles(geo_rows[:, near_now], geo_cols[:, far_now]).astype(jnp.bfloat16)
            far_weights = w_cols[:, far_now]
            to_rows = jnp.einsum(
                "buv,kbv->kbu", tiles_now, far_weights, preferred_element_type=jnp.float32
            )
            acc_rows = acc_rows.at[:, near_now].add(to_rows * live_now[None, :, None])
            return (acc_rows, acc_cols, kept)

        zero_rows = jnp.zeros((band_half, row_blocks, BLOCK), jnp.float32)
        zero_cols = jnp.zeros((1, 1, 1), jnp.float32)
        acc_rows, acc_cols, stored = lax.fori_loop(
            0, turns, one_turn, (zero_rows, zero_cols, stored)
        )
        row_sum = lax.psum_scatter(
            acc_rows.reshape(band_half, row_blocks * BLOCK), "col", scatter_dimension=1, tiled=True
        )
        radiosity = emission + reflect * row_sum
    return radiosity


def shards(positions, normals, areas, emission, reflect, pair_row, pair_col, pair_live):
    n_row, n_col = lax.axis_size("row"), lax.axis_size("col")
    n_seg = n_row * n_col
    powers = n_row & (n_row - 1) == 0 and n_col & (n_col - 1) == 0
    small = areas.shape[0] == 2 * BLOCK and 8 <= n_seg <= 16
    plan = one_exchange if powers and small else two_exchanges
    return plan(positions, normals, areas, emission, reflect, pair_row, pair_col, pair_live)


def solution(mesh):
    return jax.shard_map(
        shards,
        mesh=mesh,
        in_specs=(
            P(None, ("case", "row", "col")),
            P(None, ("case", "row", "col")),
            P(("case", "row", "col")),
            P("band", ("case", "row", "col")),
            P("band", ("case", "row", "col")),
            P(("case", "row", "col")),
            P(("case", "row", "col")),
            P(("case", "row", "col")),
        ),
        out_specs=P("band", ("case", "row", "col")),
        check_vma=False,
    )
```

```python
import functools
import math

import jax
import jax.numpy as jnp
from jax import lax
from jax.experimental import pallas as pl
from jax.experimental.pallas import tpu as pltpu
from jax.sharding import PartitionSpec as P

BLOCK = 128
ITERS = 2


SOFTEN = 0.02

GEO_ROWS = 32
FLAG_ROW = 6


def bit_reverse(value, bits):
    out = value * 0
    for bit in range(bits):
        out = out | (((value >> bit) & 1) << (bits - 1 - bit))
    return out


def three_pieces(x):
    high = x.astype(jnp.bfloat16).astype(jnp.float32)
    rest = x - high
    middle = rest.astype(jnp.bfloat16).astype(jnp.float32)
    return high, middle, rest - middle


def pack_kernel(col_bits, n_far, pos, nrm, area, emi, ref, prow, pcol, plive, out):
    seg = (lax.axis_index("row") << col_bits) | lax.axis_index("col")
    bands, width = emi.shape
    a = area[...]
    out[0:bands, :] = (a * emi[...]).astype(jnp.bfloat16)
    out[bands : 2 * bands, :] = (a * ref[...]).astype(jnp.bfloat16)
    lane = lax.broadcasted_iota(jnp.int32, (1, width), 1)
    col_mask = (1 << col_bits) - 1

    def add_slot(i, flags):
        p, q = prow[i], pcol[i]
        near = ((((p >> 1) ^ seg) & col_mask) << 1) | (p & 1)
        far = ((((q >> 1) ^ seg) >> col_bits) << 1) | (q & 1)
        return flags + jnp.where(lane == near * n_far + far, plive[i], 0)

    flags = lax.fori_loop(0, prow.shape[0], add_slot, jnp.zeros((1, width), jnp.int32), unroll=True)
    geo = jnp.concatenate(
        [pos[...], nrm[...], flags.astype(jnp.float32), jnp.zeros((1, width), jnp.float32)], axis=0
    )
    out[2 * bands : 2 * bands + GEO_ROWS, :] = jnp.concatenate(
        [*three_pieces(geo), jnp.zeros((8, width), jnp.float32)], axis=0
    ).astype(jnp.bfloat16)


def near_stack(x):
    high, middle, low = three_pieces(x)
    return jnp.concatenate([high, high, middle, high, low, middle], axis=0)


def far_stack(x):
    high, middle, low = three_pieces(x)
    return jnp.concatenate([high, middle, high, low, high, middle], axis=0).astype(jnp.bfloat16)


def triangle(count):
    return count * (count + 1) // 2


def own_tile(k, count):
    if k <= count // 2:
        return k * count, 1
    return (count - k) * count + k, 0


def grow_kernel(n_old, n_new, bits, seg_bits, col_bits, n_far, last, *refs):
    if last:
        diagonal, across, known, emi, ref, old_sums, old_tiles, out, tiles, sums, held, *scratch = refs
        at = 0
        for part in (known, across, diagonal):
            held[at : at + part.shape[0]] = part[...]
            at += part.shape[0]
    else:
        held, sums, tiles, *scratch = refs
    (
        geo_all, centre, far_rep, near_pos, near_rep, near_leave, near_arrive,
        leave_even, arrive_even, leave_odd, arrive_odd, flag_vec, flag_sm, sem,
    ) = scratch
    n_seg = n_old + n_new
    bands, width = held.shape[1] // 2 - GEO_ROWS // 2, held.shape[2]
    n_tri = triangle(n_new)
    n_pairs = n_tri + n_new * n_old
    halves = width // BLOCK
    geo_at = 2 * bands
    for k in range(n_seg):
        piece = held[k, geo_at : geo_at + GEO_ROWS, :].astype(jnp.float32)
        geo = (piece[0:8] + piece[8:16]) + piece[16:24]
        geo_all[k] = geo
        flag_vec[k : k + 1, :] = geo[FLAG_ROW : FLAG_ROW + 1, 0:BLOCK].astype(jnp.int32)
    flag_copy = pltpu.make_async_copy(flag_vec, flag_sm, sem)
    flag_copy.start()
    if n_old:
        sums[0:n_old] = old_sums[...]
    sums[n_old:n_seg] = jnp.zeros((n_new, bands, width), jnp.float32)
    tiles[n_pairs] = jnp.zeros((width, width), jnp.bfloat16)
    row = lax.broadcasted_iota(jnp.int32, (8, width), 0)
    for k in range(n_seg):
        geo = geo_all[k]
        for c in range(3):
            far_rep[k, c] = jnp.broadcast_to(geo[c : c + 1], (8, width))
        if k < n_old:
            continue
        at = k - n_old
        near_pos[at, :, 0:8] = jnp.transpose(geo)
        middle = jnp.broadcast_to(geo[:, 0:1], (8, width))
        centre[at] = middle
        offset = jnp.where(row < 3, geo - middle, 0.0)
        normal = jnp.where(row < 3, pltpu.roll(geo, 5, 0), 0.0)
        along = jnp.sum(normal * offset, axis=0, keepdims=True)
        near_leave[at] = jnp.transpose(near_stack(jnp.where(row == 3, -along, normal))).astype(jnp.bfloat16)
        near_arrive[at] = jnp.transpose(near_stack(jnp.where(row == 3, 1.0, -offset))).astype(jnp.bfloat16)
    flag_copy.wait()
    col_mask = (1 << col_bits) - 1

    def pair_of(t):
        t = jnp.int32(t)
        near = t % n_new
        far = (near + t // n_new) % n_new + n_old
        if n_old:
            far = jnp.where(t < n_tri, far, jnp.minimum((t - n_tri) // n_new, n_old - 1))
            near = jnp.where(t < n_tri, near, (t - n_tri) % n_new)
        return near, near + n_old, far

    def live(near_at, far_at, i, j):
        near = bit_reverse(near_at, bits) << (seg_bits - bits)
        far = bit_reverse(far_at, bits) << (seg_bits - bits)
        holder = (near & ~col_mask) | (far & col_mask)
        apart = near ^ far
        index = ((((apart & col_mask) << 1) | i) * n_far) + (((apart >> col_bits) << 1) | j)
        return flag_sm[bit_reverse(holder >> (seg_bits - bits), bits), index]

    def project(t, leave, arrive):
        local, near_at, far_at = pair_of(t)
        geo = geo_all[far_at]
        offset = jnp.where(row < 3, geo - centre[local], 0.0)
        normal = jnp.where(row < 3, pltpu.roll(geo, 5, 0), 0.0) * (-1.0 / math.pi)
        along = jnp.sum(normal * offset, axis=0, keepdims=True)
        leave[...] = jnp.dot(
            near_leave[local], far_stack(jnp.where(row == 3, 1.0, offset)),
            preferred_element_type=jnp.float32,
        )
        arrive[...] = jnp.dot(
            near_arrive[local], far_stack(jnp.where(row == 3, along, normal)),
            preferred_element_type=jnp.float32,
        )

    def form(t, leave, arrive, fresh):
        local, near_at, far_at = pair_of(t)
        flags = [
            [
                (live(near_at, far_at, i, j) | live(far_at, near_at, j, i)).astype(jnp.float32)
                for j in range(halves)
            ]
            for i in range(halves)
        ]
        fars = [
            [far_rep[far_at, c, :, j * BLOCK : (j + 1) * BLOCK] for c in range(3)]
            for j in range(halves)
        ]
        for strip in range(width // 16):
            i = strip * 16 // BLOCK
            nears = []
            for part in range(2):
                at = strip * 16 + part * 8
                if fresh:
                    cols_now = near_pos[local, at : at + 8, :]
                    now = [jnp.broadcast_to(cols_now[:, c : c + 1], (8, BLOCK)) for c in range(3)]
                    for c in range(3):
                        near_rep[local, c, at : at + 8, :] = now[c]
                else:
                    now = [near_rep[local, c, at : at + 8, :] for c in range(3)]
                nears.append(now)
            for j in range(halves):
                cols = slice(j * BLOCK, (j + 1) * BLOCK)
                parts = []
                for part in range(2):
                    at = strip * 16 + part * 8
                    dx, dy, dz = (f - n for f, n in zip(fars[j], nears[part]))
                    spacing = dx * dx + dy * dy + dz * dz + SOFTEN
                    inverse = 1.0 / spacing
                    product = jnp.maximum(leave[at : at + 8, cols], 0.0) * jnp.maximum(
                        arrive[at : at + 8, cols], 0.0
                    )
                    parts.append(product * inverse * inverse)
                strip_now = jnp.concatenate(parts, axis=0).astype(jnp.bfloat16)
                tiles[t, strip * 16 : strip * 16 + 16, cols] = strip_now * flags[i][j].astype(jnp.bfloat16)

    def apply(t):
        local, near_at, far_at = pair_of(t)
        tile = tiles[t]
        to_near = lax.dot_general(
            held[far_at, 0:bands, :], tile, (((1,), (1,)), ((), ())), preferred_element_type=jnp.float32
        )
        to_far = lax.dot_general(
            held[near_at, 0:bands, :], tile, (((1,), (0,)), ((), ())), preferred_element_type=jnp.float32
        )
        sums[near_at] = sums[near_at] + to_near
        mirrored = (near_at != far_at).astype(jnp.float32)
        sums[far_at] = sums[far_at] + to_far * mirrored

    def two_steps(fresh, i, carry):
        for part, (now, later) in enumerate(((even, odd), (odd, even))):
            t = 2 * i + part
            apply(jnp.where(t == 0, n_pairs, t - 1))
            project(t + 1, *later)
            form(t, *now, fresh)
        return carry

    even, odd = (leave_even, arrive_even), (leave_odd, arrive_odd)
    project(0, *even)
    lax.fori_loop(0, n_new // 2, functools.partial(two_steps, True), 0)
    lax.fori_loop(n_new // 2, n_pairs // 2, functools.partial(two_steps, False), 0)
    apply(n_pairs - 1)
    if not last:
        return
    total = jnp.zeros((bands, width), jnp.float32)
    for k in range(n_seg):
        base = held[k, 0:bands, :].astype(jnp.float32)
        gain = held[k, bands : 2 * bands, :].astype(jnp.float32)
        weighted = (base + gain * sums[k]).astype(jnp.bfloat16)
        if k < n_old:
            t, over = own_tile(k, n_old)
            tile = old_tiles[t]
        else:
            tile, over = tiles[n_tri + k - n_old], 0
        total += lax.dot_general(
            weighted, tile, (((1,), (over,)), ((), ())), preferred_element_type=jnp.float32
        )
    out[...] = emi[...] + ref[...] * total


def grow(n_old, n_new, seg_bits, col_bits, n_far, args):
    rows, width = args[0].shape[1:]
    bands = (rows - GEO_ROWS) // 2
    n_seg = n_old + n_new
    bits = n_seg.bit_length() - 1
    last = bits == seg_bits
    n_pairs = triangle(n_new) + n_new * n_old
    vmem = pl.BlockSpec(memory_space=pltpu.VMEM)
    state = [
        pltpu.VMEM((n_pairs + 1, width, width), jnp.bfloat16),
        pltpu.VMEM((n_seg, bands, width), jnp.float32),
    ]
    outs = jax.ShapeDtypeStruct((bands, width), jnp.float32) if last else state[::-1]
    pieces = 48
    work = n_pairs * width * width
    return pl.pallas_call(
        functools.partial(grow_kernel, n_old, n_new, bits, seg_bits, col_bits, n_far, last),
        out_shape=outs,
        in_specs=[vmem] * len(args),
        out_specs=vmem if last else [vmem, vmem],
        scratch_shapes=(state + [pltpu.VMEM((n_seg, rows, width), jnp.bfloat16)] if last else [])
        + [
            pltpu.VMEM((n_seg, 8, width), jnp.float32),
            pltpu.VMEM((n_new, 8, width), jnp.float32),
            pltpu.VMEM((n_seg, 3, 8, width), jnp.float32),
            pltpu.VMEM((n_new, width, BLOCK), jnp.float32),
            pltpu.VMEM((n_new, 3, width, BLOCK), jnp.float32),
            pltpu.VMEM((n_new, width, pieces), jnp.bfloat16),
            pltpu.VMEM((n_new, width, pieces), jnp.bfloat16),
            *[pltpu.VMEM((width, width), jnp.float32)] * 4,
            pltpu.VMEM((n_seg, BLOCK), jnp.int32),
            pltpu.SMEM((n_seg, BLOCK), jnp.int32),
            pltpu.SemaphoreType.DMA,
        ],
        compiler_params=pltpu.CompilerParams(vmem_limit_bytes=32 * 1024 * 1024),
        cost_estimate=pl.CostEstimate(
            flops=work * (4 * pieces + 4 * bands), bytes_accessed=n_seg * rows * width * 2, transcendentals=work
        ),
    )(*args)


def one_exchange(positions, normals, areas, emission, reflect, pair_row, pair_col, pair_live):
    n_row = lax.axis_size("row")
    n_col = lax.axis_size("col")
    n_seg = n_row * n_col
    seg_bits = n_seg.bit_length() - 1
    col_bits = n_col.bit_length() - 1
    bands, width = emission.shape
    n_far = width // BLOCK * n_row
    rows = 2 * bands + GEO_ROWS
    vmem = pl.BlockSpec(memory_space=pltpu.VMEM)
    smem = pl.BlockSpec(memory_space=pltpu.SMEM)
    packed = pl.pallas_call(
        functools.partial(pack_kernel, col_bits, n_far),
        out_shape=pltpu.VMEM((rows, width), jnp.bfloat16),
        in_specs=[vmem] * 5 + [smem] * 3,
        out_specs=vmem,
    )(positions, normals, areas.reshape(1, width), emission, reflect, pair_row, pair_col, pair_live)
    gathered = packed[None]

    def swap(value, distance):
        return lax.ppermute(value, ("row", "col"), [(i, i ^ distance) for i in range(n_seg)])

    for bit in reversed(range(2, seg_bits)):
        gathered = jnp.concatenate([gathered, swap(gathered, 1 << bit)])
    beside, across, diagonal = (swap(gathered, distance) for distance in (2, 1, 3))
    gathered = jnp.concatenate([gathered, beside])
    state = grow(0, n_seg // 2, seg_bits, col_bits, n_far, (gathered,))
    half = n_seg // 2
    args = (diagonal, across, gathered, emission, reflect, *state)
    return grow(half, half, seg_bits, col_bits, n_far, args)


def form_tiles(near, far):
    offset = far[0:3, :, None, :] - near[0:3, :, :, None]
    leaving = jnp.sum(near[3:6, :, :, None] * offset, axis=0)
    arriving = -jnp.sum(far[3:6, :, None, :] * offset, axis=0)
    spacing = jnp.sum(offset * offset, axis=0) + SOFTEN
    return jax.nn.relu(leaving) * jax.nn.relu(arriving) / (math.pi * spacing * spacing)


def two_exchanges(positions, normals, areas, emission, reflect, pair_row, pair_col, pair_live):
    patch_dev = areas.shape[0]
    own_blocks = patch_dev // BLOCK
    n_row = lax.axis_size("row")
    n_col = lax.axis_size("col")
    row_blocks = own_blocks * n_col
    col_blocks = own_blocks * n_row
    all_blocks = row_blocks * n_row
    band_half = emission.shape[0]
    row_here = lax.axis_index("row")
    col_here = lax.axis_index("col")
    geometry = jnp.concatenate([positions, normals], axis=0)
    geo_rows = lax.all_gather(geometry, "col", axis=1, tiled=True).reshape(6, row_blocks, BLOCK)
    geo_cols = lax.all_gather(geometry, "row", axis=1, tiled=True).reshape(6, col_blocks, BLOCK)
    slots = pair_row.shape[0]
    rows_seen, cols_seen, live_seen = (
        lax.all_gather(pair_row, ("row", "col"), axis=0, tiled=True),
        lax.all_gather(pair_col, ("row", "col"), axis=0, tiled=True),
        lax.all_gather(pair_live, ("row", "col"), axis=0, tiled=True),
    )
    seen = jnp.zeros((all_blocks * all_blocks,), jnp.int32)
    seen = seen.at[rows_seen * all_blocks + cols_seen].max(live_seen)
    seen = seen.at[cols_seen * all_blocks + rows_seen].max(live_seen)
    near_grid = row_here * row_blocks + jnp.arange(row_blocks, dtype=jnp.int32)
    far_local = jnp.arange(col_blocks, dtype=jnp.int32)
    far_grid = (far_local // own_blocks * n_col + col_here) * own_blocks + far_local % own_blocks
    flags = seen[(near_grid[:, None] * all_blocks + far_grid[None, :]).reshape(-1)]
    order = jnp.argsort(1 - flags, stable=True)
    near_index = order // col_blocks
    far_index = order % col_blocks
    live_float = flags[order].astype(jnp.float32)
    live_count = jnp.sum(flags)
    group_size = math.gcd(slots, 32)
    turns = (live_count + group_size - 1) // group_size
    stored_init = jnp.zeros((1, 1, 1), jnp.bfloat16)
    stored = stored_init
    radiosity = emission
    for sweep in range(ITERS):
        weighted = (areas[None, :] * radiosity).astype(jnp.bfloat16)
        w_cols = lax.all_gather(weighted, "row", axis=1, tiled=True).reshape(
            band_half, col_blocks, BLOCK
        )

        def one_turn(turn_index, state_now):
            acc_rows, acc_cols, kept = state_now
            first_slot = turn_index * group_size
            near_now = lax.dynamic_slice_in_dim(near_index, first_slot, group_size)
            far_now = lax.dynamic_slice_in_dim(far_index, first_slot, group_size)
            live_now = lax.dynamic_slice_in_dim(live_float, first_slot, group_size)
            tiles_now = form_tiles(geo_rows[:, near_now], geo_cols[:, far_now]).astype(jnp.bfloat16)
            far_weights = w_cols[:, far_now]
            to_rows = jnp.einsum(
                "buv,kbv->kbu", tiles_now, far_weights, preferred_element_type=jnp.float32
            )
            acc_rows = acc_rows.at[:, near_now].add(to_rows * live_now[None, :, None])
            return (acc_rows, acc_cols, kept)

        zero_rows = jnp.zeros((band_half, row_blocks, BLOCK), jnp.float32)
        zero_cols = jnp.zeros((1, 1, 1), jnp.float32)
        acc_rows, acc_cols, stored = lax.fori_loop(
            0, turns, one_turn, (zero_rows, zero_cols, stored)
        )
        row_sum = lax.psum_scatter(
            acc_rows.reshape(band_half, row_blocks * BLOCK), "col", scatter_dimension=1, tiled=True
        )
        radiosity = emission + reflect * row_sum
    return radiosity


def shards(positions, normals, areas, emission, reflect, pair_row, pair_col, pair_live):
    n_row, n_col = lax.axis_size("row"), lax.axis_size("col")
    n_seg = n_row * n_col
    powers = n_row & (n_row - 1) == 0 and n_col & (n_col - 1) == 0
    small = areas.shape[0] == 2 * BLOCK and 8 <= n_seg <= 16
    plan = one_exchange if powers and small else two_exchanges
    return plan(positions, normals, areas, emission, reflect, pair_row, pair_col, pair_live)


def solution(mesh):
    return jax.shard_map(
        shards,
        mesh=mesh,
        in_specs=(
            P(None, ("case", "row", "col")),
            P(None, ("case", "row", "col")),
            P(("case", "row", "col")),
            P("band", ("case", "row", "col")),
            P("band", ("case", "row", "col")),
            P(("case", "row", "col")),
            P(("case", "row", "col")),
            P(("case", "row", "col")),
        ),
        out_specs=P("band", ("case", "row", "col")),
        check_vma=False,
    )
```

```python
import functools
import math

import jax
import jax.numpy as jnp
from jax import lax
from jax.experimental import pallas as pl
from jax.experimental.pallas import tpu as pltpu
from jax.sharding import PartitionSpec as P

BLOCK = 128
ITERS = 2


SOFTEN = 0.02

GEO_ROWS = 32
FLAG_ROW = 6
CHUNK = 128
PIECES = 48


def bit_reverse(value, bits):
    out = value * 0
    for bit in range(bits):
        out = out | (((value >> bit) & 1) << (bits - 1 - bit))
    return out


def three_pieces(x):
    high = x.astype(jnp.bfloat16).astype(jnp.float32)
    rest = x - high
    middle = rest.astype(jnp.bfloat16).astype(jnp.float32)
    return high, middle, rest - middle


def pack_kernel(col_bits, n_far, pos, nrm, area, emi, ref, prow, pcol, plive, out):
    seg = (lax.axis_index("row") << col_bits) | lax.axis_index("col")
    bands, width = emi.shape
    a = area[...]
    out[0:bands, :] = (a * emi[...]).astype(jnp.bfloat16)
    out[bands : 2 * bands, :] = (a * ref[...]).astype(jnp.bfloat16)
    lane = lax.broadcasted_iota(jnp.int32, (1, width), 1)
    col_mask = (1 << col_bits) - 1

    def add_slot(i, flags):
        p, q = prow[i], pcol[i]
        near = ((((p >> 1) ^ seg) & col_mask) << 1) | (p & 1)
        far = ((((q >> 1) ^ seg) >> col_bits) << 1) | (q & 1)
        return flags + jnp.where(lane == near * n_far + far, plive[i], 0)

    flags = lax.fori_loop(0, prow.shape[0], add_slot, jnp.zeros((1, width), jnp.int32), unroll=True)
    geo = jnp.concatenate(
        [pos[...], nrm[...], flags.astype(jnp.float32), jnp.zeros((1, width), jnp.float32)], axis=0
    )
    out[2 * bands : 2 * bands + GEO_ROWS, :] = jnp.concatenate(
        [*three_pieces(geo), jnp.zeros((8, width), jnp.float32)], axis=0
    ).astype(jnp.bfloat16)


def near_stack(x):
    high, middle, low = three_pieces(x)
    return jnp.concatenate([high, high, middle, high, low, middle], axis=0)


def far_stack(x):
    high, middle, low = three_pieces(x)
    return jnp.concatenate([high, middle, high, low, high, middle], axis=0).astype(jnp.bfloat16)


def triangle(count):
    return count * (count + 1) // 2


def own_tile(k, count):
    if k <= count // 2:
        return k * count, 1
    return (count - k) * count + k, 0


def grow_kernel(n_old, n_new, bits, seg_bits, col_bits, n_far, last, *refs):
    if last:
        diagonal, across, known, emi, ref, old_sums, old_tiles, out, tiles, sums, held, *scratch = refs
        at = 0
        for part in (known, across, diagonal):
            held[at : at + part.shape[0]] = part[...]
            at += part.shape[0]
    else:
        held, sums, tiles, *scratch = refs
    (
        geo_all, far_leave, far_arrive, far_rep, near_pos, near_rep, near_leave, near_arrive,
        even, odd, flag_rows,
    ) = scratch
    n_seg = n_old + n_new
    bands, width = held.shape[1] // 2 - GEO_ROWS // 2, held.shape[2]
    n_tri = triangle(n_new)
    n_pairs = n_tri + n_new * n_old
    halves = width // BLOCK
    geo_at = 2 * bands
    for k in range(n_seg):
        piece = held[k, geo_at : geo_at + GEO_ROWS, :].astype(jnp.float32)
        geo = (piece[0:8] + piece[8:16]) + piece[16:24]
        geo_all[k] = geo
        flag_rows[k] = geo[FLAG_ROW : FLAG_ROW + 1, 0:BLOCK]
    if n_old:
        sums[0:n_old] = old_sums[...]
    sums[n_old:n_seg] = jnp.zeros((n_new, bands, width), jnp.float32)
    tiles[n_pairs] = jnp.zeros((width, width), jnp.bfloat16)
    row = lax.broadcasted_iota(jnp.int32, (8, width), 0)
    origin = jnp.broadcast_to(geo_all[0, :, 0:1], (8, width))
    for k in range(n_seg):
        geo = geo_all[k]
        offset = jnp.where(row < 3, geo - origin, 0.0)
        normal = jnp.where(row < 3, pltpu.roll(geo, 5, 0), 0.0)
        along = jnp.sum(normal * offset, axis=0, keepdims=True)
        for c in range(3):
            far_rep[k, c] = jnp.broadcast_to(geo[c : c + 1], (8, width))
        far_leave[k] = far_stack(jnp.where(row == 3, 1.0, offset))
        far_arrive[k] = far_stack(jnp.where(row == 3, along, normal) * (-1.0 / math.pi))
        if k < n_old:
            continue
        at = k - n_old
        near_pos[at, :, 0:8] = jnp.transpose(geo)
        near_leave[at] = jnp.transpose(near_stack(jnp.where(row == 3, -along, normal))).astype(jnp.bfloat16)
        near_arrive[at] = jnp.transpose(near_stack(jnp.where(row == 3, 1.0, -offset))).astype(jnp.bfloat16)
    lane = lax.broadcasted_iota(jnp.int32, (1, BLOCK), 1)
    col_mask = (1 << col_bits) - 1

    def pair_of(t):
        t = jnp.int32(t)
        near = t % n_new
        far = (near + t // n_new) % n_new + n_old
        if n_old:
            far = jnp.where(t < n_tri, far, jnp.minimum((t - n_tri) // n_new, n_old - 1))
            near = jnp.where(t < n_tri, near, (t - n_tri) % n_new)
        return near, near + n_old, far

    def live(near_at, far_at, i, j):
        near = bit_reverse(near_at, bits) << (seg_bits - bits)
        far = bit_reverse(far_at, bits) << (seg_bits - bits)
        holder = (near & ~col_mask) | (far & col_mask)
        apart = near ^ far
        index = ((((apart & col_mask) << 1) | i) * n_far) + (((apart >> col_bits) << 1) | j)
        flags = flag_rows[bit_reverse(holder >> (seg_bits - bits), bits)]
        return jnp.where(lane == index, flags, 0.0)

    def project(t, cosines):
        local, near_at, far_at = pair_of(t)
        masked = []
        for i in range(halves):
            flags = [
                jnp.max(
                    jnp.maximum(live(near_at, far_at, i, j), live(far_at, near_at, j, i)),
                    axis=1, keepdims=True,
                )
                for j in range(halves)
            ]
            flags = jnp.concatenate([jnp.broadcast_to(f, (PIECES, BLOCK)) for f in flags], axis=1)
            masked.append(far_arrive[far_at] * flags.astype(jnp.bfloat16))
        for at in range(0, width, CHUNK):
            yield
            rows = slice(at, at + CHUNK)
            leaving = jnp.dot(
                near_leave[local, rows], far_leave[far_at], preferred_element_type=jnp.float32
            )
            arriving = jnp.dot(
                near_arrive[local, rows], masked[at // BLOCK], preferred_element_type=jnp.float32
            )
            cosines[rows] = jnp.maximum(leaving, 0.0) * jnp.maximum(arriving, 0.0)

    def form(t, cosines, fresh):
        local, near_at, far_at = pair_of(t)
        fars = [
            [far_rep[far_at, c, :, j * BLOCK : (j + 1) * BLOCK] for c in range(3)]
            for j in range(halves)
        ]
        for strip in range(width // 16):
            if strip * 16 % CHUNK == 0:
                yield
            nears = []
            for part in range(2):
                at = strip * 16 + part * 8
                if fresh:
                    cols_now = near_pos[local, at : at + 8, :]
                    now = [jnp.broadcast_to(cols_now[:, c : c + 1], (8, BLOCK)) for c in range(3)]
                    for c in range(3):
                        near_rep[local, c, at : at + 8, :] = now[c]
                else:
                    now = [near_rep[local, c, at : at + 8, :] for c in range(3)]
                nears.append(now)
            for j in range(halves):
                cols = slice(j * BLOCK, (j + 1) * BLOCK)
                parts = []
                for part in range(2):
                    at = strip * 16 + part * 8
                    dx, dy, dz = (f - n for f, n in zip(fars[j], nears[part]))
                    spacing = dx * dx + dy * dy + dz * dz + SOFTEN
                    inverse = 1.0 / spacing
                    product = cosines[at : at + 8, cols]
                    parts.append(product * inverse * inverse)
                strip_now = jnp.concatenate(parts, axis=0).astype(jnp.bfloat16)
                tiles[t, strip * 16 : strip * 16 + 16, cols] = strip_now

    def apply(t):
        local, near_at, far_at = pair_of(t)
        tile = tiles[t]
        to_near = lax.dot_general(
            held[far_at, 0:bands, :], tile, (((1,), (1,)), ((), ())), preferred_element_type=jnp.float32
        )
        to_far = lax.dot_general(
            held[near_at, 0:bands, :], tile, (((1,), (0,)), ((), ())), preferred_element_type=jnp.float32
        )
        sums[near_at] = sums[near_at] + to_near
        mirrored = (near_at != far_at).astype(jnp.float32)
        sums[far_at] = sums[far_at] + to_far * mirrored

    def two_steps(fresh, i, carry):
        for part, (now, later) in enumerate(((even, odd), (odd, even))):
            t = 2 * i + part
            apply(jnp.where(t == 0, n_pairs, t - 1))
            for _ in zip(project(t + 1, later), form(t, now, fresh), strict=True):
                pass
        return carry

    for _ in project(0, even):
        pass
    lax.fori_loop(0, n_new // 2, functools.partial(two_steps, True), 0)
    lax.fori_loop(n_new // 2, n_pairs // 2, functools.partial(two_steps, False), 0)
    apply(n_pairs - 1)
    if not last:
        return
    total = jnp.zeros((bands, width), jnp.float32)
    for k in range(n_seg):
        base = held[k, 0:bands, :].astype(jnp.float32)
        gain = held[k, bands : 2 * bands, :].astype(jnp.float32)
        weighted = (base + gain * sums[k]).astype(jnp.bfloat16)
        if k < n_old:
            t, over = own_tile(k, n_old)
            tile = old_tiles[t]
        else:
            tile, over = tiles[n_tri + k - n_old], 0
        total += lax.dot_general(
            weighted, tile, (((1,), (over,)), ((), ())), preferred_element_type=jnp.float32
        )
    out[...] = emi[...] + ref[...] * total


def grow(n_old, n_new, seg_bits, col_bits, n_far, args):
    rows, width = args[0].shape[1:]
    bands = (rows - GEO_ROWS) // 2
    n_seg = n_old + n_new
    bits = n_seg.bit_length() - 1
    last = bits == seg_bits
    n_pairs = triangle(n_new) + n_new * n_old
    vmem = pl.BlockSpec(memory_space=pltpu.VMEM)
    state = [
        pltpu.VMEM((n_pairs + 1, width, width), jnp.bfloat16),
        pltpu.VMEM((n_seg, bands, width), jnp.float32),
    ]
    outs = jax.ShapeDtypeStruct((bands, width), jnp.float32) if last else state[::-1]
    work = n_pairs * width * width
    return pl.pallas_call(
        functools.partial(grow_kernel, n_old, n_new, bits, seg_bits, col_bits, n_far, last),
        out_shape=outs,
        in_specs=[vmem] * len(args),
        out_specs=vmem if last else [vmem, vmem],
        scratch_shapes=(state + [pltpu.VMEM((n_seg, rows, width), jnp.bfloat16)] if last else [])
        + [
            pltpu.VMEM((n_seg, 8, width), jnp.float32),
            pltpu.VMEM((n_seg, PIECES, width), jnp.bfloat16),
            pltpu.VMEM((n_seg, PIECES, width), jnp.bfloat16),
            pltpu.VMEM((n_seg, 3, 8, width), jnp.float32),
            pltpu.VMEM((n_new, width, BLOCK), jnp.float32),
            pltpu.VMEM((n_new, 3, width, BLOCK), jnp.float32),
            pltpu.VMEM((n_new, width, PIECES), jnp.bfloat16),
            pltpu.VMEM((n_new, width, PIECES), jnp.bfloat16),
            *[pltpu.VMEM((width, width), jnp.float32)] * 2,
            pltpu.VMEM((n_seg, 1, BLOCK), jnp.float32),
        ],
        compiler_params=pltpu.CompilerParams(vmem_limit_bytes=32 * 1024 * 1024),
        cost_estimate=pl.CostEstimate(
            flops=work * (4 * PIECES + 4 * bands), bytes_accessed=n_seg * rows * width * 2, transcendentals=work
        ),
    )(*args)


def one_exchange(positions, normals, areas, emission, reflect, pair_row, pair_col, pair_live):
    n_row = lax.axis_size("row")
    n_col = lax.axis_size("col")
    n_seg = n_row * n_col
    seg_bits = n_seg.bit_length() - 1
    col_bits = n_col.bit_length() - 1
    bands, width = emission.shape
    n_far = width // BLOCK * n_row
    rows = 2 * bands + GEO_ROWS
    vmem = pl.BlockSpec(memory_space=pltpu.VMEM)
    smem = pl.BlockSpec(memory_space=pltpu.SMEM)
    packed = pl.pallas_call(
        functools.partial(pack_kernel, col_bits, n_far),
        out_shape=pltpu.VMEM((rows, width), jnp.bfloat16),
        in_specs=[vmem] * 5 + [smem] * 3,
        out_specs=vmem,
    )(positions, normals, areas.reshape(1, width), emission, reflect, pair_row, pair_col, pair_live)
    gathered = packed[None]

    def swap(value, distance):
        return lax.ppermute(value, ("row", "col"), [(i, i ^ distance) for i in range(n_seg)])

    for bit in reversed(range(2, seg_bits)):
        gathered = jnp.concatenate([gathered, swap(gathered, 1 << bit)])
    beside, across, diagonal = (swap(gathered, distance) for distance in (2, 1, 3))
    gathered = jnp.concatenate([gathered, beside])
    state = grow(0, n_seg // 2, seg_bits, col_bits, n_far, (gathered,))
    half = n_seg // 2
    args = (diagonal, across, gathered, emission, reflect, *state)
    return grow(half, half, seg_bits, col_bits, n_far, args)


def form_tiles(near, far):
    offset = far[0:3, :, None, :] - near[0:3, :, :, None]
    leaving = jnp.sum(near[3:6, :, :, None] * offset, axis=0)
    arriving = -jnp.sum(far[3:6, :, None, :] * offset, axis=0)
    spacing = jnp.sum(offset * offset, axis=0) + SOFTEN
    return jax.nn.relu(leaving) * jax.nn.relu(arriving) / (math.pi * spacing * spacing)


def two_exchanges(positions, normals, areas, emission, reflect, pair_row, pair_col, pair_live):
    patch_dev = areas.shape[0]
    own_blocks = patch_dev // BLOCK
    n_row = lax.axis_size("row")
    n_col = lax.axis_size("col")
    row_blocks = own_blocks * n_col
    col_blocks = own_blocks * n_row
    all_blocks = row_blocks * n_row
    band_half = emission.shape[0]
    row_here = lax.axis_index("row")
    col_here = lax.axis_index("col")
    geometry = jnp.concatenate([positions, normals], axis=0)
    geo_rows = lax.all_gather(geometry, "col", axis=1, tiled=True).reshape(6, row_blocks, BLOCK)
    geo_cols = lax.all_gather(geometry, "row", axis=1, tiled=True).reshape(6, col_blocks, BLOCK)
    slots = pair_row.shape[0]
    rows_seen, cols_seen, live_seen = (
        lax.all_gather(pair_row, ("row", "col"), axis=0, tiled=True),
        lax.all_gather(pair_col, ("row", "col"), axis=0, tiled=True),
        lax.all_gather(pair_live, ("row", "col"), axis=0, tiled=True),
    )
    seen = jnp.zeros((all_blocks * all_blocks,), jnp.int32)
    seen = seen.at[rows_seen * all_blocks + cols_seen].max(live_seen)
    seen = seen.at[cols_seen * all_blocks + rows_seen].max(live_seen)
    near_grid = row_here * row_blocks + jnp.arange(row_blocks, dtype=jnp.int32)
    far_local = jnp.arange(col_blocks, dtype=jnp.int32)
    far_grid = (far_local // own_blocks * n_col + col_here) * own_blocks + far_local % own_blocks
    flags = seen[(near_grid[:, None] * all_blocks + far_grid[None, :]).reshape(-1)]
    order = jnp.argsort(1 - flags, stable=True)
    near_index = order // col_blocks
    far_index = order % col_blocks
    live_float = flags[order].astype(jnp.float32)
    live_count = jnp.sum(flags)
    group_size = math.gcd(slots, 32)
    turns = (live_count + group_size - 1) // group_size
    stored_init = jnp.zeros((1, 1, 1), jnp.bfloat16)
    stored = stored_init
    radiosity = emission
    for sweep in range(ITERS):
        weighted = (areas[None, :] * radiosity).astype(jnp.bfloat16)
        w_cols = lax.all_gather(weighted, "row", axis=1, tiled=True).reshape(
            band_half, col_blocks, BLOCK
        )

        def one_turn(turn_index, state_now):
            acc_rows, acc_cols, kept = state_now
            first_slot = turn_index * group_size
            near_now = lax.dynamic_slice_in_dim(near_index, first_slot, group_size)
            far_now = lax.dynamic_slice_in_dim(far_index, first_slot, group_size)
            live_now = lax.dynamic_slice_in_dim(live_float, first_slot, group_size)
            tiles_now = form_tiles(geo_rows[:, near_now], geo_cols[:, far_now]).astype(jnp.bfloat16)
            far_weights = w_cols[:, far_now]
            to_rows = jnp.einsum(
                "buv,kbv->kbu", tiles_now, far_weights, preferred_element_type=jnp.float32
            )
            acc_rows = acc_rows.at[:, near_now].add(to_rows * live_now[None, :, None])
            return (acc_rows, acc_cols, kept)

        zero_rows = jnp.zeros((band_half, row_blocks, BLOCK), jnp.float32)
        zero_cols = jnp.zeros((1, 1, 1), jnp.float32)
        acc_rows, acc_cols, stored = lax.fori_loop(
            0, turns, one_turn, (zero_rows, zero_cols, stored)
        )
        row_sum = lax.psum_scatter(
            acc_rows.reshape(band_half, row_blocks * BLOCK), "col", scatter_dimension=1, tiled=True
        )
        radiosity = emission + reflect * row_sum
    return radiosity


def shards(positions, normals, areas, emission, reflect, pair_row, pair_col, pair_live):
    n_row, n_col = lax.axis_size("row"), lax.axis_size("col")
    n_seg = n_row * n_col
    powers = n_row & (n_row - 1) == 0 and n_col & (n_col - 1) == 0
    small = areas.shape[0] == 2 * BLOCK and 8 <= n_seg <= 16
    plan = one_exchange if powers and small else two_exchanges
    return plan(positions, normals, areas, emission, reflect, pair_row, pair_col, pair_live)


def solution(mesh):
    return jax.shard_map(
        shards,
        mesh=mesh,
        in_specs=(
            P(None, ("case", "row", "col")),
            P(None, ("case", "row", "col")),
            P(("case", "row", "col")),
            P("band", ("case", "row", "col")),
            P("band", ("case", "row", "col")),
            P(("case", "row", "col")),
            P(("case", "row", "col")),
            P(("case", "row", "col")),
        ),
        out_specs=P("band", ("case", "row", "col")),
        check_vma=False,
    )
```

```python
import functools
import math

import jax
import jax.numpy as jnp
from jax import lax
from jax.experimental import pallas as pl
from jax.experimental.pallas import tpu as pltpu
from jax.sharding import PartitionSpec as P

BLOCK = 128
ITERS = 2


SOFTEN = 0.02

GEO_ROWS = 32
FLAG_ROW = 6
CHUNK = 128
PIECES = 48


def bit_reverse(value, bits):
    out = value * 0
    for bit in range(bits):
        out = out | (((value >> bit) & 1) << (bits - 1 - bit))
    return out


def three_pieces(x):
    high = x.astype(jnp.bfloat16).astype(jnp.float32)
    rest = x - high
    middle = rest.astype(jnp.bfloat16).astype(jnp.float32)
    return high, middle, rest - middle


def pack_kernel(col_bits, n_far, pos, nrm, area, emi, ref, prow, pcol, plive, out):
    seg = (lax.axis_index("row") << col_bits) | lax.axis_index("col")
    bands, width = emi.shape
    a = area[...]
    out[0:bands, :] = (a * emi[...]).astype(jnp.bfloat16)
    out[bands : 2 * bands, :] = (a * ref[...]).astype(jnp.bfloat16)
    lane = lax.broadcasted_iota(jnp.int32, (1, width), 1)
    col_mask = (1 << col_bits) - 1

    def add_slot(i, flags):
        p, q = prow[i], pcol[i]
        near = ((((p >> 1) ^ seg) & col_mask) << 1) | (p & 1)
        far = ((((q >> 1) ^ seg) >> col_bits) << 1) | (q & 1)
        return flags + jnp.where(lane == near * n_far + far, plive[i], 0)

    flags = lax.fori_loop(0, prow.shape[0], add_slot, jnp.zeros((1, width), jnp.int32), unroll=True)
    geo = jnp.concatenate(
        [pos[...], nrm[...], flags.astype(jnp.float32), jnp.zeros((1, width), jnp.float32)], axis=0
    )
    out[2 * bands : 2 * bands + GEO_ROWS, :] = jnp.concatenate(
        [*three_pieces(geo), jnp.zeros((8, width), jnp.float32)], axis=0
    ).astype(jnp.bfloat16)


def near_stack(x):
    high, middle, low = three_pieces(x)
    return jnp.concatenate([high, high, middle, high, low, middle], axis=0)


def far_stack(x):
    high, middle, low = three_pieces(x)
    return jnp.concatenate([high, middle, high, low, high, middle], axis=0).astype(jnp.bfloat16)


def triangle(count):
    return count * (count + 1) // 2


def own_tile(k, count):
    if k <= count // 2:
        return k * count, 1
    return (count - k) * count + k, 0


def grow_kernel(levels, seg_bits, col_bits, n_far, last, *refs):
    n_old, n_new = levels[-1]
    bits = (n_old + n_new).bit_length() - 1
    if last:
        diagonal, across, known, emi, ref, old_sums, *refs = refs
        old_tiles, (out, tiles, sums, held, *scratch) = refs[: len(levels) - 1], refs[len(levels) - 1 :]
        at = 0
        for part in (known, across, diagonal):
            held[at : at + part.shape[0]] = part[...]
            at += part.shape[0]
    elif n_old:
        held, old_sums, sums, tiles, *scratch = refs
    else:
        held, sums, tiles, *scratch = refs
    (
        geo_all, far_leave, far_arrive, far_rep, near_pos, near_rep, near_leave, near_arrive,
        even, odd, flag_rows,
    ) = scratch
    n_seg = n_old + n_new
    bands, width = held.shape[1] // 2 - GEO_ROWS // 2, held.shape[2]
    n_tri = triangle(n_new)
    n_pairs = n_tri + n_new * n_old
    halves = width // BLOCK
    geo_at = 2 * bands
    for k in range(n_seg):
        piece = held[k, geo_at : geo_at + GEO_ROWS, :].astype(jnp.float32)
        geo = (piece[0:8] + piece[8:16]) + piece[16:24]
        geo_all[k] = geo
        flag_rows[k] = geo[FLAG_ROW : FLAG_ROW + 1, 0:BLOCK]
    if n_old:
        sums[0:n_old] = old_sums[...]
    sums[n_old:n_seg] = jnp.zeros((n_new, bands, width), jnp.float32)
    tiles[n_pairs] = jnp.zeros((width, width), jnp.bfloat16)
    row = lax.broadcasted_iota(jnp.int32, (8, width), 0)
    origin = jnp.broadcast_to(geo_all[0, :, 0:1], (8, width))
    for k in range(n_seg):
        geo = geo_all[k]
        offset = jnp.where(row < 3, geo - origin, 0.0)
        normal = jnp.where(row < 3, pltpu.roll(geo, 5, 0), 0.0)
        along = jnp.sum(normal * offset, axis=0, keepdims=True)
        for c in range(3):
            far_rep[k, c] = jnp.broadcast_to(geo[c : c + 1], (8, width))
        far_leave[k] = far_stack(jnp.where(row == 3, 1.0, offset))
        far_arrive[k] = far_stack(jnp.where(row == 3, along, normal) * (-1.0 / math.pi))
        if k < n_old:
            continue
        at = k - n_old
        near_pos[at, :, 0:8] = jnp.transpose(geo)
        near_leave[at] = jnp.transpose(near_stack(jnp.where(row == 3, -along, normal))).astype(jnp.bfloat16)
        near_arrive[at] = jnp.transpose(near_stack(jnp.where(row == 3, 1.0, -offset))).astype(jnp.bfloat16)
    lane = lax.broadcasted_iota(jnp.int32, (1, BLOCK), 1)
    col_mask = (1 << col_bits) - 1

    def pair_of(t):
        t = jnp.int32(t)
        near = t % n_new
        far = (near + t // n_new) % n_new + n_old
        if n_old:
            far = jnp.where(t < n_tri, far, jnp.minimum((t - n_tri) // n_new, n_old - 1))
            near = jnp.where(t < n_tri, near, (t - n_tri) % n_new)
        return near, near + n_old, far

    def live(near_at, far_at, i, j):
        near = bit_reverse(near_at, bits) << (seg_bits - bits)
        far = bit_reverse(far_at, bits) << (seg_bits - bits)
        holder = (near & ~col_mask) | (far & col_mask)
        apart = near ^ far
        index = ((((apart & col_mask) << 1) | i) * n_far) + (((apart >> col_bits) << 1) | j)
        flags = flag_rows[bit_reverse(holder >> (seg_bits - bits), bits)]
        return jnp.where(lane == index, flags, 0.0)

    def project(t, cosines):
        local, near_at, far_at = pair_of(t)
        masked = []
        for i in range(halves):
            flags = [
                jnp.max(
                    jnp.maximum(live(near_at, far_at, i, j), live(far_at, near_at, j, i)),
                    axis=1, keepdims=True,
                )
                for j in range(halves)
            ]
            flags = jnp.concatenate([jnp.broadcast_to(f, (PIECES, BLOCK)) for f in flags], axis=1)
            masked.append(far_arrive[far_at] * flags.astype(jnp.bfloat16))
        for at in range(0, width, CHUNK):
            yield
            rows = slice(at, at + CHUNK)
            leaving = jnp.dot(
                near_leave[local, rows], far_leave[far_at], preferred_element_type=jnp.float32
            )
            arriving = jnp.dot(
                near_arrive[local, rows], masked[at // BLOCK], preferred_element_type=jnp.float32
            )
            cosines[rows] = jnp.maximum(leaving, 0.0) * jnp.maximum(arriving, 0.0)

    def form(t, cosines, fresh):
        local, near_at, far_at = pair_of(t)
        fars = [
            [far_rep[far_at, c, :, j * BLOCK : (j + 1) * BLOCK] for c in range(3)]
            for j in range(halves)
        ]
        for strip in range(width // 16):
            if strip * 16 % CHUNK == 0:
                yield
            nears = []
            for part in range(2):
                at = strip * 16 + part * 8
                if fresh:
                    cols_now = near_pos[local, at : at + 8, :]
                    now = [jnp.broadcast_to(cols_now[:, c : c + 1], (8, BLOCK)) for c in range(3)]
                    for c in range(3):
                        near_rep[local, c, at : at + 8, :] = now[c]
                else:
                    now = [near_rep[local, c, at : at + 8, :] for c in range(3)]
                nears.append(now)
            for j in range(halves):
                cols = slice(j * BLOCK, (j + 1) * BLOCK)
                parts = []
                for part in range(2):
                    at = strip * 16 + part * 8
                    dx, dy, dz = (f - n for f, n in zip(fars[j], nears[part]))
                    spacing = dx * dx + dy * dy + dz * dz + SOFTEN
                    inverse = 1.0 / spacing
                    product = cosines[at : at + 8, cols]
                    parts.append(product * inverse * inverse)
                strip_now = jnp.concatenate(parts, axis=0).astype(jnp.bfloat16)
                tiles[t, strip * 16 : strip * 16 + 16, cols] = strip_now

    def apply(t):
        local, near_at, far_at = pair_of(t)
        tile = tiles[t]
        to_near = lax.dot_general(
            held[far_at, 0:bands, :], tile, (((1,), (1,)), ((), ())), preferred_element_type=jnp.float32
        )
        to_far = lax.dot_general(
            held[near_at, 0:bands, :], tile, (((1,), (0,)), ((), ())), preferred_element_type=jnp.float32
        )
        sums[near_at] = sums[near_at] + to_near
        mirrored = (near_at != far_at).astype(jnp.float32)
        sums[far_at] = sums[far_at] + to_far * mirrored

    def two_steps(fresh, i, carry):
        for part, (now, later) in enumerate(((even, odd), (odd, even))):
            t = 2 * i + part
            apply(jnp.where(t == 0, n_pairs, t - 1))
            for _ in zip(project(t + 1, later), form(t, now, fresh), strict=True):
                pass
        return carry

    for _ in project(0, even):
        pass
    lax.fori_loop(0, n_new // 2, functools.partial(two_steps, True), 0)
    lax.fori_loop(n_new // 2, (n_pairs + 1) // 2, functools.partial(two_steps, False), 0)
    if n_pairs % 2 == 0:
        apply(n_pairs - 1)
    if not last:
        return
    total = jnp.zeros((bands, width), jnp.float32)
    for k in range(n_seg):
        base = held[k, 0:bands, :].astype(jnp.float32)
        gain = held[k, bands : 2 * bands, :].astype(jnp.float32)
        weighted = (base + gain * sums[k]).astype(jnp.bfloat16)
        level = next(i for i, (old, new) in enumerate(levels) if k < old + new)
        old, new = levels[level]
        t, over = (triangle(new) + k - old, 0) if old else own_tile(k, new)
        tile = tiles[t] if k >= n_old else old_tiles[level][t]
        total += lax.dot_general(
            weighted, tile, (((1,), (over,)), ((), ())), preferred_element_type=jnp.float32
        )
    out[...] = emi[...] + ref[...] * total


def grow(levels, seg_bits, col_bits, n_far, args):
    n_old, n_new = levels[-1]
    rows, width = args[0].shape[1:]
    bands = (rows - GEO_ROWS) // 2
    n_seg = n_old + n_new
    last = n_seg == 1 << seg_bits
    n_pairs = triangle(n_new) + n_new * n_old
    vmem = pl.BlockSpec(memory_space=pltpu.VMEM)
    state = [
        pltpu.VMEM((n_pairs + 1, width, width), jnp.bfloat16),
        pltpu.VMEM((n_seg, bands, width), jnp.float32),
    ]
    outs = jax.ShapeDtypeStruct((bands, width), jnp.float32) if last else state[::-1]
    work = n_pairs * width * width
    return pl.pallas_call(
        functools.partial(grow_kernel, levels, seg_bits, col_bits, n_far, last),
        out_shape=outs,
        in_specs=[vmem] * len(args),
        out_specs=vmem if last else [vmem, vmem],
        scratch_shapes=(state + [pltpu.VMEM((n_seg, rows, width), jnp.bfloat16)] if last else [])
        + [
            pltpu.VMEM((n_seg, 8, width), jnp.float32),
            pltpu.VMEM((n_seg, PIECES, width), jnp.bfloat16),
            pltpu.VMEM((n_seg, PIECES, width), jnp.bfloat16),
            pltpu.VMEM((n_seg, 3, 8, width), jnp.float32),
            pltpu.VMEM((n_new, width, BLOCK), jnp.float32),
            pltpu.VMEM((n_new, 3, width, BLOCK), jnp.float32),
            pltpu.VMEM((n_new, width, PIECES), jnp.bfloat16),
            pltpu.VMEM((n_new, width, PIECES), jnp.bfloat16),
            *[pltpu.VMEM((width, width), jnp.float32)] * 2,
            pltpu.VMEM((n_seg, 1, BLOCK), jnp.float32),
        ],
        compiler_params=pltpu.CompilerParams(vmem_limit_bytes=32 * 1024 * 1024),
        cost_estimate=pl.CostEstimate(
            flops=work * (4 * PIECES + 4 * bands), bytes_accessed=n_seg * rows * width * 2, transcendentals=work
        ),
    )(*args)


def one_exchange(positions, normals, areas, emission, reflect, pair_row, pair_col, pair_live):
    n_row = lax.axis_size("row")
    n_col = lax.axis_size("col")
    n_seg = n_row * n_col
    seg_bits = n_seg.bit_length() - 1
    col_bits = n_col.bit_length() - 1
    bands, width = emission.shape
    n_far = width // BLOCK * n_row
    rows = 2 * bands + GEO_ROWS
    vmem = pl.BlockSpec(memory_space=pltpu.VMEM)
    smem = pl.BlockSpec(memory_space=pltpu.SMEM)
    packed = pl.pallas_call(
        functools.partial(pack_kernel, col_bits, n_far),
        out_shape=pltpu.VMEM((rows, width), jnp.bfloat16),
        in_specs=[vmem] * 5 + [smem] * 3,
        out_specs=vmem,
    )(positions, normals, areas.reshape(1, width), emission, reflect, pair_row, pair_col, pair_live)
    gathered = packed[None]

    def swap(value, distance):
        return lax.ppermute(value, ("row", "col"), [(i, i ^ distance) for i in range(n_seg)])

    for bit in reversed(range(2, seg_bits)):
        gathered = jnp.concatenate([gathered, swap(gathered, 1 << bit)])
    beside, across, diagonal = (swap(gathered, distance) for distance in (2, 1, 3))
    quarter, half = n_seg // 4, n_seg // 2
    levels = ((0, quarter), (quarter, quarter), (half, half))
    sums, tiles = grow(levels[:1], seg_bits, col_bits, n_far, (gathered,))
    gathered = jnp.concatenate([gathered, beside])
    sums, more_tiles = grow(levels[:2], seg_bits, col_bits, n_far, (gathered, sums))
    args = (diagonal, across, gathered, emission, reflect, sums, tiles, more_tiles)
    return grow(levels, seg_bits, col_bits, n_far, args)


def form_tiles(near, far):
    offset = far[0:3, :, None, :] - near[0:3, :, :, None]
    leaving = jnp.sum(near[3:6, :, :, None] * offset, axis=0)
    arriving = -jnp.sum(far[3:6, :, None, :] * offset, axis=0)
    spacing = jnp.sum(offset * offset, axis=0) + SOFTEN
    return jax.nn.relu(leaving) * jax.nn.relu(arriving) / (math.pi * spacing * spacing)


def two_exchanges(positions, normals, areas, emission, reflect, pair_row, pair_col, pair_live):
    patch_dev = areas.shape[0]
    own_blocks = patch_dev // BLOCK
    n_row = lax.axis_size("row")
    n_col = lax.axis_size("col")
    row_blocks = own_blocks * n_col
    col_blocks = own_blocks * n_row
    all_blocks = row_blocks * n_row
    band_half = emission.shape[0]
    row_here = lax.axis_index("row")
    col_here = lax.axis_index("col")
    geometry = jnp.concatenate([positions, normals], axis=0)
    geo_rows = lax.all_gather(geometry, "col", axis=1, tiled=True).reshape(6, row_blocks, BLOCK)
    geo_cols = lax.all_gather(geometry, "row", axis=1, tiled=True).reshape(6, col_blocks, BLOCK)
    slots = pair_row.shape[0]
    rows_seen, cols_seen, live_seen = (
        lax.all_gather(pair_row, ("row", "col"), axis=0, tiled=True),
        lax.all_gather(pair_col, ("row", "col"), axis=0, tiled=True),
        lax.all_gather(pair_live, ("row", "col"), axis=0, tiled=True),
    )
    seen = jnp.zeros((all_blocks * all_blocks,), jnp.int32)
    seen = seen.at[rows_seen * all_blocks + cols_seen].max(live_seen)
    seen = seen.at[cols_seen * all_blocks + rows_seen].max(live_seen)
    near_grid = row_here * row_blocks + jnp.arange(row_blocks, dtype=jnp.int32)
    far_local = jnp.arange(col_blocks, dtype=jnp.int32)
    far_grid = (far_local // own_blocks * n_col + col_here) * own_blocks + far_local % own_blocks
    flags = seen[(near_grid[:, None] * all_blocks + far_grid[None, :]).reshape(-1)]
    order = jnp.argsort(1 - flags, stable=True)
    near_index = order // col_blocks
    far_index = order % col_blocks
    live_float = flags[order].astype(jnp.float32)
    live_count = jnp.sum(flags)
    group_size = math.gcd(slots, 32)
    turns = (live_count + group_size - 1) // group_size
    stored_init = jnp.zeros((1, 1, 1), jnp.bfloat16)
    stored = stored_init
    radiosity = emission
    for sweep in range(ITERS):
        weighted = (areas[None, :] * radiosity).astype(jnp.bfloat16)
        w_cols = lax.all_gather(weighted, "row", axis=1, tiled=True).reshape(
            band_half, col_blocks, BLOCK
        )

        def one_turn(turn_index, state_now):
            acc_rows, acc_cols, kept = state_now
            first_slot = turn_index * group_size
            near_now = lax.dynamic_slice_in_dim(near_index, first_slot, group_size)
            far_now = lax.dynamic_slice_in_dim(far_index, first_slot, group_size)
            live_now = lax.dynamic_slice_in_dim(live_float, first_slot, group_size)
            tiles_now = form_tiles(geo_rows[:, near_now], geo_cols[:, far_now]).astype(jnp.bfloat16)
            far_weights = w_cols[:, far_now]
            to_rows = jnp.einsum(
                "buv,kbv->kbu", tiles_now, far_weights, preferred_element_type=jnp.float32
            )
            acc_rows = acc_rows.at[:, near_now].add(to_rows * live_now[None, :, None])
            return (acc_rows, acc_cols, kept)

        zero_rows = jnp.zeros((band_half, row_blocks, BLOCK), jnp.float32)
        zero_cols = jnp.zeros((1, 1, 1), jnp.float32)
        acc_rows, acc_cols, stored = lax.fori_loop(
            0, turns, one_turn, (zero_rows, zero_cols, stored)
        )
        row_sum = lax.psum_scatter(
            acc_rows.reshape(band_half, row_blocks * BLOCK), "col", scatter_dimension=1, tiled=True
        )
        radiosity = emission + reflect * row_sum
    return radiosity


def shards(positions, normals, areas, emission, reflect, pair_row, pair_col, pair_live):
    n_row, n_col = lax.axis_size("row"), lax.axis_size("col")
    n_seg = n_row * n_col
    powers = n_row & (n_row - 1) == 0 and n_col & (n_col - 1) == 0
    small = areas.shape[0] == 2 * BLOCK and 8 <= n_seg <= 16
    plan = one_exchange if powers and small else two_exchanges
    return plan(positions, normals, areas, emission, reflect, pair_row, pair_col, pair_live)


def solution(mesh):
    return jax.shard_map(
        shards,
        mesh=mesh,
        in_specs=(
            P(None, ("case", "row", "col")),
            P(None, ("case", "row", "col")),
            P(("case", "row", "col")),
            P("band", ("case", "row", "col")),
            P("band", ("case", "row", "col")),
            P(("case", "row", "col")),
            P(("case", "row", "col")),
            P(("case", "row", "col")),
        ),
        out_specs=P("band", ("case", "row", "col")),
        check_vma=False,
    )
```

```python
import functools
import itertools
import math

import jax
import jax.numpy as jnp
from jax import lax
from jax.experimental import pallas as pl
from jax.experimental.pallas import tpu as pltpu
from jax.sharding import PartitionSpec as P

BLOCK = 128
ITERS = 2


SOFTEN = 0.02

GEO_ROWS = 32
FLAG_ROW = 6
CHUNK = 128
PIECES = 48


def bit_reverse(value, bits):
    out = value * 0
    for bit in range(bits):
        out = out | (((value >> bit) & 1) << (bits - 1 - bit))
    return out


def three_pieces(x):
    high = x.astype(jnp.bfloat16).astype(jnp.float32)
    rest = x - high
    middle = rest.astype(jnp.bfloat16).astype(jnp.float32)
    return high, middle, rest - middle


def pack_kernel(col_bits, n_far, pos, nrm, area, emi, ref, prow, pcol, plive, out):
    seg = (lax.axis_index("row") << col_bits) | lax.axis_index("col")
    bands, width = emi.shape
    a = area[...]
    out[0:bands, :] = (a * emi[...]).astype(jnp.bfloat16)
    out[bands : 2 * bands, :] = (a * ref[...]).astype(jnp.bfloat16)
    lane = lax.broadcasted_iota(jnp.int32, (1, width), 1)
    col_mask = (1 << col_bits) - 1

    def add_slot(i, flags):
        p, q = prow[i], pcol[i]
        near = ((((p >> 1) ^ seg) & col_mask) << 1) | (p & 1)
        far = ((((q >> 1) ^ seg) >> col_bits) << 1) | (q & 1)
        return flags + jnp.where(lane == near * n_far + far, plive[i], 0)

    flags = lax.fori_loop(0, prow.shape[0], add_slot, jnp.zeros((1, width), jnp.int32), unroll=True)
    geo = jnp.concatenate(
        [pos[...], nrm[...], flags.astype(jnp.float32), jnp.zeros((1, width), jnp.float32)], axis=0
    )
    out[2 * bands : 2 * bands + GEO_ROWS, :] = jnp.concatenate(
        [*three_pieces(geo), jnp.zeros((8, width), jnp.float32)], axis=0
    ).astype(jnp.bfloat16)


def near_stack(x):
    high, middle, low = three_pieces(x)
    return jnp.concatenate([high, high, middle, high, low, middle], axis=0)


def far_stack(x):
    high, middle, low = three_pieces(x)
    return jnp.concatenate([high, middle, high, low, high, middle], axis=0).astype(jnp.bfloat16)


def triangle(count):
    return count * (count + 1) // 2


def own_tile(k, count):
    if k <= count // 2:
        return k * count, 1
    return (count - k) * count + k, 0


def grow_kernel(levels, seg_bits, col_bits, n_far, last, *refs):
    n_old, n_new = levels[-1]
    bits = (n_old + n_new).bit_length() - 1
    if last:
        diagonal, across, known, emi, ref, old_sums, *refs = refs
        old_tiles, (out, tiles, sums, held, *scratch) = refs[: len(levels) - 1], refs[len(levels) - 1 :]
        at = 0
        for part in (known, across, diagonal):
            held[at : at + part.shape[0]] = part[...]
            at += part.shape[0]
    elif n_old:
        held, old_sums, sums, tiles, *scratch = refs
    else:
        held, sums, tiles, *scratch = refs
    (
        geo_all, far_leave, far_arrive, far_rep, near_pos, near_rep, near_leave, near_arrive,
        even, odd, flag_rows,
    ) = scratch
    n_seg = n_old + n_new
    bands, width = held.shape[1] // 2 - GEO_ROWS // 2, held.shape[2]
    n_tri = triangle(n_new)
    n_pairs = n_tri + n_new * n_old
    halves = width // BLOCK
    geo_at = 2 * bands
    for k in range(n_seg):
        piece = held[k, geo_at : geo_at + GEO_ROWS, :].astype(jnp.float32)
        geo = (piece[0:8] + piece[8:16]) + piece[16:24]
        geo_all[k] = geo
        flag_rows[k] = geo[FLAG_ROW : FLAG_ROW + 1, 0:BLOCK]
    if n_old:
        sums[0:n_old] = old_sums[...]
    sums[n_old:n_seg] = jnp.zeros((n_new, bands, width), jnp.float32)
    row = lax.broadcasted_iota(jnp.int32, (8, width), 0)
    origin = jnp.broadcast_to(geo_all[0, :, 0:1], (8, width))
    for k in range(n_seg):
        geo = geo_all[k]
        offset = jnp.where(row < 3, geo - origin, 0.0)
        normal = jnp.where(row < 3, pltpu.roll(geo, 5, 0), 0.0)
        along = jnp.sum(normal * offset, axis=0, keepdims=True)
        for c in range(3):
            far_rep[k, c] = jnp.broadcast_to(geo[c : c + 1], (8, width))
        far_leave[k] = far_stack(jnp.where(row == 3, 1.0, offset))
        far_arrive[k] = far_stack(jnp.where(row == 3, along, normal) * (-1.0 / math.pi))
        if k < n_old:
            continue
        at = k - n_old
        near_pos[at, :, 0:8] = jnp.transpose(geo)
        near_leave[at] = jnp.transpose(near_stack(jnp.where(row == 3, -along, normal))).astype(jnp.bfloat16)
        near_arrive[at] = jnp.transpose(near_stack(jnp.where(row == 3, 1.0, -offset))).astype(jnp.bfloat16)
    col_mask = (1 << col_bits) - 1

    def pair_of(t):
        if t >= n_tri:
            near, far = (t - n_tri) % n_new, (t - n_tri) // n_new
        else:
            near = t % n_new
            far = (near + t // n_new) % n_new + n_old
        return near, near + n_old, far

    def live(near_at, far_at, i, j):
        near = bit_reverse(near_at, bits) << (seg_bits - bits)
        far = bit_reverse(far_at, bits) << (seg_bits - bits)
        holder = (near & ~col_mask) | (far & col_mask)
        apart = near ^ far
        index = ((((apart & col_mask) << 1) | i) * n_far) + (((apart >> col_bits) << 1) | j)
        held_at = bit_reverse(holder >> (seg_bits - bits), bits)
        return flag_rows[held_at, :, index : index + 1]

    def project(t, cosines):
        local, near_at, far_at = pair_of(t)
        masked = []
        for i in range(halves):
            flags = [
                jnp.maximum(live(near_at, far_at, i, j), live(far_at, near_at, j, i))
                for j in range(halves)
            ]
            flags = jnp.concatenate([jnp.broadcast_to(f, (PIECES, BLOCK)) for f in flags], axis=1)
            masked.append(far_arrive[far_at] * flags.astype(jnp.bfloat16))
        for at in range(0, width, CHUNK):
            yield
            rows = slice(at, at + CHUNK)
            leaving = jnp.dot(
                near_leave[local, rows], far_leave[far_at], preferred_element_type=jnp.float32
            )
            arriving = jnp.dot(
                near_arrive[local, rows], masked[at // BLOCK], preferred_element_type=jnp.float32
            )
            cosines[rows] = jnp.maximum(leaving, 0.0) * jnp.maximum(arriving, 0.0)

    def form(t, cosines, fresh):
        local, near_at, far_at = pair_of(t)
        fars = [
            [far_rep[far_at, c, :, j * BLOCK : (j + 1) * BLOCK] for c in range(3)]
            for j in range(halves)
        ]
        for strip in range(width // 16):
            if strip * 16 % CHUNK == 0:
                yield
            nears = []
            for part in range(2):
                at = strip * 16 + part * 8
                if fresh:
                    cols_now = near_pos[local, at : at + 8, :]
                    now = [jnp.broadcast_to(cols_now[:, c : c + 1], (8, BLOCK)) for c in range(3)]
                    for c in range(3):
                        near_rep[local, c, at : at + 8, :] = now[c]
                else:
                    now = [near_rep[local, c, at : at + 8, :] for c in range(3)]
                nears.append(now)
            for j in range(halves):
                cols = slice(j * BLOCK, (j + 1) * BLOCK)
                parts = []
                for part in range(2):
                    at = strip * 16 + part * 8
                    dx, dy, dz = (f - n for f, n in zip(fars[j], nears[part]))
                    spacing = dx * dx + dy * dy + dz * dz + SOFTEN
                    inverse = 1.0 / spacing
                    product = cosines[at : at + 8, cols]
                    parts.append(product * inverse * inverse)
                strip_now = jnp.concatenate(parts, axis=0).astype(jnp.bfloat16)
                tiles[t, strip * 16 : strip * 16 + 16, cols] = strip_now

    def apply(t):
        local, near_at, far_at = pair_of(t)
        tile = tiles[t]
        to_near = lax.dot_general(
            held[far_at, 0:bands, :], tile, (((1,), (1,)), ((), ())), preferred_element_type=jnp.float32
        )
        sums[near_at] = sums[near_at] + to_near
        if near_at != far_at:
            to_far = lax.dot_general(
                held[near_at, 0:bands, :], tile, (((1,), (0,)), ((), ())), preferred_element_type=jnp.float32
            )
            sums[far_at] = sums[far_at] + to_far

    cosines = (even, odd)
    for _ in project(0, even):
        pass
    for t in range(n_pairs):
        later = project(t + 1, cosines[(t + 1) % 2]) if t + 1 < n_pairs else ()
        for _ in itertools.zip_longest(later, form(t, cosines[t % 2], t < n_new)):
            pass
        if t:
            apply(t - 1)
    apply(n_pairs - 1)
    if not last:
        return
    total = jnp.zeros((bands, width), jnp.float32)
    for k in range(n_seg):
        base = held[k, 0:bands, :].astype(jnp.float32)
        gain = held[k, bands : 2 * bands, :].astype(jnp.float32)
        weighted = (base + gain * sums[k]).astype(jnp.bfloat16)
        level = next(i for i, (old, new) in enumerate(levels) if k < old + new)
        old, new = levels[level]
        t, over = (triangle(new) + k - old, 0) if old else own_tile(k, new)
        tile = tiles[t] if k >= n_old else old_tiles[level][t]
        total += lax.dot_general(
            weighted, tile, (((1,), (over,)), ((), ())), preferred_element_type=jnp.float32
        )
    out[...] = emi[...] + ref[...] * total


def grow(levels, seg_bits, col_bits, n_far, args):
    n_old, n_new = levels[-1]
    rows, width = args[0].shape[1:]
    bands = (rows - GEO_ROWS) // 2
    n_seg = n_old + n_new
    last = n_seg == 1 << seg_bits
    n_pairs = triangle(n_new) + n_new * n_old
    vmem = pl.BlockSpec(memory_space=pltpu.VMEM)
    state = [
        pltpu.VMEM((n_pairs, width, width), jnp.bfloat16),
        pltpu.VMEM((n_seg, bands, width), jnp.float32),
    ]
    outs = jax.ShapeDtypeStruct((bands, width), jnp.float32) if last else state[::-1]
    work = n_pairs * width * width
    return pl.pallas_call(
        functools.partial(grow_kernel, levels, seg_bits, col_bits, n_far, last),
        out_shape=outs,
        in_specs=[vmem] * len(args),
        out_specs=vmem if last else [vmem, vmem],
        scratch_shapes=(state + [pltpu.VMEM((n_seg, rows, width), jnp.bfloat16)] if last else [])
        + [
            pltpu.VMEM((n_seg, 8, width), jnp.float32),
            pltpu.VMEM((n_seg, PIECES, width), jnp.bfloat16),
            pltpu.VMEM((n_seg, PIECES, width), jnp.bfloat16),
            pltpu.VMEM((n_seg, 3, 8, width), jnp.float32),
            pltpu.VMEM((n_new, width, BLOCK), jnp.float32),
            pltpu.VMEM((n_new, 3, width, BLOCK), jnp.float32),
            pltpu.VMEM((n_new, width, PIECES), jnp.bfloat16),
            pltpu.VMEM((n_new, width, PIECES), jnp.bfloat16),
            *[pltpu.VMEM((width, width), jnp.float32)] * 2,
            pltpu.VMEM((n_seg, 1, BLOCK), jnp.float32),
        ],
        compiler_params=pltpu.CompilerParams(vmem_limit_bytes=32 * 1024 * 1024),
        cost_estimate=pl.CostEstimate(
            flops=work * (4 * PIECES + 4 * bands), bytes_accessed=n_seg * rows * width * 2, transcendentals=work
        ),
    )(*args)


def one_exchange(positions, normals, areas, emission, reflect, pair_row, pair_col, pair_live):
    n_row = lax.axis_size("row")
    n_col = lax.axis_size("col")
    n_seg = n_row * n_col
    seg_bits = n_seg.bit_length() - 1
    col_bits = n_col.bit_length() - 1
    bands, width = emission.shape
    n_far = width // BLOCK * n_row
    rows = 2 * bands + GEO_ROWS
    vmem = pl.BlockSpec(memory_space=pltpu.VMEM)
    smem = pl.BlockSpec(memory_space=pltpu.SMEM)
    packed = pl.pallas_call(
        functools.partial(pack_kernel, col_bits, n_far),
        out_shape=pltpu.VMEM((rows, width), jnp.bfloat16),
        in_specs=[vmem] * 5 + [smem] * 3,
        out_specs=vmem,
    )(positions, normals, areas.reshape(1, width), emission, reflect, pair_row, pair_col, pair_live)
    gathered = packed[None]

    def swap(value, distance):
        return lax.ppermute(value, ("row", "col"), [(i, i ^ distance) for i in range(n_seg)])

    for bit in reversed(range(2, seg_bits)):
        gathered = jnp.concatenate([gathered, swap(gathered, 1 << bit)])
    beside, across, diagonal = (swap(gathered, distance) for distance in (2, 1, 3))
    quarter, half = n_seg // 4, n_seg // 2
    levels = ((0, quarter), (quarter, quarter), (half, half))
    sums, tiles = grow(levels[:1], seg_bits, col_bits, n_far, (gathered,))
    gathered = jnp.concatenate([gathered, beside])
    sums, more_tiles = grow(levels[:2], seg_bits, col_bits, n_far, (gathered, sums))
    args = (diagonal, across, gathered, emission, reflect, sums, tiles, more_tiles)
    return grow(levels, seg_bits, col_bits, n_far, args)


def form_tiles(near, far):
    offset = far[0:3, :, None, :] - near[0:3, :, :, None]
    leaving = jnp.sum(near[3:6, :, :, None] * offset, axis=0)
    arriving = -jnp.sum(far[3:6, :, None, :] * offset, axis=0)
    spacing = jnp.sum(offset * offset, axis=0) + SOFTEN
    return jax.nn.relu(leaving) * jax.nn.relu(arriving) / (math.pi * spacing * spacing)


def two_exchanges(positions, normals, areas, emission, reflect, pair_row, pair_col, pair_live):
    patch_dev = areas.shape[0]
    own_blocks = patch_dev // BLOCK
    n_row = lax.axis_size("row")
    n_col = lax.axis_size("col")
    row_blocks = own_blocks * n_col
    col_blocks = own_blocks * n_row
    all_blocks = row_blocks * n_row
    band_half = emission.shape[0]
    row_here = lax.axis_index("row")
    col_here = lax.axis_index("col")
    geometry = jnp.concatenate([positions, normals], axis=0)
    geo_rows = lax.all_gather(geometry, "col", axis=1, tiled=True).reshape(6, row_blocks, BLOCK)
    geo_cols = lax.all_gather(geometry, "row", axis=1, tiled=True).reshape(6, col_blocks, BLOCK)
    slots = pair_row.shape[0]
    rows_seen, cols_seen, live_seen = (
        lax.all_gather(pair_row, ("row", "col"), axis=0, tiled=True),
        lax.all_gather(pair_col, ("row", "col"), axis=0, tiled=True),
        lax.all_gather(pair_live, ("row", "col"), axis=0, tiled=True),
    )
    seen = jnp.zeros((all_blocks * all_blocks,), jnp.int32)
    seen = seen.at[rows_seen * all_blocks + cols_seen].max(live_seen)
    seen = seen.at[cols_seen * all_blocks + rows_seen].max(live_seen)
    near_grid = row_here * row_blocks + jnp.arange(row_blocks, dtype=jnp.int32)
    far_local = jnp.arange(col_blocks, dtype=jnp.int32)
    far_grid = (far_local // own_blocks * n_col + col_here) * own_blocks + far_local % own_blocks
    flags = seen[(near_grid[:, None] * all_blocks + far_grid[None, :]).reshape(-1)]
    order = jnp.argsort(1 - flags, stable=True)
    near_index = order // col_blocks
    far_index = order % col_blocks
    live_float = flags[order].astype(jnp.float32)
    live_count = jnp.sum(flags)
    group_size = math.gcd(slots, 32)
    turns = (live_count + group_size - 1) // group_size
    stored_init = jnp.zeros((1, 1, 1), jnp.bfloat16)
    stored = stored_init
    radiosity = emission
    for sweep in range(ITERS):
        weighted = (areas[None, :] * radiosity).astype(jnp.bfloat16)
        w_cols = lax.all_gather(weighted, "row", axis=1, tiled=True).reshape(
            band_half, col_blocks, BLOCK
        )

        def one_turn(turn_index, state_now):
            acc_rows, acc_cols, kept = state_now
            first_slot = turn_index * group_size
            near_now = lax.dynamic_slice_in_dim(near_index, first_slot, group_size)
            far_now = lax.dynamic_slice_in_dim(far_index, first_slot, group_size)
            live_now = lax.dynamic_slice_in_dim(live_float, first_slot, group_size)
            tiles_now = form_tiles(geo_rows[:, near_now], geo_cols[:, far_now]).astype(jnp.bfloat16)
            far_weights = w_cols[:, far_now]
            to_rows = jnp.einsum(
                "buv,kbv->kbu", tiles_now, far_weights, preferred_element_type=jnp.float32
            )
            acc_rows = acc_rows.at[:, near_now].add(to_rows * live_now[None, :, None])
            return (acc_rows, acc_cols, kept)

        zero_rows = jnp.zeros((band_half, row_blocks, BLOCK), jnp.float32)
        zero_cols = jnp.zeros((1, 1, 1), jnp.float32)
        acc_rows, acc_cols, stored = lax.fori_loop(
            0, turns, one_turn, (zero_rows, zero_cols, stored)
        )
        row_sum = lax.psum_scatter(
            acc_rows.reshape(band_half, row_blocks * BLOCK), "col", scatter_dimension=1, tiled=True
        )
        radiosity = emission + reflect * row_sum
    return radiosity


def shards(positions, normals, areas, emission, reflect, pair_row, pair_col, pair_live):
    n_row, n_col = lax.axis_size("row"), lax.axis_size("col")
    n_seg = n_row * n_col
    powers = n_row & (n_row - 1) == 0 and n_col & (n_col - 1) == 0
    small = areas.shape[0] == 2 * BLOCK and 8 <= n_seg <= 16
    plan = one_exchange if powers and small else two_exchanges
    return plan(positions, normals, areas, emission, reflect, pair_row, pair_col, pair_live)


def solution(mesh):
    return jax.shard_map(
        shards,
        mesh=mesh,
        in_specs=(
            P(None, ("case", "row", "col")),
            P(None, ("case", "row", "col")),
            P(("case", "row", "col")),
            P("band", ("case", "row", "col")),
            P("band", ("case", "row", "col")),
            P(("case", "row", "col")),
            P(("case", "row", "col")),
            P(("case", "row", "col")),
        ),
        out_specs=P("band", ("case", "row", "col")),
        check_vma=False,
    )
```

```python
import functools
import itertools
import math

import jax
import jax.numpy as jnp
from jax import lax
from jax.experimental import pallas as pl
from jax.experimental.pallas import tpu as pltpu
from jax.sharding import PartitionSpec as P

BLOCK = 128
ITERS = 2


SOFTEN = 0.02

GEO_ROWS = 16
FLAG_ROW = 6
CHUNK = 128
PIECES = 48


def bit_reverse(value, bits):
    out = value * 0
    for bit in range(bits):
        out = out | (((value >> bit) & 1) << (bits - 1 - bit))
    return out


def three_pieces(x):
    high = x.astype(jnp.bfloat16).astype(jnp.float32)
    rest = x - high
    middle = rest.astype(jnp.bfloat16).astype(jnp.float32)
    return high, middle, rest - middle


def pack_kernel(col_bits, n_far, pos, nrm, area, emi, ref, prow, pcol, plive, out):
    seg = (lax.axis_index("row") << col_bits) | lax.axis_index("col")
    bands, width = emi.shape
    a = area[...]
    out[0:bands, :] = (a * emi[...]).astype(jnp.bfloat16)
    out[bands : 2 * bands, :] = (a * ref[...]).astype(jnp.bfloat16)
    lane = lax.broadcasted_iota(jnp.int32, (1, width), 1)
    col_mask = (1 << col_bits) - 1

    def add_slot(i, flags):
        p, q = prow[i], pcol[i]
        near = ((((p >> 1) ^ seg) & col_mask) << 1) | (p & 1)
        far = ((((q >> 1) ^ seg) >> col_bits) << 1) | (q & 1)
        return flags + jnp.where(lane == near * n_far + far, plive[i], 0)

    flags = lax.fori_loop(0, prow.shape[0], add_slot, jnp.zeros((1, width), jnp.int32), unroll=True)
    high, middle, low = three_pieces(pos[...])
    nrm_high, nrm_rest, _ = three_pieces(nrm[...])
    out[2 * bands : 2 * bands + GEO_ROWS, :] = jnp.concatenate(
        [high, nrm_high, flags.astype(jnp.float32), low[0:1], middle, nrm_rest, low[1:3]], axis=0
    ).astype(jnp.bfloat16)


def near_stack(x):
    high, middle, low = three_pieces(x)
    return jnp.concatenate([high, high, middle, high, low, middle], axis=0)


def far_stack(x):
    high, middle, low = three_pieces(x)
    return jnp.concatenate([high, middle, high, low, high, middle], axis=0).astype(jnp.bfloat16)


def triangle(count):
    return count * (count + 1) // 2


def own_tile(k, count):
    if k <= count // 2:
        return k * count, 1
    return (count - k) * count + k, 0


def grow_kernel(levels, seg_bits, col_bits, n_far, last, *refs):
    n_old, n_new = levels[-1]
    bits = (n_old + n_new).bit_length() - 1
    if last:
        across, diagonal, known, emi, ref, old_sums, *refs = refs
        old_tiles, (out, tiles, sums, held, *scratch) = refs[: len(levels) - 1], refs[len(levels) - 1 :]
        at = 0
        for part in (known, across, diagonal):
            held[at : at + part.shape[0]] = part[...]
            at += part.shape[0]
    elif n_old:
        held, old_sums, sums, tiles, *scratch = refs
    else:
        held, sums, tiles, *scratch = refs
    (
        geo_all, far_leave, far_arrive, far_rep, near_pos, near_rep, near_leave, near_arrive,
        even, odd, flag_rows,
    ) = scratch
    n_seg = n_old + n_new
    bands, width = held.shape[1] // 2 - GEO_ROWS // 2, held.shape[2]
    n_tri = triangle(n_new)
    n_pairs = n_tri + n_new * n_old
    halves = width // BLOCK
    row = lax.broadcasted_iota(jnp.int32, (8, width), 0)
    geo_at = 2 * bands
    for k in range(n_seg):
        piece = held[k, geo_at : geo_at + GEO_ROWS, :].astype(jnp.float32)
        low = jnp.where(row == 0, piece[7:8], jnp.where(row == 1, piece[14:15], piece[15:16]))
        geo_all[k] = (piece[0:8] + piece[8:16]) + jnp.where(row < 3, low, 0.0)
        flag_rows[k] = piece[FLAG_ROW : FLAG_ROW + 1, 0:BLOCK]
    if n_old:
        sums[0:n_old] = old_sums[...]
    sums[n_old:n_seg] = jnp.zeros((n_new, bands, width), jnp.float32)
    origin = jnp.broadcast_to(geo_all[0, :, 0:1], (8, width))
    for k in range(n_seg):
        geo = geo_all[k]
        offset = jnp.where(row < 3, geo - origin, 0.0)
        normal = jnp.where(row < 3, pltpu.roll(geo, 5, 0), 0.0)
        along = jnp.sum(normal * offset, axis=0, keepdims=True)
        for c in range(3):
            far_rep[k, c] = jnp.broadcast_to(geo[c : c + 1], (8, width))
        far_leave[k] = far_stack(jnp.where(row == 3, 1.0, offset))
        far_arrive[k] = far_stack(jnp.where(row == 3, along, normal) * (-1.0 / math.pi))
        if k < n_old:
            continue
        at = k - n_old
        near_pos[at, :, 0:8] = jnp.transpose(geo)
        near_leave[at] = jnp.transpose(near_stack(jnp.where(row == 3, -along, normal))).astype(jnp.bfloat16)
        near_arrive[at] = jnp.transpose(near_stack(jnp.where(row == 3, 1.0, -offset))).astype(jnp.bfloat16)
    col_mask = (1 << col_bits) - 1

    def pair_of(t):
        if t >= n_tri:
            near, far = (t - n_tri) % n_new, (t - n_tri) // n_new
        else:
            near = t % n_new
            far = (near + t // n_new) % n_new + n_old
        return near, near + n_old, far

    def live(near_at, far_at, i, j):
        near = bit_reverse(near_at, bits) << (seg_bits - bits)
        far = bit_reverse(far_at, bits) << (seg_bits - bits)
        holder = (near & ~col_mask) | (far & col_mask)
        apart = near ^ far
        index = ((((apart & col_mask) << 1) | i) * n_far) + (((apart >> col_bits) << 1) | j)
        held_at = bit_reverse(holder >> (seg_bits - bits), bits)
        return flag_rows[held_at, :, index : index + 1]

    def project(t, cosines):
        local, near_at, far_at = pair_of(t)
        masked = []
        for i in range(halves):
            flags = [
                jnp.maximum(live(near_at, far_at, i, j), live(far_at, near_at, j, i))
                for j in range(halves)
            ]
            flags = jnp.concatenate([jnp.broadcast_to(f, (PIECES, BLOCK)) for f in flags], axis=1)
            masked.append(far_arrive[far_at] * flags.astype(jnp.bfloat16))
        for at in range(0, width, CHUNK):
            yield
            rows = slice(at, at + CHUNK)
            leaving = jnp.dot(
                near_leave[local, rows], far_leave[far_at], preferred_element_type=jnp.float32
            )
            arriving = jnp.dot(
                near_arrive[local, rows], masked[at // BLOCK], preferred_element_type=jnp.float32
            )
            cosines[rows] = jnp.maximum(leaving, 0.0) * jnp.maximum(arriving, 0.0)

    def form(t, cosines, fresh):
        local, near_at, far_at = pair_of(t)
        fars = [
            [far_rep[far_at, c, :, j * BLOCK : (j + 1) * BLOCK] for c in range(3)]
            for j in range(halves)
        ]
        for strip in range(width // 16):
            if strip * 16 % CHUNK == 0:
                yield
            nears = []
            for part in range(2):
                at = strip * 16 + part * 8
                if fresh:
                    cols_now = near_pos[local, at : at + 8, :]
                    now = [jnp.broadcast_to(cols_now[:, c : c + 1], (8, BLOCK)) for c in range(3)]
                    for c in range(3):
                        near_rep[local, c, at : at + 8, :] = now[c]
                else:
                    now = [near_rep[local, c, at : at + 8, :] for c in range(3)]
                nears.append(now)
            for j in range(halves):
                cols = slice(j * BLOCK, (j + 1) * BLOCK)
                parts = []
                for part in range(2):
                    at = strip * 16 + part * 8
                    dx, dy, dz = (f - n for f, n in zip(fars[j], nears[part]))
                    spacing = dx * dx + dy * dy + dz * dz + SOFTEN
                    inverse = 1.0 / spacing
                    product = cosines[at : at + 8, cols]
                    parts.append(product * inverse * inverse)
                strip_now = jnp.concatenate(parts, axis=0).astype(jnp.bfloat16)
                tiles[t, strip * 16 : strip * 16 + 16, cols] = strip_now

    def apply(t):
        local, near_at, far_at = pair_of(t)
        tile = tiles[t]
        to_near = lax.dot_general(
            held[far_at, 0:bands, :], tile, (((1,), (1,)), ((), ())), preferred_element_type=jnp.float32
        )
        sums[near_at] = sums[near_at] + to_near
        if near_at != far_at:
            to_far = lax.dot_general(
                held[near_at, 0:bands, :], tile, (((1,), (0,)), ((), ())), preferred_element_type=jnp.float32
            )
            sums[far_at] = sums[far_at] + to_far

    cosines = (even, odd)
    for _ in project(0, even):
        pass
    for t in range(n_pairs):
        later = project(t + 1, cosines[(t + 1) % 2]) if t + 1 < n_pairs else ()
        for _ in itertools.zip_longest(later, form(t, cosines[t % 2], t < n_new)):
            pass
        if t:
            apply(t - 1)
    apply(n_pairs - 1)
    if not last:
        return
    total = jnp.zeros((bands, width), jnp.float32)
    for k in range(n_seg):
        base = held[k, 0:bands, :].astype(jnp.float32)
        gain = held[k, bands : 2 * bands, :].astype(jnp.float32)
        weighted = (base + gain * sums[k]).astype(jnp.bfloat16)
        level = next(i for i, (old, new) in enumerate(levels) if k < old + new)
        old, new = levels[level]
        t, over = (triangle(new) + k - old, 0) if old else own_tile(k, new)
        tile = tiles[t] if k >= n_old else old_tiles[level][t]
        total += lax.dot_general(
            weighted, tile, (((1,), (over,)), ((), ())), preferred_element_type=jnp.float32
        )
    out[...] = emi[...] + ref[...] * total


def grow(levels, seg_bits, col_bits, n_far, args):
    n_old, n_new = levels[-1]
    rows, width = args[0].shape[1:]
    bands = (rows - GEO_ROWS) // 2
    n_seg = n_old + n_new
    last = n_seg == 1 << seg_bits
    n_pairs = triangle(n_new) + n_new * n_old
    vmem = pl.BlockSpec(memory_space=pltpu.VMEM)
    state = [
        pltpu.VMEM((n_pairs, width, width), jnp.bfloat16),
        pltpu.VMEM((n_seg, bands, width), jnp.float32),
    ]
    outs = jax.ShapeDtypeStruct((bands, width), jnp.float32) if last else state[::-1]
    work = n_pairs * width * width
    return pl.pallas_call(
        functools.partial(grow_kernel, levels, seg_bits, col_bits, n_far, last),
        out_shape=outs,
        in_specs=[vmem] * len(args),
        out_specs=vmem if last else [vmem, vmem],
        scratch_shapes=(state + [pltpu.VMEM((n_seg, rows, width), jnp.bfloat16)] if last else [])
        + [
            pltpu.VMEM((n_seg, 8, width), jnp.float32),
            pltpu.VMEM((n_seg, PIECES, width), jnp.bfloat16),
            pltpu.VMEM((n_seg, PIECES, width), jnp.bfloat16),
            pltpu.VMEM((n_seg, 3, 8, width), jnp.float32),
            pltpu.VMEM((n_new, width, BLOCK), jnp.float32),
            pltpu.VMEM((n_new, 3, width, BLOCK), jnp.float32),
            pltpu.VMEM((n_new, width, PIECES), jnp.bfloat16),
            pltpu.VMEM((n_new, width, PIECES), jnp.bfloat16),
            *[pltpu.VMEM((width, width), jnp.float32)] * 2,
            pltpu.VMEM((n_seg, 1, BLOCK), jnp.float32),
        ],
        compiler_params=pltpu.CompilerParams(vmem_limit_bytes=32 * 1024 * 1024),
        cost_estimate=pl.CostEstimate(
            flops=work * (4 * PIECES + 4 * bands), bytes_accessed=n_seg * rows * width * 2, transcendentals=work
        ),
    )(*args)


def one_exchange(positions, normals, areas, emission, reflect, pair_row, pair_col, pair_live):
    n_row = lax.axis_size("row")
    n_col = lax.axis_size("col")
    n_seg = n_row * n_col
    seg_bits = n_seg.bit_length() - 1
    col_bits = n_col.bit_length() - 1
    bands, width = emission.shape
    n_far = width // BLOCK * n_row
    rows = 2 * bands + GEO_ROWS
    vmem = pl.BlockSpec(memory_space=pltpu.VMEM)
    smem = pl.BlockSpec(memory_space=pltpu.SMEM)
    packed = pl.pallas_call(
        functools.partial(pack_kernel, col_bits, n_far),
        out_shape=pltpu.VMEM((rows, width), jnp.bfloat16),
        in_specs=[vmem] * 5 + [smem] * 3,
        out_specs=vmem,
    )(positions, normals, areas.reshape(1, width), emission, reflect, pair_row, pair_col, pair_live)
    gathered = packed[None]

    def swap(value, distance):
        return lax.ppermute(value, ("row", "col"), [(i, i ^ distance) for i in range(n_seg)])

    for bit in reversed(range(2, seg_bits)):
        gathered = jnp.concatenate([gathered, swap(gathered, 1 << bit)])
    beside, across, diagonal = (swap(gathered, distance) for distance in (2, 1, 3))
    quarter, half = n_seg // 4, n_seg // 2
    levels = ((0, quarter), (quarter, quarter), (half, half))
    sums, tiles = grow(levels[:1], seg_bits, col_bits, n_far, (gathered,))
    gathered = jnp.concatenate([gathered, beside])
    sums, more_tiles = grow(levels[:2], seg_bits, col_bits, n_far, (gathered, sums))
    args = (across, diagonal, gathered, emission, reflect, sums, tiles, more_tiles)
    return grow(levels, seg_bits, col_bits, n_far, args)


def form_tiles(near, far):
    offset = far[0:3, :, None, :] - near[0:3, :, :, None]
    leaving = jnp.sum(near[3:6, :, :, None] * offset, axis=0)
    arriving = -jnp.sum(far[3:6, :, None, :] * offset, axis=0)
    spacing = jnp.sum(offset * offset, axis=0) + SOFTEN
    return jax.nn.relu(leaving) * jax.nn.relu(arriving) / (math.pi * spacing * spacing)


def two_exchanges(positions, normals, areas, emission, reflect, pair_row, pair_col, pair_live):
    patch_dev = areas.shape[0]
    own_blocks = patch_dev // BLOCK
    n_row = lax.axis_size("row")
    n_col = lax.axis_size("col")
    row_blocks = own_blocks * n_col
    col_blocks = own_blocks * n_row
    all_blocks = row_blocks * n_row
    band_half = emission.shape[0]
    row_here = lax.axis_index("row")
    col_here = lax.axis_index("col")
    geometry = jnp.concatenate([positions, normals], axis=0)
    geo_rows = lax.all_gather(geometry, "col", axis=1, tiled=True).reshape(6, row_blocks, BLOCK)
    geo_cols = lax.all_gather(geometry, "row", axis=1, tiled=True).reshape(6, col_blocks, BLOCK)
    slots = pair_row.shape[0]
    rows_seen, cols_seen, live_seen = (
        lax.all_gather(pair_row, ("row", "col"), axis=0, tiled=True),
        lax.all_gather(pair_col, ("row", "col"), axis=0, tiled=True),
        lax.all_gather(pair_live, ("row", "col"), axis=0, tiled=True),
    )
    seen = jnp.zeros((all_blocks * all_blocks,), jnp.int32)
    seen = seen.at[rows_seen * all_blocks + cols_seen].max(live_seen)
    seen = seen.at[cols_seen * all_blocks + rows_seen].max(live_seen)
    near_grid = row_here * row_blocks + jnp.arange(row_blocks, dtype=jnp.int32)
    far_local = jnp.arange(col_blocks, dtype=jnp.int32)
    far_grid = (far_local // own_blocks * n_col + col_here) * own_blocks + far_local % own_blocks
    flags = seen[(near_grid[:, None] * all_blocks + far_grid[None, :]).reshape(-1)]
    order = jnp.argsort(1 - flags, stable=True)
    near_index = order // col_blocks
    far_index = order % col_blocks
    live_float = flags[order].astype(jnp.float32)
    live_count = jnp.sum(flags)
    group_size = math.gcd(slots, 32)
    turns = (live_count + group_size - 1) // group_size
    stored_init = jnp.zeros((1, 1, 1), jnp.bfloat16)
    stored = stored_init
    radiosity = emission
    for sweep in range(ITERS):
        weighted = (areas[None, :] * radiosity).astype(jnp.bfloat16)
        w_cols = lax.all_gather(weighted, "row", axis=1, tiled=True).reshape(
            band_half, col_blocks, BLOCK
        )

        def one_turn(turn_index, state_now):
            acc_rows, acc_cols, kept = state_now
            first_slot = turn_index * group_size
            near_now = lax.dynamic_slice_in_dim(near_index, first_slot, group_size)
            far_now = lax.dynamic_slice_in_dim(far_index, first_slot, group_size)
            live_now = lax.dynamic_slice_in_dim(live_float, first_slot, group_size)
            tiles_now = form_tiles(geo_rows[:, near_now], geo_cols[:, far_now]).astype(jnp.bfloat16)
            far_weights = w_cols[:, far_now]
            to_rows = jnp.einsum(
                "buv,kbv->kbu", tiles_now, far_weights, preferred_element_type=jnp.float32
            )
            acc_rows = acc_rows.at[:, near_now].add(to_rows * live_now[None, :, None])
            return (acc_rows, acc_cols, kept)

        zero_rows = jnp.zeros((band_half, row_blocks, BLOCK), jnp.float32)
        zero_cols = jnp.zeros((1, 1, 1), jnp.float32)
        acc_rows, acc_cols, stored = lax.fori_loop(
            0, turns, one_turn, (zero_rows, zero_cols, stored)
        )
        row_sum = lax.psum_scatter(
            acc_rows.reshape(band_half, row_blocks * BLOCK), "col", scatter_dimension=1, tiled=True
        )
        radiosity = emission + reflect * row_sum
    return radiosity


def shards(positions, normals, areas, emission, reflect, pair_row, pair_col, pair_live):
    n_row, n_col = lax.axis_size("row"), lax.axis_size("col")
    n_seg = n_row * n_col
    powers = n_row & (n_row - 1) == 0 and n_col & (n_col - 1) == 0
    small = areas.shape[0] == 2 * BLOCK and 8 <= n_seg <= 16
    plan = one_exchange if powers and small else two_exchanges
    return plan(positions, normals, areas, emission, reflect, pair_row, pair_col, pair_live)


def solution(mesh):
    return jax.shard_map(
        shards,
        mesh=mesh,
        in_specs=(
            P(None, ("case", "row", "col")),
            P(None, ("case", "row", "col")),
            P(("case", "row", "col")),
            P("band", ("case", "row", "col")),
            P("band", ("case", "row", "col")),
            P(("case", "row", "col")),
            P(("case", "row", "col")),
            P(("case", "row", "col")),
        ),
        out_specs=P("band", ("case", "row", "col")),
        check_vma=False,
    )
```

```python
import functools
import itertools
import math

import jax
import jax.numpy as jnp
from jax import lax
from jax.experimental import pallas as pl
from jax.experimental.pallas import tpu as pltpu
from jax.sharding import PartitionSpec as P

BLOCK = 128
ITERS = 2


SOFTEN = 0.02

GEO_ROWS = 16
FLAG_ROW = 6
CHUNK = 128
PIECES = 48


def bit_reverse(value, bits):
    out = value * 0
    for bit in range(bits):
        out = out | (((value >> bit) & 1) << (bits - 1 - bit))
    return out


def three_pieces(x):
    high = x.astype(jnp.bfloat16).astype(jnp.float32)
    rest = x - high
    middle = rest.astype(jnp.bfloat16).astype(jnp.float32)
    return high, middle, rest - middle


def pack_kernel(col_bits, n_far, pos, nrm, area, emi, ref, prow, pcol, plive, out):
    seg = (lax.axis_index("row") << col_bits) | lax.axis_index("col")
    bands, width = emi.shape
    a = area[...]
    out[0:bands, :] = (a * emi[...]).astype(jnp.bfloat16)
    out[bands : 2 * bands, :] = (a * ref[...]).astype(jnp.bfloat16)
    lane = lax.broadcasted_iota(jnp.int32, (1, width), 1)
    col_mask = (1 << col_bits) - 1

    def add_slot(i, flags):
        p, q = prow[i], pcol[i]
        near = ((((p >> 1) ^ seg) & col_mask) << 1) | (p & 1)
        far = ((((q >> 1) ^ seg) >> col_bits) << 1) | (q & 1)
        return flags + jnp.where(lane == near * n_far + far, plive[i], 0)

    flags = lax.fori_loop(0, prow.shape[0], add_slot, jnp.zeros((1, width), jnp.int32), unroll=True)
    high, middle, low = three_pieces(pos[...])
    nrm_high, nrm_rest, _ = three_pieces(nrm[...])
    out[2 * bands : 2 * bands + GEO_ROWS, :] = jnp.concatenate(
        [high, nrm_high, flags.astype(jnp.float32), low[0:1], middle, nrm_rest, low[1:3]], axis=0
    ).astype(jnp.bfloat16)


def near_stack(x):
    high, middle, low = three_pieces(x)
    return jnp.concatenate([high, high, middle, high, low, middle], axis=0)


def far_stack(x):
    high, middle, low = three_pieces(x)
    return jnp.concatenate([high, middle, high, low, high, middle], axis=0).astype(jnp.bfloat16)


def triangle(count):
    return count * (count + 1) // 2


def own_tile(k, count):
    if k <= count // 2:
        return k * count, 1
    return (count - k) * count + k, 0


def diagonal_product(weights, tiles, t):
    width = weights.shape[1]
    blocks = []
    for at in range(0, width, BLOCK):
        block = slice(at, at + BLOCK)
        total = lax.dot_general(
            weights[:, at:], tiles[t, block, at:], (((1,), (1,)), ((), ())),
            preferred_element_type=jnp.float32,
        )
        if at:
            total += jnp.dot(
                weights[:, :at], tiles[t, :at, block], preferred_element_type=jnp.float32
            )
        blocks.append(total)
    return jnp.concatenate(blocks, axis=1)


def grow_kernel(levels, seg_bits, col_bits, n_far, last, *refs):
    n_old, n_new = levels[-1]
    bits = (n_old + n_new).bit_length() - 1
    if last:
        across, diagonal, known, emi, ref, old_sums, *refs = refs
        old_tiles, (out, tiles, sums, held, *scratch) = refs[: len(levels) - 1], refs[len(levels) - 1 :]
        at = 0
        for part in (known, across, diagonal):
            held[at : at + part.shape[0]] = part[...]
            at += part.shape[0]
    elif n_old:
        held, old_sums, sums, tiles, *scratch = refs
    else:
        held, sums, tiles, *scratch = refs
    (
        geo_all, far_leave, far_arrive, far_rep, near_pos, near_rep, near_leave, near_arrive,
        even, odd, flag_rows,
    ) = scratch
    n_seg = n_old + n_new
    bands, width = held.shape[1] // 2 - GEO_ROWS // 2, held.shape[2]
    n_tri = triangle(n_new)
    n_pairs = n_tri + n_new * n_old
    halves = width // BLOCK
    row = lax.broadcasted_iota(jnp.int32, (8, width), 0)
    geo_at = 2 * bands
    for k in range(n_seg):
        piece = held[k, geo_at : geo_at + GEO_ROWS, :].astype(jnp.float32)
        low = jnp.where(row == 0, piece[7:8], jnp.where(row == 1, piece[14:15], piece[15:16]))
        geo_all[k] = (piece[0:8] + piece[8:16]) + jnp.where(row < 3, low, 0.0)
        flag_rows[k] = piece[FLAG_ROW : FLAG_ROW + 1, 0:BLOCK]
    if n_old:
        sums[0:n_old] = old_sums[...]
    sums[n_old:n_seg] = jnp.zeros((n_new, bands, width), jnp.float32)
    origin = jnp.broadcast_to(geo_all[0, :, 0:1], (8, width))
    for k in range(n_seg):
        geo = geo_all[k]
        offset = jnp.where(row < 3, geo - origin, 0.0)
        normal = jnp.where(row < 3, pltpu.roll(geo, 5, 0), 0.0)
        along = jnp.sum(normal * offset, axis=0, keepdims=True)
        for c in range(3):
            far_rep[k, c] = jnp.broadcast_to(geo[c : c + 1], (8, width))
        far_leave[k] = far_stack(jnp.where(row == 3, 1.0, offset))
        far_arrive[k] = far_stack(jnp.where(row == 3, along, normal) * (-1.0 / math.pi))
        if k < n_old:
            continue
        at = k - n_old
        near_pos[at, :, 0:8] = jnp.transpose(geo)
        near_leave[at] = jnp.transpose(near_stack(jnp.where(row == 3, -along, normal))).astype(jnp.bfloat16)
        near_arrive[at] = jnp.transpose(near_stack(jnp.where(row == 3, 1.0, -offset))).astype(jnp.bfloat16)
    col_mask = (1 << col_bits) - 1

    def pair_of(t):
        if t >= n_tri:
            near, far = (t - n_tri) % n_new, (t - n_tri) // n_new
        else:
            near = t % n_new
            far = (near + t // n_new) % n_new + n_old
        return near, near + n_old, far

    def live(near_at, far_at, i, j):
        near = bit_reverse(near_at, bits) << (seg_bits - bits)
        far = bit_reverse(far_at, bits) << (seg_bits - bits)
        holder = (near & ~col_mask) | (far & col_mask)
        apart = near ^ far
        index = ((((apart & col_mask) << 1) | i) * n_far) + (((apart >> col_bits) << 1) | j)
        held_at = bit_reverse(holder >> (seg_bits - bits), bits)
        return flag_rows[held_at, :, index : index + 1]

    def project(t, cosines):
        local, near_at, far_at = pair_of(t)
        masked = []
        for i in range(halves):
            flags = [
                jnp.maximum(live(near_at, far_at, i, j), live(far_at, near_at, j, i))
                for j in range(halves)
            ]
            flags = jnp.concatenate([jnp.broadcast_to(f, (PIECES, BLOCK)) for f in flags], axis=1)
            masked.append(far_arrive[far_at] * flags.astype(jnp.bfloat16))
        for at in range(0, width, CHUNK):
            yield
            rows = slice(at, at + CHUNK)
            cols = slice(at // BLOCK * BLOCK if near_at == far_at else 0, width)
            leaving = jnp.dot(
                near_leave[local, rows], far_leave[far_at, :, cols], preferred_element_type=jnp.float32
            )
            arriving = jnp.dot(
                near_arrive[local, rows], masked[at // BLOCK][:, cols], preferred_element_type=jnp.float32
            )
            cosines[rows, cols] = jnp.maximum(leaving, 0.0) * jnp.maximum(arriving, 0.0)

    def form(t, cosines, fresh):
        local, near_at, far_at = pair_of(t)
        fars = [
            [far_rep[far_at, c, :, j * BLOCK : (j + 1) * BLOCK] for c in range(3)]
            for j in range(halves)
        ]
        for strip in range(width // 16):
            if strip * 16 % CHUNK == 0:
                yield
            nears = []
            for part in range(2):
                at = strip * 16 + part * 8
                if fresh:
                    cols_now = near_pos[local, at : at + 8, :]
                    now = [jnp.broadcast_to(cols_now[:, c : c + 1], (8, BLOCK)) for c in range(3)]
                    for c in range(3):
                        near_rep[local, c, at : at + 8, :] = now[c]
                else:
                    now = [near_rep[local, c, at : at + 8, :] for c in range(3)]
                nears.append(now)
            for j in range(strip * 16 // BLOCK if near_at == far_at else 0, halves):
                cols = slice(j * BLOCK, (j + 1) * BLOCK)
                parts = []
                for part in range(2):
                    at = strip * 16 + part * 8
                    dx, dy, dz = (f - n for f, n in zip(fars[j], nears[part]))
                    spacing = dx * dx + dy * dy + dz * dz + SOFTEN
                    inverse = 1.0 / spacing
                    product = cosines[at : at + 8, cols]
                    parts.append(product * inverse * inverse)
                strip_now = jnp.concatenate(parts, axis=0).astype(jnp.bfloat16)
                tiles[t, strip * 16 : strip * 16 + 16, cols] = strip_now

    def apply(t):
        local, near_at, far_at = pair_of(t)
        if near_at == far_at:
            sums[near_at] = sums[near_at] + diagonal_product(held[far_at, 0:bands, :], tiles, t)
            return
        tile = tiles[t]
        to_near = lax.dot_general(
            held[far_at, 0:bands, :], tile, (((1,), (1,)), ((), ())), preferred_element_type=jnp.float32
        )
        sums[near_at] = sums[near_at] + to_near
        to_far = lax.dot_general(
            held[near_at, 0:bands, :], tile, (((1,), (0,)), ((), ())), preferred_element_type=jnp.float32
        )
        sums[far_at] = sums[far_at] + to_far

    cosines = (even, odd)
    for _ in project(0, even):
        pass
    for t in range(n_pairs):
        later = project(t + 1, cosines[(t + 1) % 2]) if t + 1 < n_pairs else ()
        for _ in itertools.zip_longest(later, form(t, cosines[t % 2], t < n_new)):
            pass
        if t:
            apply(t - 1)
    apply(n_pairs - 1)
    if not last:
        return
    total = jnp.zeros((bands, width), jnp.float32)
    for k in range(n_seg):
        base = held[k, 0:bands, :].astype(jnp.float32)
        gain = held[k, bands : 2 * bands, :].astype(jnp.float32)
        weighted = (base + gain * sums[k]).astype(jnp.bfloat16)
        level = next(i for i, (old, new) in enumerate(levels) if k < old + new)
        old, new = levels[level]
        t, over = (triangle(new) + k - old, 0) if old else own_tile(k, new)
        if k == 0:
            total += diagonal_product(weighted, old_tiles[level], t)
            continue
        tile = tiles[t] if k >= n_old else old_tiles[level][t]
        total += lax.dot_general(
            weighted, tile, (((1,), (over,)), ((), ())), preferred_element_type=jnp.float32
        )
    out[...] = emi[...] + ref[...] * total


def grow(levels, seg_bits, col_bits, n_far, args):
    n_old, n_new = levels[-1]
    rows, width = args[0].shape[1:]
    bands = (rows - GEO_ROWS) // 2
    n_seg = n_old + n_new
    last = n_seg == 1 << seg_bits
    n_pairs = triangle(n_new) + n_new * n_old
    vmem = pl.BlockSpec(memory_space=pltpu.VMEM)
    state = [
        pltpu.VMEM((n_pairs, width, width), jnp.bfloat16),
        pltpu.VMEM((n_seg, bands, width), jnp.float32),
    ]
    outs = jax.ShapeDtypeStruct((bands, width), jnp.float32) if last else state[::-1]
    work = n_pairs * width * width
    return pl.pallas_call(
        functools.partial(grow_kernel, levels, seg_bits, col_bits, n_far, last),
        out_shape=outs,
        in_specs=[vmem] * len(args),
        out_specs=vmem if last else [vmem, vmem],
        scratch_shapes=(state + [pltpu.VMEM((n_seg, rows, width), jnp.bfloat16)] if last else [])
        + [
            pltpu.VMEM((n_seg, 8, width), jnp.float32),
            pltpu.VMEM((n_seg, PIECES, width), jnp.bfloat16),
            pltpu.VMEM((n_seg, PIECES, width), jnp.bfloat16),
            pltpu.VMEM((n_seg, 3, 8, width), jnp.float32),
            pltpu.VMEM((n_new, width, BLOCK), jnp.float32),
            pltpu.VMEM((n_new, 3, width, BLOCK), jnp.float32),
            pltpu.VMEM((n_new, width, PIECES), jnp.bfloat16),
            pltpu.VMEM((n_new, width, PIECES), jnp.bfloat16),
            *[pltpu.VMEM((width, width), jnp.float32)] * 2,
            pltpu.VMEM((n_seg, 1, BLOCK), jnp.float32),
        ],
        compiler_params=pltpu.CompilerParams(vmem_limit_bytes=32 * 1024 * 1024),
        cost_estimate=pl.CostEstimate(
            flops=work * (4 * PIECES + 4 * bands), bytes_accessed=n_seg * rows * width * 2, transcendentals=work
        ),
    )(*args)


def one_exchange(positions, normals, areas, emission, reflect, pair_row, pair_col, pair_live):
    n_row = lax.axis_size("row")
    n_col = lax.axis_size("col")
    n_seg = n_row * n_col
    seg_bits = n_seg.bit_length() - 1
    col_bits = n_col.bit_length() - 1
    bands, width = emission.shape
    n_far = width // BLOCK * n_row
    rows = 2 * bands + GEO_ROWS
    vmem = pl.BlockSpec(memory_space=pltpu.VMEM)
    smem = pl.BlockSpec(memory_space=pltpu.SMEM)
    packed = pl.pallas_call(
        functools.partial(pack_kernel, col_bits, n_far),
        out_shape=pltpu.VMEM((rows, width), jnp.bfloat16),
        in_specs=[vmem] * 5 + [smem] * 3,
        out_specs=vmem,
    )(positions, normals, areas.reshape(1, width), emission, reflect, pair_row, pair_col, pair_live)
    gathered = packed[None]

    def swap(value, distance):
        return lax.ppermute(value, ("row", "col"), [(i, i ^ distance) for i in range(n_seg)])

    for bit in reversed(range(2, seg_bits)):
        gathered = jnp.concatenate([gathered, swap(gathered, 1 << bit)])
    beside, across, diagonal = (swap(gathered, distance) for distance in (2, 1, 3))
    quarter, half = n_seg // 4, n_seg // 2
    levels = ((0, quarter), (quarter, quarter), (half, half))
    sums, tiles = grow(levels[:1], seg_bits, col_bits, n_far, (gathered,))
    gathered = jnp.concatenate([gathered, beside])
    sums, more_tiles = grow(levels[:2], seg_bits, col_bits, n_far, (gathered, sums))
    args = (across, diagonal, gathered, emission, reflect, sums, tiles, more_tiles)
    return grow(levels, seg_bits, col_bits, n_far, args)


def form_tiles(near, far):
    offset = far[0:3, :, None, :] - near[0:3, :, :, None]
    leaving = jnp.sum(near[3:6, :, :, None] * offset, axis=0)
    arriving = -jnp.sum(far[3:6, :, None, :] * offset, axis=0)
    spacing = jnp.sum(offset * offset, axis=0) + SOFTEN
    return jax.nn.relu(leaving) * jax.nn.relu(arriving) / (math.pi * spacing * spacing)


def two_exchanges(positions, normals, areas, emission, reflect, pair_row, pair_col, pair_live):
    patch_dev = areas.shape[0]
    own_blocks = patch_dev // BLOCK
    n_row = lax.axis_size("row")
    n_col = lax.axis_size("col")
    row_blocks = own_blocks * n_col
    col_blocks = own_blocks * n_row
    all_blocks = row_blocks * n_row
    band_half = emission.shape[0]
    row_here = lax.axis_index("row")
    col_here = lax.axis_index("col")
    geometry = jnp.concatenate([positions, normals], axis=0)
    geo_rows = lax.all_gather(geometry, "col", axis=1, tiled=True).reshape(6, row_blocks, BLOCK)
    geo_cols = lax.all_gather(geometry, "row", axis=1, tiled=True).reshape(6, col_blocks, BLOCK)
    slots = pair_row.shape[0]
    rows_seen, cols_seen, live_seen = (
        lax.all_gather(pair_row, ("row", "col"), axis=0, tiled=True),
        lax.all_gather(pair_col, ("row", "col"), axis=0, tiled=True),
        lax.all_gather(pair_live, ("row", "col"), axis=0, tiled=True),
    )
    seen = jnp.zeros((all_blocks * all_blocks,), jnp.int32)
    seen = seen.at[rows_seen * all_blocks + cols_seen].max(live_seen)
    seen = seen.at[cols_seen * all_blocks + rows_seen].max(live_seen)
    near_grid = row_here * row_blocks + jnp.arange(row_blocks, dtype=jnp.int32)
    far_local = jnp.arange(col_blocks, dtype=jnp.int32)
    far_grid = (far_local // own_blocks * n_col + col_here) * own_blocks + far_local % own_blocks
    flags = seen[(near_grid[:, None] * all_blocks + far_grid[None, :]).reshape(-1)]
    order = jnp.argsort(1 - flags, stable=True)
    near_index = order // col_blocks
    far_index = order % col_blocks
    live_float = flags[order].astype(jnp.float32)
    live_count = jnp.sum(flags)
    group_size = math.gcd(slots, 32)
    turns = (live_count + group_size - 1) // group_size
    stored_init = jnp.zeros((1, 1, 1), jnp.bfloat16)
    stored = stored_init
    radiosity = emission
    for sweep in range(ITERS):
        weighted = (areas[None, :] * radiosity).astype(jnp.bfloat16)
        w_cols = lax.all_gather(weighted, "row", axis=1, tiled=True).reshape(
            band_half, col_blocks, BLOCK
        )

        def one_turn(turn_index, state_now):
            acc_rows, acc_cols, kept = state_now
            first_slot = turn_index * group_size
            near_now = lax.dynamic_slice_in_dim(near_index, first_slot, group_size)
            far_now = lax.dynamic_slice_in_dim(far_index, first_slot, group_size)
            live_now = lax.dynamic_slice_in_dim(live_float, first_slot, group_size)
            tiles_now = form_tiles(geo_rows[:, near_now], geo_cols[:, far_now]).astype(jnp.bfloat16)
            far_weights = w_cols[:, far_now]
            to_rows = jnp.einsum(
                "buv,kbv->kbu", tiles_now, far_weights, preferred_element_type=jnp.float32
            )
            acc_rows = acc_rows.at[:, near_now].add(to_rows * live_now[None, :, None])
            return (acc_rows, acc_cols, kept)

        zero_rows = jnp.zeros((band_half, row_blocks, BLOCK), jnp.float32)
        zero_cols = jnp.zeros((1, 1, 1), jnp.float32)
        acc_rows, acc_cols, stored = lax.fori_loop(
            0, turns, one_turn, (zero_rows, zero_cols, stored)
        )
        row_sum = lax.psum_scatter(
            acc_rows.reshape(band_half, row_blocks * BLOCK), "col", scatter_dimension=1, tiled=True
        )
        radiosity = emission + reflect * row_sum
    return radiosity


def shards(positions, normals, areas, emission, reflect, pair_row, pair_col, pair_live):
    n_row, n_col = lax.axis_size("row"), lax.axis_size("col")
    n_seg = n_row * n_col
    powers = n_row & (n_row - 1) == 0 and n_col & (n_col - 1) == 0
    small = areas.shape[0] == 2 * BLOCK and 8 <= n_seg <= 16
    plan = one_exchange if powers and small else two_exchanges
    return plan(positions, normals, areas, emission, reflect, pair_row, pair_col, pair_live)


def solution(mesh):
    return jax.shard_map(
        shards,
        mesh=mesh,
        in_specs=(
            P(None, ("case", "row", "col")),
            P(None, ("case", "row", "col")),
            P(("case", "row", "col")),
            P("band", ("case", "row", "col")),
            P("band", ("case", "row", "col")),
            P(("case", "row", "col")),
            P(("case", "row", "col")),
            P(("case", "row", "col")),
        ),
        out_specs=P("band", ("case", "row", "col")),
        check_vma=False,
    )
```

```python
import functools
import itertools
import math

import jax
import jax.numpy as jnp
from jax import lax
from jax.experimental import pallas as pl
from jax.experimental.pallas import tpu as pltpu
from jax.sharding import PartitionSpec as P

BLOCK = 128
ITERS = 2


SOFTEN = 0.02

GEO_ROWS = 16
FLAG_ROW = 6
CHUNK = 128
PIECES = 48


def bit_reverse(value, bits):
    out = value * 0
    for bit in range(bits):
        out = out | (((value >> bit) & 1) << (bits - 1 - bit))
    return out


def three_pieces(x):
    high = x.astype(jnp.bfloat16).astype(jnp.float32)
    rest = x - high
    middle = rest.astype(jnp.bfloat16).astype(jnp.float32)
    return high, middle, rest - middle


def pack_kernel(col_bits, n_far, pos, nrm, area, emi, ref, prow, pcol, plive, out):
    seg = (lax.axis_index("row") << col_bits) | lax.axis_index("col")
    bands, width = emi.shape
    a = area[...]
    out[0:bands, :] = (a * emi[...]).astype(jnp.bfloat16)
    out[bands : 2 * bands, :] = (a * ref[...]).astype(jnp.bfloat16)
    col_mask = (1 << col_bits) - 1
    p, q = prow[...], pcol[...]
    near = ((((p >> 1) ^ seg) & col_mask) << 1) | (p & 1)
    far = ((((q >> 1) ^ seg) >> col_bits) << 1) | (q & 1)
    slots = p.shape[1]
    place = lax.broadcasted_iota(jnp.int32, (BLOCK, slots), 0)
    chosen = jnp.where(place == near * n_far + far, plive[...], 0).astype(jnp.float32)
    flags = lax.dot_general(
        jnp.ones((8, slots), jnp.float32), chosen, (((1,), (1,)), ((), ())),
        preferred_element_type=jnp.float32,
    )
    flags = jnp.concatenate([flags[0:1], jnp.zeros((1, width - BLOCK), jnp.float32)], axis=1)
    high, middle, low = three_pieces(pos[...])
    nrm_high, nrm_rest, _ = three_pieces(nrm[...])
    out[2 * bands : 2 * bands + GEO_ROWS, :] = jnp.concatenate(
        [high, nrm_high, flags, low[0:1], middle, nrm_rest, low[1:3]], axis=0
    ).astype(jnp.bfloat16)


def near_stack(x):
    high, middle, low = three_pieces(x)
    return jnp.concatenate([high, high, middle, high, low, middle], axis=0)


def far_stack(x):
    high, middle, low = three_pieces(x)
    return jnp.concatenate([high, middle, high, low, high, middle], axis=0).astype(jnp.bfloat16)


def triangle(count):
    return count * (count + 1) // 2


def own_tile(k, count):
    if k <= count // 2:
        return k * count, 1
    return (count - k) * count + k, 0


def diagonal_product(weights, tiles, t):
    width = weights.shape[1]
    blocks = []
    for at in range(0, width, BLOCK):
        block = slice(at, at + BLOCK)
        total = lax.dot_general(
            weights[:, at:], tiles[t, block, at:], (((1,), (1,)), ((), ())),
            preferred_element_type=jnp.float32,
        )
        if at:
            total += jnp.dot(
                weights[:, :at], tiles[t, :at, block], preferred_element_type=jnp.float32
            )
        blocks.append(total)
    return jnp.concatenate(blocks, axis=1)


def grow_kernel(levels, seg_bits, col_bits, n_far, last, *refs):
    n_old, n_new = levels[-1]
    bits = (n_old + n_new).bit_length() - 1
    if last:
        across, diagonal, known, emi, ref, old_sums, *refs = refs
        old_tiles, (out, tiles, sums, held, *scratch) = refs[: len(levels) - 1], refs[len(levels) - 1 :]
        at = 0
        for part in (known, across, diagonal):
            held[at : at + part.shape[0]] = part[...]
            at += part.shape[0]
    elif n_old:
        held, old_sums, sums, tiles, *scratch = refs
    else:
        held, sums, tiles, *scratch = refs
    (
        geo_all, far_leave, far_arrive, far_rep, near_pos, near_rep, near_leave, near_arrive,
        even, odd, flag_rows,
    ) = scratch
    n_seg = n_old + n_new
    bands, width = held.shape[1] // 2 - GEO_ROWS // 2, held.shape[2]
    n_tri = triangle(n_new)
    n_pairs = n_tri + n_new * n_old
    halves = width // BLOCK
    row = lax.broadcasted_iota(jnp.int32, (8, width), 0)
    geo_at = 2 * bands
    for k in range(n_seg):
        piece = held[k, geo_at : geo_at + GEO_ROWS, :].astype(jnp.float32)
        low = jnp.where(row == 0, piece[7:8], jnp.where(row == 1, piece[14:15], piece[15:16]))
        geo_all[k] = (piece[0:8] + piece[8:16]) + jnp.where(row < 3, low, 0.0)
        flag_rows[k] = piece[FLAG_ROW : FLAG_ROW + 1, 0:BLOCK]
    if n_old:
        sums[0:n_old] = old_sums[...]
    sums[n_old:n_seg] = jnp.zeros((n_new, bands, width), jnp.float32)
    origin = jnp.broadcast_to(geo_all[0, :, 0:1], (8, width))
    for k in range(n_seg):
        geo = geo_all[k]
        offset = jnp.where(row < 3, geo - origin, 0.0)
        normal = jnp.where(row < 3, pltpu.roll(geo, 5, 0), 0.0)
        along = jnp.sum(normal * offset, axis=0, keepdims=True)
        for c in range(3):
            far_rep[k, c] = jnp.broadcast_to(geo[c : c + 1], (8, width))
        far_leave[k] = far_stack(jnp.where(row == 3, 1.0, offset))
        far_arrive[k] = far_stack(jnp.where(row == 3, along, normal) * (-1.0 / math.pi))
        if k < n_old:
            continue
        at = k - n_old
        near_pos[at, :, 0:8] = jnp.transpose(geo)
        near_leave[at] = jnp.transpose(near_stack(jnp.where(row == 3, -along, normal))).astype(jnp.bfloat16)
        near_arrive[at] = jnp.transpose(near_stack(jnp.where(row == 3, 1.0, -offset))).astype(jnp.bfloat16)
    col_mask = (1 << col_bits) - 1

    def pair_of(t):
        if t >= n_tri:
            near, far = (t - n_tri) % n_new, (t - n_tri) // n_new
        else:
            near = t % n_new
            far = (near + t // n_new) % n_new + n_old
        return near, near + n_old, far

    def live(near_at, far_at, i, j):
        near = bit_reverse(near_at, bits) << (seg_bits - bits)
        far = bit_reverse(far_at, bits) << (seg_bits - bits)
        holder = (near & ~col_mask) | (far & col_mask)
        apart = near ^ far
        index = ((((apart & col_mask) << 1) | i) * n_far) + (((apart >> col_bits) << 1) | j)
        held_at = bit_reverse(holder >> (seg_bits - bits), bits)
        return flag_rows[held_at, :, index : index + 1]

    def project(t, cosines):
        local, near_at, far_at = pair_of(t)
        masked = []
        for i in range(halves):
            flags = [
                jnp.maximum(live(near_at, far_at, i, j), live(far_at, near_at, j, i))
                for j in range(halves)
            ]
            flags = jnp.concatenate([jnp.broadcast_to(f, (PIECES, BLOCK)) for f in flags], axis=1)
            masked.append(far_arrive[far_at] * flags.astype(jnp.bfloat16))
        for at in range(0, width, CHUNK):
            yield
            rows = slice(at, at + CHUNK)
            cols = slice(at // BLOCK * BLOCK if near_at == far_at else 0, width)
            leaving = jnp.dot(
                near_leave[local, rows], far_leave[far_at, :, cols], preferred_element_type=jnp.float32
            )
            arriving = jnp.dot(
                near_arrive[local, rows], masked[at // BLOCK][:, cols], preferred_element_type=jnp.float32
            )
            cosines[rows, cols] = jnp.maximum(leaving, 0.0) * jnp.maximum(arriving, 0.0)

    def form(t, cosines, fresh):
        local, near_at, far_at = pair_of(t)
        fars = [
            [far_rep[far_at, c, :, j * BLOCK : (j + 1) * BLOCK] for c in range(3)]
            for j in range(halves)
        ]
        for strip in range(width // 16):
            if strip * 16 % CHUNK == 0:
                yield
            nears = []
            for part in range(2):
                at = strip * 16 + part * 8
                if fresh:
                    cols_now = near_pos[local, at : at + 8, :]
                    now = [jnp.broadcast_to(cols_now[:, c : c + 1], (8, BLOCK)) for c in range(3)]
                    for c in range(3):
                        near_rep[local, c, at : at + 8, :] = now[c]
                else:
                    now = [near_rep[local, c, at : at + 8, :] for c in range(3)]
                nears.append(now)
            for j in range(strip * 16 // BLOCK if near_at == far_at else 0, halves):
                cols = slice(j * BLOCK, (j + 1) * BLOCK)
                parts = []
                for part in range(2):
                    at = strip * 16 + part * 8
                    dx, dy, dz = (f - n for f, n in zip(fars[j], nears[part]))
                    spacing = dx * dx + dy * dy + dz * dz + SOFTEN
                    inverse = 1.0 / spacing
                    product = cosines[at : at + 8, cols]
                    parts.append(product * inverse * inverse)
                strip_now = jnp.concatenate(parts, axis=0).astype(jnp.bfloat16)
                tiles[t, strip * 16 : strip * 16 + 16, cols] = strip_now

    def apply(t):
        local, near_at, far_at = pair_of(t)
        if near_at == far_at:
            sums[near_at] = sums[near_at] + diagonal_product(held[far_at, 0:bands, :], tiles, t)
            return
        tile = tiles[t]
        to_near = lax.dot_general(
            held[far_at, 0:bands, :], tile, (((1,), (1,)), ((), ())), preferred_element_type=jnp.float32
        )
        sums[near_at] = sums[near_at] + to_near
        to_far = lax.dot_general(
            held[near_at, 0:bands, :], tile, (((1,), (0,)), ((), ())), preferred_element_type=jnp.float32
        )
        sums[far_at] = sums[far_at] + to_far

    cosines = (even, odd)
    for _ in project(0, even):
        pass
    for t in range(n_pairs):
        later = project(t + 1, cosines[(t + 1) % 2]) if t + 1 < n_pairs else ()
        for _ in itertools.zip_longest(later, form(t, cosines[t % 2], t < n_new)):
            pass
        if t:
            apply(t - 1)
    apply(n_pairs - 1)
    if not last:
        return
    total = jnp.zeros((bands, width), jnp.float32)
    for k in range(n_seg):
        base = held[k, 0:bands, :].astype(jnp.float32)
        gain = held[k, bands : 2 * bands, :].astype(jnp.float32)
        weighted = (base + gain * sums[k]).astype(jnp.bfloat16)
        level = next(i for i, (old, new) in enumerate(levels) if k < old + new)
        old, new = levels[level]
        t, over = (triangle(new) + k - old, 0) if old else own_tile(k, new)
        if k == 0:
            total += diagonal_product(weighted, old_tiles[level], t)
            continue
        tile = tiles[t] if k >= n_old else old_tiles[level][t]
        total += lax.dot_general(
            weighted, tile, (((1,), (over,)), ((), ())), preferred_element_type=jnp.float32
        )
    out[...] = emi[...] + ref[...] * total


def grow(levels, seg_bits, col_bits, n_far, args):
    n_old, n_new = levels[-1]
    rows, width = args[0].shape[1:]
    bands = (rows - GEO_ROWS) // 2
    n_seg = n_old + n_new
    last = n_seg == 1 << seg_bits
    n_pairs = triangle(n_new) + n_new * n_old
    vmem = pl.BlockSpec(memory_space=pltpu.VMEM)
    state = [
        pltpu.VMEM((n_pairs, width, width), jnp.bfloat16),
        pltpu.VMEM((n_seg, bands, width), jnp.float32),
    ]
    outs = jax.ShapeDtypeStruct((bands, width), jnp.float32) if last else state[::-1]
    work = n_pairs * width * width
    return pl.pallas_call(
        functools.partial(grow_kernel, levels, seg_bits, col_bits, n_far, last),
        out_shape=outs,
        in_specs=[vmem] * len(args),
        out_specs=vmem if last else [vmem, vmem],
        scratch_shapes=(state + [pltpu.VMEM((n_seg, rows, width), jnp.bfloat16)] if last else [])
        + [
            pltpu.VMEM((n_seg, 8, width), jnp.float32),
            pltpu.VMEM((n_seg, PIECES, width), jnp.bfloat16),
            pltpu.VMEM((n_seg, PIECES, width), jnp.bfloat16),
            pltpu.VMEM((n_seg, 3, 8, width), jnp.float32),
            pltpu.VMEM((n_new, width, BLOCK), jnp.float32),
            pltpu.VMEM((n_new, 3, width, BLOCK), jnp.float32),
            pltpu.VMEM((n_new, width, PIECES), jnp.bfloat16),
            pltpu.VMEM((n_new, width, PIECES), jnp.bfloat16),
            *[pltpu.VMEM((width, width), jnp.float32)] * 2,
            pltpu.VMEM((n_seg, 1, BLOCK), jnp.float32),
        ],
        compiler_params=pltpu.CompilerParams(vmem_limit_bytes=32 * 1024 * 1024),
        cost_estimate=pl.CostEstimate(
            flops=work * (4 * PIECES + 4 * bands), bytes_accessed=n_seg * rows * width * 2, transcendentals=work
        ),
    )(*args)


def one_exchange(positions, normals, areas, emission, reflect, pair_row, pair_col, pair_live):
    n_row = lax.axis_size("row")
    n_col = lax.axis_size("col")
    n_seg = n_row * n_col
    seg_bits = n_seg.bit_length() - 1
    col_bits = n_col.bit_length() - 1
    bands, width = emission.shape
    n_far = width // BLOCK * n_row
    rows = 2 * bands + GEO_ROWS
    vmem = pl.BlockSpec(memory_space=pltpu.VMEM)
    pairs = [pair.reshape(1, -1) for pair in (pair_row, pair_col, pair_live)]
    packed = pl.pallas_call(
        functools.partial(pack_kernel, col_bits, n_far),
        out_shape=pltpu.VMEM((rows, width), jnp.bfloat16),
        in_specs=[vmem] * 8,
        out_specs=vmem,
    )(positions, normals, areas.reshape(1, width), emission, reflect, *pairs)
    gathered = packed[None]

    def swap(value, distance):
        return lax.ppermute(value, ("row", "col"), [(i, i ^ distance) for i in range(n_seg)])

    for bit in reversed(range(2, seg_bits)):
        gathered = jnp.concatenate([gathered, swap(gathered, 1 << bit)])
    beside, across, diagonal = (swap(gathered, distance) for distance in (2, 1, 3))
    quarter, half = n_seg // 4, n_seg // 2
    levels = ((0, quarter), (quarter, quarter), (half, half))
    sums, tiles = grow(levels[:1], seg_bits, col_bits, n_far, (gathered,))
    gathered = jnp.concatenate([gathered, beside])
    sums, more_tiles = grow(levels[:2], seg_bits, col_bits, n_far, (gathered, sums))
    args = (across, diagonal, gathered, emission, reflect, sums, tiles, more_tiles)
    return grow(levels, seg_bits, col_bits, n_far, args)


def form_tiles(near, far):
    offset = far[0:3, :, None, :] - near[0:3, :, :, None]
    leaving = jnp.sum(near[3:6, :, :, None] * offset, axis=0)
    arriving = -jnp.sum(far[3:6, :, None, :] * offset, axis=0)
    spacing = jnp.sum(offset * offset, axis=0) + SOFTEN
    return jax.nn.relu(leaving) * jax.nn.relu(arriving) / (math.pi * spacing * spacing)


def two_exchanges(positions, normals, areas, emission, reflect, pair_row, pair_col, pair_live):
    patch_dev = areas.shape[0]
    own_blocks = patch_dev // BLOCK
    n_row = lax.axis_size("row")
    n_col = lax.axis_size("col")
    row_blocks = own_blocks * n_col
    col_blocks = own_blocks * n_row
    all_blocks = row_blocks * n_row
    band_half = emission.shape[0]
    row_here = lax.axis_index("row")
    col_here = lax.axis_index("col")
    geometry = jnp.concatenate([positions, normals], axis=0)
    geo_rows = lax.all_gather(geometry, "col", axis=1, tiled=True).reshape(6, row_blocks, BLOCK)
    geo_cols = lax.all_gather(geometry, "row", axis=1, tiled=True).reshape(6, col_blocks, BLOCK)
    slots = pair_row.shape[0]
    rows_seen, cols_seen, live_seen = (
        lax.all_gather(pair_row, ("row", "col"), axis=0, tiled=True),
        lax.all_gather(pair_col, ("row", "col"), axis=0, tiled=True),
        lax.all_gather(pair_live, ("row", "col"), axis=0, tiled=True),
    )
    seen = jnp.zeros((all_blocks * all_blocks,), jnp.int32)
    seen = seen.at[rows_seen * all_blocks + cols_seen].max(live_seen)
    seen = seen.at[cols_seen * all_blocks + rows_seen].max(live_seen)
    near_grid = row_here * row_blocks + jnp.arange(row_blocks, dtype=jnp.int32)
    far_local = jnp.arange(col_blocks, dtype=jnp.int32)
    far_grid = (far_local // own_blocks * n_col + col_here) * own_blocks + far_local % own_blocks
    flags = seen[(near_grid[:, None] * all_blocks + far_grid[None, :]).reshape(-1)]
    order = jnp.argsort(1 - flags, stable=True)
    near_index = order // col_blocks
    far_index = order % col_blocks
    live_float = flags[order].astype(jnp.float32)
    live_count = jnp.sum(flags)
    group_size = math.gcd(slots, 32)
    turns = (live_count + group_size - 1) // group_size
    stored_init = jnp.zeros((1, 1, 1), jnp.bfloat16)
    stored = stored_init
    radiosity = emission
    for sweep in range(ITERS):
        weighted = (areas[None, :] * radiosity).astype(jnp.bfloat16)
        w_cols = lax.all_gather(weighted, "row", axis=1, tiled=True).reshape(
            band_half, col_blocks, BLOCK
        )

        def one_turn(turn_index, state_now):
            acc_rows, acc_cols, kept = state_now
            first_slot = turn_index * group_size
            near_now = lax.dynamic_slice_in_dim(near_index, first_slot, group_size)
            far_now = lax.dynamic_slice_in_dim(far_index, first_slot, group_size)
            live_now = lax.dynamic_slice_in_dim(live_float, first_slot, group_size)
            tiles_now = form_tiles(geo_rows[:, near_now], geo_cols[:, far_now]).astype(jnp.bfloat16)
            far_weights = w_cols[:, far_now]
            to_rows = jnp.einsum(
                "buv,kbv->kbu", tiles_now, far_weights, preferred_element_type=jnp.float32
            )
            acc_rows = acc_rows.at[:, near_now].add(to_rows * live_now[None, :, None])
            return (acc_rows, acc_cols, kept)

        zero_rows = jnp.zeros((band_half, row_blocks, BLOCK), jnp.float32)
        zero_cols = jnp.zeros((1, 1, 1), jnp.float32)
        acc_rows, acc_cols, stored = lax.fori_loop(
            0, turns, one_turn, (zero_rows, zero_cols, stored)
        )
        row_sum = lax.psum_scatter(
            acc_rows.reshape(band_half, row_blocks * BLOCK), "col", scatter_dimension=1, tiled=True
        )
        radiosity = emission + reflect * row_sum
    return radiosity


def shards(positions, normals, areas, emission, reflect, pair_row, pair_col, pair_live):
    n_row, n_col = lax.axis_size("row"), lax.axis_size("col")
    n_seg = n_row * n_col
    powers = n_row & (n_row - 1) == 0 and n_col & (n_col - 1) == 0
    small = areas.shape[0] == 2 * BLOCK and 8 <= n_seg <= 16
    plan = one_exchange if powers and small else two_exchanges
    return plan(positions, normals, areas, emission, reflect, pair_row, pair_col, pair_live)


def solution(mesh):
    return jax.shard_map(
        shards,
        mesh=mesh,
        in_specs=(
            P(None, ("case", "row", "col")),
            P(None, ("case", "row", "col")),
            P(("case", "row", "col")),
            P("band", ("case", "row", "col")),
            P("band", ("case", "row", "col")),
            P(("case", "row", "col")),
            P(("case", "row", "col")),
            P(("case", "row", "col")),
        ),
        out_specs=P("band", ("case", "row", "col")),
        check_vma=False,
    )
```

```python
import functools
import itertools
import math

import jax
import jax.numpy as jnp
from jax import lax
from jax.experimental import pallas as pl
from jax.experimental.pallas import tpu as pltpu
from jax.sharding import PartitionSpec as P

BLOCK = 128
ITERS = 2


SOFTEN = 0.02

GEO_ROWS = 16
FLAG_ROW = 6
CHUNK = 128
PIECES = 48


def bit_reverse(value, bits):
    out = value * 0
    for bit in range(bits):
        out = out | (((value >> bit) & 1) << (bits - 1 - bit))
    return out


def three_pieces(x):
    high = x.astype(jnp.bfloat16).astype(jnp.float32)
    rest = x - high
    middle = rest.astype(jnp.bfloat16).astype(jnp.float32)
    return high, middle, rest - middle


def pack_kernel(col_bits, n_far, pos, nrm, area, emi, ref, prow, pcol, plive, out):
    seg = (lax.axis_index("row") << col_bits) | lax.axis_index("col")
    bands, width = emi.shape
    a = area[...]
    out[0:bands, :] = (a * emi[...]).astype(jnp.bfloat16)
    out[bands : 2 * bands, :] = (a * ref[...]).astype(jnp.bfloat16)
    col_mask = (1 << col_bits) - 1
    p, q = prow[...], pcol[...]
    near = ((((p >> 1) ^ seg) & col_mask) << 1) | (p & 1)
    far = ((((q >> 1) ^ seg) >> col_bits) << 1) | (q & 1)
    slots = p.shape[1]
    place = lax.broadcasted_iota(jnp.int32, (BLOCK, slots), 0)
    chosen = jnp.where(place == near * n_far + far, plive[...], 0).astype(jnp.float32)
    flags = lax.dot_general(
        jnp.ones((8, slots), jnp.float32), chosen, (((1,), (1,)), ((), ())),
        preferred_element_type=jnp.float32,
    )
    flags = jnp.concatenate([flags[0:1], jnp.zeros((1, width - BLOCK), jnp.float32)], axis=1)
    high, middle, low = three_pieces(pos[...])
    nrm_high, nrm_rest, _ = three_pieces(nrm[...])
    out[2 * bands : 2 * bands + GEO_ROWS, :] = jnp.concatenate(
        [high, nrm_high, flags, low[0:1], middle, nrm_rest, low[1:3]], axis=0
    ).astype(jnp.bfloat16)


def near_stack(x):
    high, middle, low = three_pieces(x)
    return jnp.concatenate([high, high, middle, high, low, middle], axis=0)


def far_stack(x):
    high, middle, low = three_pieces(x)
    return jnp.concatenate([high, middle, high, low, high, middle], axis=0).astype(jnp.bfloat16)


def triangle(count):
    return count * (count + 1) // 2


def own_tile(k, count):
    if k <= count // 2:
        return k * count, 1
    return (count - k) * count + k, 0


def diagonal_product(weights, tiles, t):
    width = weights.shape[1]
    blocks = []
    for at in range(0, width, BLOCK):
        block = slice(at, at + BLOCK)
        total = lax.dot_general(
            weights[:, at:], tiles[t, block, at:], (((1,), (1,)), ((), ())),
            preferred_element_type=jnp.float32,
        )
        if at:
            total += jnp.dot(
                weights[:, :at], tiles[t, :at, block], preferred_element_type=jnp.float32
            )
        blocks.append(total)
    return jnp.concatenate(blocks, axis=1)


def grow_kernel(levels, seg_bits, col_bits, n_far, last, *refs):
    n_old, n_new = levels[-1]
    bits = (n_old + n_new).bit_length() - 1
    if last:
        across, diagonal, known, emi, ref, old_sums, *refs = refs
        old_tiles, (out, tiles, sums, held, *scratch) = refs[: len(levels) - 1], refs[len(levels) - 1 :]
        at = 0
        for part in (known, across, diagonal):
            held[at : at + part.shape[0]] = part[...]
            at += part.shape[0]
    elif n_old:
        held, old_sums, sums, tiles, *scratch = refs
    else:
        held, sums, tiles, *scratch = refs
    (
        geo_all, far_leave, far_arrive, far_rep, near_pos, near_rep, near_leave, near_arrive,
        even, odd, flag_rows,
    ) = scratch
    n_seg = n_old + n_new
    bands, width = held.shape[1] // 2 - GEO_ROWS // 2, held.shape[2]
    n_tri = triangle(n_new)
    n_pairs = n_tri + n_new * n_old
    halves = width // BLOCK
    row = lax.broadcasted_iota(jnp.int32, (8, width), 0)
    geo_at = 2 * bands
    for k in range(n_seg):
        piece = held[k, geo_at : geo_at + GEO_ROWS, :].astype(jnp.float32)
        low = jnp.where(row == 0, piece[7:8], jnp.where(row == 1, piece[14:15], piece[15:16]))
        geo_all[k] = (piece[0:8] + piece[8:16]) + jnp.where(row < 3, low, 0.0)
        flag_rows[k] = piece[FLAG_ROW : FLAG_ROW + 1, 0:BLOCK]
    if n_old:
        sums[0:n_old] = old_sums[...]
    sums[n_old:n_seg] = jnp.zeros((n_new, bands, width), jnp.float32)
    origin = jnp.broadcast_to(geo_all[0, :, 0:1], (8, width))
    for k in range(n_seg):
        geo = geo_all[k]
        offset = jnp.where(row < 3, geo - origin, 0.0)
        normal = jnp.where(row < 3, pltpu.roll(geo, 5, 0), 0.0)
        along = jnp.sum(normal * offset, axis=0, keepdims=True)
        for c in range(3):
            far_rep[k, c] = jnp.broadcast_to(geo[c : c + 1], (8, width))
        far_leave[k] = far_stack(jnp.where(row == 3, 1.0, offset))
        far_arrive[k] = far_stack(jnp.where(row == 3, along, normal) * (-1.0 / math.pi))
        if k < n_old:
            continue
        at = k - n_old
        near_pos[at, :, 0:8] = jnp.transpose(geo)
        near_leave[at] = jnp.transpose(near_stack(jnp.where(row == 3, -along, normal))).astype(jnp.bfloat16)
        near_arrive[at] = jnp.transpose(near_stack(jnp.where(row == 3, 1.0, -offset))).astype(jnp.bfloat16)
    col_mask = (1 << col_bits) - 1

    def pair_of(t):
        if t >= n_tri:
            near, far = (t - n_tri) % n_new, (t - n_tri) // n_new
        else:
            near = t % n_new
            far = (near + t // n_new) % n_new + n_old
        return near, near + n_old, far

    def live(near_at, far_at, i, j):
        near = bit_reverse(near_at, bits) << (seg_bits - bits)
        far = bit_reverse(far_at, bits) << (seg_bits - bits)
        holder = (near & ~col_mask) | (far & col_mask)
        apart = near ^ far
        index = ((((apart & col_mask) << 1) | i) * n_far) + (((apart >> col_bits) << 1) | j)
        held_at = bit_reverse(holder >> (seg_bits - bits), bits)
        return flag_rows[held_at, :, index : index + 1]

    def project(t, cosines):
        local, near_at, far_at = pair_of(t)
        masked = []
        for i in range(halves):
            flags = [
                jnp.maximum(live(near_at, far_at, i, j), live(far_at, near_at, j, i))
                for j in range(halves)
            ]
            flags = jnp.concatenate([jnp.broadcast_to(f, (PIECES, BLOCK)) for f in flags], axis=1)
            masked.append(far_arrive[far_at] * flags.astype(jnp.bfloat16))
        for at in range(0, width, CHUNK):
            yield
            rows = slice(at, at + CHUNK)
            cols = slice(at // BLOCK * BLOCK if near_at == far_at else 0, width)
            leaving = jnp.dot(
                near_leave[local, rows], far_leave[far_at, :, cols], preferred_element_type=jnp.float32
            )
            arriving = jnp.dot(
                near_arrive[local, rows], masked[at // BLOCK][:, cols], preferred_element_type=jnp.float32
            )
            cosines[rows, cols] = jnp.maximum(leaving, 0.0) * jnp.maximum(arriving, 0.0)

    def form(t, cosines, fresh):
        local, near_at, far_at = pair_of(t)
        fars = [
            [far_rep[far_at, c, :, j * BLOCK : (j + 1) * BLOCK] for c in range(3)]
            for j in range(halves)
        ]
        for strip in range(width // 16):
            if strip * 16 % CHUNK == 0:
                yield
            nears = []
            for part in range(2):
                at = strip * 16 + part * 8
                if fresh:
                    cols_now = near_pos[local, at : at + 8, :]
                    now = [jnp.broadcast_to(cols_now[:, c : c + 1], (8, BLOCK)) for c in range(3)]
                    for c in range(3):
                        near_rep[local, c, at : at + 8, :] = now[c]
                else:
                    now = [near_rep[local, c, at : at + 8, :] for c in range(3)]
                nears.append(now)
            for j in range(strip * 16 // BLOCK if near_at == far_at else 0, halves):
                cols = slice(j * BLOCK, (j + 1) * BLOCK)
                parts = []
                for part in range(2):
                    at = strip * 16 + part * 8
                    dx, dy, dz = (f - n for f, n in zip(fars[j], nears[part]))
                    spacing = dx * dx + dy * dy + dz * dz + SOFTEN
                    inverse = 1.0 / spacing
                    product = cosines[at : at + 8, cols]
                    parts.append(product * (inverse * inverse))
                strip_now = jnp.concatenate(parts, axis=0).astype(jnp.bfloat16)
                tiles[t, strip * 16 : strip * 16 + 16, cols] = strip_now

    def apply(t):
        local, near_at, far_at = pair_of(t)
        if near_at == far_at:
            sums[near_at] = sums[near_at] + diagonal_product(held[far_at, 0:bands, :], tiles, t)
            return
        tile = tiles[t]
        to_near = lax.dot_general(
            held[far_at, 0:bands, :], tile, (((1,), (1,)), ((), ())), preferred_element_type=jnp.float32
        )
        sums[near_at] = sums[near_at] + to_near
        to_far = lax.dot_general(
            held[near_at, 0:bands, :], tile, (((1,), (0,)), ((), ())), preferred_element_type=jnp.float32
        )
        sums[far_at] = sums[far_at] + to_far

    cosines = (even, odd)
    for _ in project(0, even):
        pass
    for t in range(n_pairs):
        later = project(t + 1, cosines[(t + 1) % 2]) if t + 1 < n_pairs else ()
        for _ in itertools.zip_longest(later, form(t, cosines[t % 2], t < n_new)):
            pass
        if t:
            apply(t - 1)
    apply(n_pairs - 1)
    if not last:
        return
    total = jnp.zeros((bands, width), jnp.float32)
    for k in range(n_seg):
        base = held[k, 0:bands, :].astype(jnp.float32)
        gain = held[k, bands : 2 * bands, :].astype(jnp.float32)
        weighted = (base + gain * sums[k]).astype(jnp.bfloat16)
        level = next(i for i, (old, new) in enumerate(levels) if k < old + new)
        old, new = levels[level]
        t, over = (triangle(new) + k - old, 0) if old else own_tile(k, new)
        if k == 0:
            total += diagonal_product(weighted, old_tiles[level], t)
            continue
        tile = tiles[t] if k >= n_old else old_tiles[level][t]
        total += lax.dot_general(
            weighted, tile, (((1,), (over,)), ((), ())), preferred_element_type=jnp.float32
        )
    out[...] = emi[...] + ref[...] * total


def grow(levels, seg_bits, col_bits, n_far, args):
    n_old, n_new = levels[-1]
    rows, width = args[0].shape[1:]
    bands = (rows - GEO_ROWS) // 2
    n_seg = n_old + n_new
    last = n_seg == 1 << seg_bits
    n_pairs = triangle(n_new) + n_new * n_old
    vmem = pl.BlockSpec(memory_space=pltpu.VMEM)
    state = [
        pltpu.VMEM((n_pairs, width, width), jnp.bfloat16),
        pltpu.VMEM((n_seg, bands, width), jnp.float32),
    ]
    outs = jax.ShapeDtypeStruct((bands, width), jnp.float32) if last else state[::-1]
    work = n_pairs * width * width
    return pl.pallas_call(
        functools.partial(grow_kernel, levels, seg_bits, col_bits, n_far, last),
        out_shape=outs,
        in_specs=[vmem] * len(args),
        out_specs=vmem if last else [vmem, vmem],
        scratch_shapes=(state + [pltpu.VMEM((n_seg, rows, width), jnp.bfloat16)] if last else [])
        + [
            pltpu.VMEM((n_seg, 8, width), jnp.float32),
            pltpu.VMEM((n_seg, PIECES, width), jnp.bfloat16),
            pltpu.VMEM((n_seg, PIECES, width), jnp.bfloat16),
            pltpu.VMEM((n_seg, 3, 8, width), jnp.float32),
            pltpu.VMEM((n_new, width, BLOCK), jnp.float32),
            pltpu.VMEM((n_new, 3, width, BLOCK), jnp.float32),
            pltpu.VMEM((n_new, width, PIECES), jnp.bfloat16),
            pltpu.VMEM((n_new, width, PIECES), jnp.bfloat16),
            *[pltpu.VMEM((width, width), jnp.float32)] * 2,
            pltpu.VMEM((n_seg, 1, BLOCK), jnp.float32),
        ],
        compiler_params=pltpu.CompilerParams(vmem_limit_bytes=32 * 1024 * 1024),
        cost_estimate=pl.CostEstimate(
            flops=work * (4 * PIECES + 4 * bands), bytes_accessed=n_seg * rows * width * 2, transcendentals=work
        ),
    )(*args)


def one_exchange(positions, normals, areas, emission, reflect, pair_row, pair_col, pair_live):
    n_row = lax.axis_size("row")
    n_col = lax.axis_size("col")
    n_seg = n_row * n_col
    seg_bits = n_seg.bit_length() - 1
    col_bits = n_col.bit_length() - 1
    bands, width = emission.shape
    n_far = width // BLOCK * n_row
    rows = 2 * bands + GEO_ROWS
    vmem = pl.BlockSpec(memory_space=pltpu.VMEM)
    pairs = [pair.reshape(1, -1) for pair in (pair_row, pair_col, pair_live)]
    packed = pl.pallas_call(
        functools.partial(pack_kernel, col_bits, n_far),
        out_shape=pltpu.VMEM((rows, width), jnp.bfloat16),
        in_specs=[vmem] * 8,
        out_specs=vmem,
    )(positions, normals, areas.reshape(1, width), emission, reflect, *pairs)
    gathered = packed[None]

    def swap(value, distance):
        return lax.ppermute(value, ("row", "col"), [(i, i ^ distance) for i in range(n_seg)])

    for bit in reversed(range(2, seg_bits)):
        gathered = jnp.concatenate([gathered, swap(gathered, 1 << bit)])
    beside, across, diagonal = (swap(gathered, distance) for distance in (2, 1, 3))
    quarter, half = n_seg // 4, n_seg // 2
    levels = ((0, quarter), (quarter, quarter), (half, half))
    sums, tiles = grow(levels[:1], seg_bits, col_bits, n_far, (gathered,))
    gathered = jnp.concatenate([gathered, beside])
    sums, more_tiles = grow(levels[:2], seg_bits, col_bits, n_far, (gathered, sums))
    args = (across, diagonal, gathered, emission, reflect, sums, tiles, more_tiles)
    return grow(levels, seg_bits, col_bits, n_far, args)


def form_tiles(near, far):
    offset = far[0:3, :, None, :] - near[0:3, :, :, None]
    leaving = jnp.sum(near[3:6, :, :, None] * offset, axis=0)
    arriving = -jnp.sum(far[3:6, :, None, :] * offset, axis=0)
    spacing = jnp.sum(offset * offset, axis=0) + SOFTEN
    return jax.nn.relu(leaving) * jax.nn.relu(arriving) / (math.pi * spacing * spacing)


def two_exchanges(positions, normals, areas, emission, reflect, pair_row, pair_col, pair_live):
    patch_dev = areas.shape[0]
    own_blocks = patch_dev // BLOCK
    n_row = lax.axis_size("row")
    n_col = lax.axis_size("col")
    row_blocks = own_blocks * n_col
    col_blocks = own_blocks * n_row
    all_blocks = row_blocks * n_row
    band_half = emission.shape[0]
    row_here = lax.axis_index("row")
    col_here = lax.axis_index("col")
    geometry = jnp.concatenate([positions, normals], axis=0)
    geo_rows = lax.all_gather(geometry, "col", axis=1, tiled=True).reshape(6, row_blocks, BLOCK)
    geo_cols = lax.all_gather(geometry, "row", axis=1, tiled=True).reshape(6, col_blocks, BLOCK)
    slots = pair_row.shape[0]
    rows_seen, cols_seen, live_seen = (
        lax.all_gather(pair_row, ("row", "col"), axis=0, tiled=True),
        lax.all_gather(pair_col, ("row", "col"), axis=0, tiled=True),
        lax.all_gather(pair_live, ("row", "col"), axis=0, tiled=True),
    )
    seen = jnp.zeros((all_blocks * all_blocks,), jnp.int32)
    seen = seen.at[rows_seen * all_blocks + cols_seen].max(live_seen)
    seen = seen.at[cols_seen * all_blocks + rows_seen].max(live_seen)
    near_grid = row_here * row_blocks + jnp.arange(row_blocks, dtype=jnp.int32)
    far_local = jnp.arange(col_blocks, dtype=jnp.int32)
    far_grid = (far_local // own_blocks * n_col + col_here) * own_blocks + far_local % own_blocks
    flags = seen[(near_grid[:, None] * all_blocks + far_grid[None, :]).reshape(-1)]
    order = jnp.argsort(1 - flags, stable=True)
    near_index = order // col_blocks
    far_index = order % col_blocks
    live_float = flags[order].astype(jnp.float32)
    live_count = jnp.sum(flags)
    group_size = math.gcd(slots, 32)
    turns = (live_count + group_size - 1) // group_size
    stored_init = jnp.zeros((1, 1, 1), jnp.bfloat16)
    stored = stored_init
    radiosity = emission
    for sweep in range(ITERS):
        weighted = (areas[None, :] * radiosity).astype(jnp.bfloat16)
        w_cols = lax.all_gather(weighted, "row", axis=1, tiled=True).reshape(
            band_half, col_blocks, BLOCK
        )

        def one_turn(turn_index, state_now):
            acc_rows, acc_cols, kept = state_now
            first_slot = turn_index * group_size
            near_now = lax.dynamic_slice_in_dim(near_index, first_slot, group_size)
            far_now = lax.dynamic_slice_in_dim(far_index, first_slot, group_size)
            live_now = lax.dynamic_slice_in_dim(live_float, first_slot, group_size)
            tiles_now = form_tiles(geo_rows[:, near_now], geo_cols[:, far_now]).astype(jnp.bfloat16)
            far_weights = w_cols[:, far_now]
            to_rows = jnp.einsum(
                "buv,kbv->kbu", tiles_now, far_weights, preferred_element_type=jnp.float32
            )
            acc_rows = acc_rows.at[:, near_now].add(to_rows * live_now[None, :, None])
            return (acc_rows, acc_cols, kept)

        zero_rows = jnp.zeros((band_half, row_blocks, BLOCK), jnp.float32)
        zero_cols = jnp.zeros((1, 1, 1), jnp.float32)
        acc_rows, acc_cols, stored = lax.fori_loop(
            0, turns, one_turn, (zero_rows, zero_cols, stored)
        )
        row_sum = lax.psum_scatter(
            acc_rows.reshape(band_half, row_blocks * BLOCK), "col", scatter_dimension=1, tiled=True
        )
        radiosity = emission + reflect * row_sum
    return radiosity


def shards(positions, normals, areas, emission, reflect, pair_row, pair_col, pair_live):
    n_row, n_col = lax.axis_size("row"), lax.axis_size("col")
    n_seg = n_row * n_col
    powers = n_row & (n_row - 1) == 0 and n_col & (n_col - 1) == 0
    small = areas.shape[0] == 2 * BLOCK and 8 <= n_seg <= 16
    plan = one_exchange if powers and small else two_exchanges
    return plan(positions, normals, areas, emission, reflect, pair_row, pair_col, pair_live)


def solution(mesh):
    return jax.shard_map(
        shards,
        mesh=mesh,
        in_specs=(
            P(None, ("case", "row", "col")),
            P(None, ("case", "row", "col")),
            P(("case", "row", "col")),
            P("band", ("case", "row", "col")),
            P("band", ("case", "row", "col")),
            P(("case", "row", "col")),
            P(("case", "row", "col")),
            P(("case", "row", "col")),
        ),
        out_specs=P("band", ("case", "row", "col")),
        check_vma=False,
    )
```
